32 devices in a mesh: sx: 4 (over y, x), sy: 8 (over z, core).
Axes of the slice: x: 2, y: 2, z: 4, core: 2. Of those that a mesh axis runs over, the one named last changes fastest.
Arguments:
- text_tokens: bfloat16 [8, 32, 4096], P('sy', 'sx'), may hold values from -2.5 to 2.5
- latent: bfloat16 [8, 16, 512], P('sy', 'sx'), may hold values from -6 to 6
- image_offset: int32 [8], P('sy'), may hold values from 0 to 32
- norm_gain: bfloat16 [4096], replicated, may hold values from 0.099609375 to 1.8984375
- w_query: bfloat16 [4096, 4096], P(None, 'sx')
- w_key: bfloat16 [4096, 4096], P(None, 'sx')
- w_value: bfloat16 [4096, 4096], P(None, 'sx'), may hold values from -0.09375 to 0.09375
- w_out: bfloat16 [4096, 4096], P('sx'), may hold values from -0.09375 to 0.09375
- w_down_conv: bfloat16 [288, 128], replicated, may hold values from -0.375 to 0.375
- w_down_proj: bfloat16 [128, 4096], replicated, may hold values from -0.5 to 0.5
- w_up_proj: bfloat16 [4096, 128], replicated, may hold values from -0.09375 to 0.09375
- w_up_out: bfloat16 [128, 32], replicated, may hold values from -0.5 to 0.5
- pred_grad: bfloat16 [8, 16, 512], P('sy', 'sx'), may hold values from -0.8984375 to 0.8984375
- text_grad: bfloat16 [8, 32, 4096], P('sy', 'sx'), may hold values from -0.29882812 to 0.29882812
Outputs:
- prediction: bfloat16 [8, 16, 512], P('sy', 'sx')
- text_out: bfloat16 [8, 32, 4096], P('sy', 'sx')
- grad_down_conv: float32 [288, 128], replicated
- grad_down_proj: float32 [128, 4096], replicated
- grad_up_proj: float32 [4096, 128], replicated
- grad_up_out: float32 [128, 32], replicated
The draws below stay inside these ranges and needn't reach their ends.
All inputs are finite; a program needn't handle non-finite values.
Results may differ from the reference program's by a relative error of at most 0.028.
Values may be sent and summed in bfloat16 or wider, within the bound.
No kernel may reach another device: no remote copies, remote signals or barrier semaphores. Data moves between devices by JAX's collectives and lax.ppermute only.
A program may use at most 192 MiB of HBM per device.

```python
import math
import jax
import jax.numpy as jnp
from jax import lax

D = 4096
HEADS = 32
HD = 128
LAT_C = 32
UC = 128
PH = 16
PW = 16
TXT_B = 32
N_IMG = 8
SB = 288
SEQ = 2304


def shared_projection(key):
    base = jax.random.normal(key, (D, HEADS * HD), jnp.float32) * D ** (-0.5)
    return base


def draw_w_query(key, part):
    base = shared_projection(key)
    return base.astype(jnp.bfloat16)


def draw_w_key(key, part):
    key = jax.random.fold_in(key, 12)
    noise = jax.random.normal(key, (D, HEADS * HD), jnp.float32) * D ** (-0.5)
    return noise.astype(jnp.bfloat16)


def plant(drawn, own_key, least, high):
    shape = drawn.shape
    spot = [jax.random.randint(jax.random.fold_in(own_key, axis), (), 0, shape[axis]) for axis in range(len(shape))]
    drawn = drawn.at[tuple(spot)].set(least)
    longest = shape.index(max(shape))
    spot[longest] = (spot[longest] + 1) % shape[longest]
    return drawn.at[tuple(spot)].set(high)


def block_levels(rng, dims, shards, low, largest):
    loudness = 1.0
    for axis_at, blocks in shards:
        heights = jax.random.uniform(jax.random.fold_in(jax.random.fold_in(rng, 6), axis_at), (blocks,), jnp.float32, low / len(shards), largest / len(shards))
        loudness = loudness * jnp.repeat(jnp.exp(heights), dims[axis_at] // blocks).reshape((-1,) + (1,) * (len(dims) - 1 - axis_at))
    return loudness


def bell_draw(stream_key, extent, spread, most, shards=(), kind=jnp.bfloat16):
    factor_of = block_levels(stream_key, extent, shards, -0.22, 0.18) if shards else 1.0
    result = jax.random.normal(stream_key, extent, jnp.float32) * spread * factor_of
    return jnp.minimum(jnp.maximum(result, -most), most).astype(kind)


def setup_inputs(seed: int = 0) -> dict:
    seeds = jax.random.split(jax.random.key(seed), 15)
    text_tokens = bell_draw(seeds[0], (N_IMG, TXT_B, D), 0.4, 2.5, ((0, 8), (1, 4)))
    latent = bell_draw(seeds[1], (N_IMG, PH, PW * LAT_C), 1.0, 6.0, ((0, 8), (1, 4)))
    image_offset = plant(jax.random.randint(seeds[2], (N_IMG,), 0, TXT_B + 1), jax.random.fold_in(seeds[2], 1), 0, TXT_B).astype(jnp.int32)
    norm_gain = jnp.clip(1.0 + 0.18 * jax.random.normal(seeds[3], (D,), jnp.float32), 0.099609375, 1.8984375).astype(jnp.bfloat16)
    w_query = draw_w_query(jax.random.fold_in(seeds[14], 71), 0)
    w_key = draw_w_key(jax.random.fold_in(seeds[14], 71), 0)
    w_value = bell_draw(seeds[6], (D, HEADS * HD), D ** -0.5, 0.09375, ((1, 4),))
    w_out = bell_draw(seeds[7], (HEADS * HD, D), (HEADS * HD) ** -0.5, 0.09375, ((0, 4),))
    w_down_conv = bell_draw(seeds[8], (9 * LAT_C, UC), (9 * LAT_C) ** -0.5, 0.375)
    w_down_proj = bell_draw(seeds[9], (UC, D), UC ** -0.5, 0.5)
    w_up_proj = bell_draw(seeds[10], (D, UC), D ** -0.5, 0.09375)
    w_up_out = bell_draw(seeds[11], (UC, LAT_C), UC ** -0.5, 0.5)
    pred_grad = bell_draw(seeds[12], (N_IMG, PH, PW * LAT_C), 0.15, 0.8984375, ((0, 8), (1, 4)))
    text_grad = bell_draw(seeds[13], (N_IMG, TXT_B, D), 0.05, 0.29882812, ((0, 8), (1, 4)))
    return dict(text_tokens=text_tokens, latent=latent, image_offset=image_offset, norm_gain=norm_gain, w_query=w_query, w_key=w_key, w_value=w_value, w_out=w_out, w_down_conv=w_down_conv, w_down_proj=w_down_proj, w_up_proj=w_up_proj, w_up_out=w_up_out, pred_grad=pred_grad, text_grad=text_grad)


epsilon = 1e-05
NEG_SCORE = -1e+30
rope_base = 500000.0

def silu_slope(values):
    sigma = jax.nn.sigmoid(values)
    return sigma * (1.0 + values * (1.0 - sigma))

def neighbour_cells(padded, rows, cols):
    wide = jnp.pad(padded, ((0, 0), (1, 1), (0, 0)))
    parts = [wide[r:r + rows, c:c + cols, :] for r in range(3) for c in range(3)]
    return jnp.concatenate(parts, axis=-1)

def rope_tables(positions, head_size):
    half = head_size // 2
    freq = jnp.exp(-(2.0 * jnp.arange(half, dtype=jnp.float32) / head_size) * math.log(rope_base))
    angle = positions.astype(jnp.float32)[:, None] * freq[None, :]
    return (jnp.cos(angle)[:, None, :], jnp.sin(angle)[:, None, :])

def rotate(values, cosine, sine):
    half = values.shape[-1] // 2
    first = values[..., :half]
    second = values[..., half:]
    return jnp.concatenate([first * cosine - second * sine, second * cosine + first * sine], axis=-1)

def block_layout(offset):
    text_index = jnp.arange(TXT_B, dtype=jnp.int32)
    text_pos = text_index + jnp.where(text_index >= offset, PH * PW, 0).astype(jnp.int32)
    image_pos = offset + jnp.arange(PH * PW, dtype=jnp.int32)
    image_flags = jnp.concatenate([jnp.zeros((TXT_B,), bool), jnp.ones((PH * PW,), bool)])
    return (jnp.concatenate([text_pos, image_pos]).astype(jnp.int32), image_flags)

def reference(text_tokens, latent, image_offset, norm_gain, w_query, w_key, w_value, w_out, w_down_conv, w_down_proj, w_up_proj, w_up_out, pred_grad, text_grad):
    wide_type = jnp.float32
    grids = latent.reshape(N_IMG, PH, PW, LAT_C)
    padded = jnp.pad(grids, ((0, 0), (1, 1), (0, 0), (0, 0)))
    patches = jax.vmap(lambda grid: neighbour_cells(grid, PH, PW))(padded).reshape(N_IMG * PH * PW, 9 * LAT_C)
    pre_down = jnp.dot(patches, w_down_conv, preferred_element_type=wide_type)
    down_act = jax.nn.silu(pre_down).astype(jnp.bfloat16)
    embedded = jnp.dot(down_act, w_down_proj, preferred_element_type=wide_type).astype(jnp.bfloat16)
    layer_in = jnp.concatenate([text_tokens, embedded.reshape(N_IMG, PH * PW, D)], axis=1).reshape(SEQ, D)
    inputs = layer_in.astype(wide_type)
    inverse = lax.rsqrt(lax.optimization_barrier(jnp.mean(inputs * inputs, axis=-1, keepdims=True)) + epsilon)
    gain = norm_gain.astype(wide_type)
    normed = (inputs * inverse * gain).astype(jnp.bfloat16)
    positions, image_flags = jax.vmap(block_layout)(image_offset)
    key_pos = positions.reshape(SEQ)
    key_image = image_flags.reshape(SEQ)
    key_block = jnp.arange(SEQ, dtype=jnp.int32) // SB
    cosine, sine = rope_tables(key_pos + key_block * SB, HD)
    queries = rotate(jnp.dot(normed, w_query, preferred_element_type=wide_type).reshape(SEQ, HEADS, HD), cosine, sine).astype(jnp.bfloat16)
    keys = rotate(jnp.dot(normed, w_key, preferred_element_type=wide_type).reshape(SEQ, HEADS, HD), cosine, sine).astype(jnp.bfloat16)
    values = jnp.dot(normed, w_value, preferred_element_type=wide_type).astype(jnp.bfloat16).reshape(SEQ, HEADS, HD)
    score_scale = HD ** (-0.5)
    keys_wide = keys.astype(wide_type)
    values_wide = values.astype(wide_type)

    def probabilities(index):
        query_blk = lax.dynamic_slice_in_dim(queries, index * SB, SB, 0)
        query_pos = lax.dynamic_slice_in_dim(key_pos, index * SB, SB, 0)
        query_image = lax.dynamic_slice_in_dim(key_image, index * SB, SB, 0)
        same = (key_block == index)[None, :] & ((key_pos[None, :] <= query_pos[:, None]) | key_image[None, :] & query_image[:, None])
        visible = (key_block < index)[None, :] | same
        scores = jnp.einsum('qhd,khd->hqk', query_blk.astype(wide_type), keys_wide) * score_scale
        scores = jnp.where(visible[None], scores, NEG_SCORE)
        peak = lax.optimization_barrier(jnp.max(scores, axis=-1, keepdims=True))
        raised = jnp.where(visible[None], jnp.exp(scores - peak), 0.0)
        return (query_blk, raised / lax.optimization_barrier(jnp.sum(raised, axis=-1, keepdims=True)))

    def attend(index):
        query_blk, probs = probabilities(index)
        weights = probs.astype(jnp.bfloat16)
        mixed = jnp.einsum('hqk,khd->qhd', weights.astype(wide_type), values_wide)
        return mixed.astype(jnp.bfloat16).reshape(SB, HEADS * HD)
    block_ids = jnp.arange(N_IMG, dtype=jnp.int32)
    attended = lax.map(attend, block_ids).reshape(SEQ, HEADS * HD)
    layer_out = (inputs + jnp.dot(attended, w_out, preferred_element_type=wide_type)).astype(jnp.bfloat16)
    rows_out = layer_out.reshape(N_IMG, SB, D)
    text_out = rows_out[:, :TXT_B]
    image_out = rows_out[:, TXT_B:].reshape(N_IMG * PH * PW, D)
    pre_up = jnp.dot(image_out, w_up_proj, preferred_element_type=wide_type)
    up_act = jax.nn.silu(pre_up).astype(jnp.bfloat16)
    prediction = jnp.dot(up_act, w_up_out, preferred_element_type=wide_type).astype(jnp.bfloat16).reshape(N_IMG, PH, PW * LAT_C)
    out_grad = pred_grad.reshape(N_IMG * PH * PW, LAT_C)
    grad_up_out = jnp.dot(up_act.T, out_grad, preferred_element_type=wide_type)
    grad_pre_up = (jnp.dot(out_grad, w_up_out.T, preferred_element_type=wide_type) * silu_slope(pre_up)).astype(jnp.bfloat16)
    grad_up_proj = jnp.dot(image_out.T, grad_pre_up, preferred_element_type=wide_type)
    grad_image = jnp.dot(grad_pre_up, w_up_proj.T, preferred_element_type=wide_type)
    grad_rows = jnp.concatenate([text_grad.astype(wide_type), grad_image.reshape(N_IMG, PH * PW, D)], axis=1).reshape(SEQ, D).astype(jnp.bfloat16)
    grad_attended = jnp.dot(grad_rows, w_out.T, preferred_element_type=wide_type).astype(jnp.bfloat16)
    grad_heads = grad_attended.reshape(SEQ, HEADS, HD)
    attended_heads = attended.reshape(SEQ, HEADS, HD)

    def backward_block(totals, index):
        query_blk, probs = probabilities(index)
        weights = lax.optimization_barrier(probs.astype(jnp.bfloat16)).astype(wide_type)
        grad_blk = lax.dynamic_slice_in_dim(grad_heads, index * SB, SB, 0).astype(wide_type)
        out_blk = lax.dynamic_slice_in_dim(attended_heads, index * SB, SB, 0).astype(wide_type)
        delta = jnp.einsum('qhd,qhd->hq', grad_blk, out_blk)
        grad_prob = jnp.einsum('qhd,khd->hqk', grad_blk, values_wide)
        grad_score = probs * (grad_prob - delta[:, :, None]) * score_scale
        grad_score = lax.optimization_barrier(grad_score.astype(jnp.bfloat16)).astype(wide_type)
        grad_query = jnp.einsum('hqk,khd->qhd', grad_score, keys_wide)
        key_part = lax.optimization_barrier(jnp.einsum('hqk,qhd->khd', grad_score, query_blk.astype(wide_type)).astype(jnp.bfloat16))
        value_part = lax.optimization_barrier(jnp.einsum('hqk,qhd->khd', weights, grad_blk).astype(jnp.bfloat16))
        return ((totals[0] + key_part.astype(wide_type), totals[1] + value_part.astype(wide_type)), grad_query)
    empty = jnp.zeros((SEQ, HEADS, HD), wide_type)
    totals, grad_queries = lax.scan(backward_block, (empty, empty), block_ids)
    grad_queries = rotate(grad_queries.reshape(SEQ, HEADS, HD), cosine, -sine).astype(jnp.bfloat16).reshape(SEQ, HEADS * HD)
    grad_keys = rotate(totals[0], cosine, -sine).astype(jnp.bfloat16).reshape(SEQ, HEADS * HD)
    grad_values = totals[1].astype(jnp.bfloat16).reshape(SEQ, HEADS * HD)
    grad_normed = jnp.dot(grad_queries, w_query.T, preferred_element_type=wide_type)
    grad_normed = grad_normed + jnp.dot(grad_keys, w_key.T, preferred_element_type=wide_type)
    grad_normed = grad_normed + jnp.dot(grad_values, w_value.T, preferred_element_type=wide_type)
    scaled = grad_normed * gain
    grad_in = grad_rows.astype(wide_type) + inverse * scaled - inputs * inverse ** 3 * lax.optimization_barrier(jnp.mean(inputs * scaled, axis=-1, keepdims=True))
    grad_embedded = grad_in.reshape(N_IMG, SB, D)[:, TXT_B:].reshape(N_IMG * PH * PW, D).astype(jnp.bfloat16)
    grad_down_proj = jnp.dot(down_act.T, grad_embedded, preferred_element_type=wide_type)
    grad_pre_down = (jnp.dot(grad_embedded, w_down_proj.T, preferred_element_type=wide_type) * silu_slope(pre_down)).astype(jnp.bfloat16)
    grad_down_conv = jnp.dot(patches.T, grad_pre_down, preferred_element_type=wide_type)
    return (prediction, text_out, grad_down_conv, grad_down_proj, grad_up_proj, grad_up_out)
```

```python
import math

import jax
import jax.numpy as jnp
import numpy as np
from jax import lax
from jax.experimental import pallas as pl
from jax.experimental.pallas import tpu as pltpu
from jax.sharding import PartitionSpec as P

HD = 128
EPSILON = 1e-05
NEG_SCORE = -1e30
ROPE_BASE = 500000.0
SCALE = HD ** (-0.5)
LOG2E = math.log2(math.e)
LN2 = math.log(2.0)
F32 = jnp.float32
BF16 = jnp.bfloat16
MIB = 1024 * 1024
VMEM_BYTES = 56 * MIB
SMALL_BYTES = 16 * MIB


def dot(left, right):
    return jnp.dot(left, right, preferred_element_type=F32)


def dot_nt(left, right):
    return lax.dot_general(left, right, (((1,), (1,)), ((), ())), preferred_element_type=F32)


def silu_slope(values):
    sigma = jax.nn.sigmoid(values)
    return sigma * (1.0 + values * (1.0 - sigma))


def silu(values):
    return values * jax.nn.sigmoid(values)


def iota(shape, dim):
    return lax.broadcasted_iota(jnp.int32, shape, dim)


def flip(values):
    return values.astype(F32).T.astype(BF16)


def call(kernel, head, inputs, outs, scratch=(), flops=0, after=(), out_kind=None, room=VMEM_BYTES):
    inputs = [(a, "any") for a in after] + list(inputs)
    skip = len(after)

    def spec(array, block):
        if block == "smem":
            return pl.BlockSpec(memory_space=pltpu.SMEM)
        if block == "cols":
            return pl.BlockSpec((array.shape[0], HD), lambda i, h: (0, h[0]))
        if block == "rows":
            return pl.BlockSpec((HD, array.shape[1]), lambda i, h: (h[0], 0))
        if block == "any":
            return pl.BlockSpec(memory_space=pl.ANY)
        if block == "mine":
            return pl.BlockSpec((1,) + array.shape[1:], lambda i, h: (h[1], 0, 0))
        rank = len(array.shape)
        return pl.BlockSpec(array.shape, lambda i, h: (0,) * rank)

    moved = sum(math.prod(a.shape) * a.dtype.itemsize for a in outs) + sum(
        math.prod(a.shape) * a.dtype.itemsize // (a.shape[1 if b == "cols" else 0] // HD if b in ("cols", "rows") else 1)
        for a, b in inputs
    )
    return pl.pallas_call(
        lambda head_ref, *refs: kernel(head_ref, *refs[skip:]),
        out_shape=outs,
        grid_spec=pltpu.PrefetchScalarGridSpec(
            num_scalar_prefetch=1,
            grid=(1,),
            in_specs=[spec(a, b) for a, b in inputs],
            out_specs=[spec(a, out_kind) for a in outs],
            scratch_shapes=list(scratch),
        ),
        compiler_params=pltpu.CompilerParams(vmem_limit_bytes=room),
        cost_estimate=pl.CostEstimate(flops=flops, bytes_accessed=moved, transcendentals=0),
    )(head, *[a for a, _ in inputs])


def weights_kernel(
    head, wq, wk, wv, wo, gain, w_down, w_up, w_conv,
    proj, proj_t, mapped, u, gram, z, conv_t,
    proj_sum, u_sum, gram_sum, z_sum,
):
    step = pl.program_id(0)
    down = w_down[...]
    scaled = (down.astype(F32) * gain[...].astype(F32)).astype(BF16)
    terms = [(proj_sum.at[n], dot(scaled, w[...])) for n, w in enumerate((wq, wk, wv))]
    terms += [(u_sum, dot(wo[...], w_up[...])), (gram_sum, dot_nt(down, down)), (z_sum, dot(down, w_up[...]))]

    @pl.when(step == 0)
    def _():
        for total, term in terms:
            total[...] = term

    @pl.when(step > 0)
    def _():
        for total, term in terms:
            total[...] += term

    @pl.when(step == pl.num_programs(0) - 1)
    def _():
        for n in range(3):
            cols = slice(n * HD, (n + 1) * HD)
            proj[:, cols] = proj_sum[n].astype(BF16)
            proj_t[cols, :] = proj_sum[n].T.astype(BF16)
            mapped[:, cols] = proj_sum[n].astype(BF16)
        for n in range(2):
            mapped[:, (3 + n) * HD : (4 + n) * HD] = pltpu.roll(proj_sum[n], HD // 2, 1).astype(BF16)
        u[...] = u_sum[...].astype(BF16)
        gram[...] = gram_sum[...].astype(BF16)
        z[...] = z_sum[...].astype(BF16)
        conv_t[...] = flip(w_conv[...])


def small_products(place, wq, wk, wv, wo, gain, w_down, w_up, w_conv):
    rank, width = w_down.shape
    up_chan = w_up.shape[1]
    step_rows = math.gcd(width, 1024)
    cols = pl.BlockSpec((step_rows, HD), lambda i, p: (i, p[0]))
    outs = [(rank, 3 * HD), (3 * HD, rank), (rank, 5 * HD), (HD, up_chan), (rank, rank), (rank, up_chan), w_conv.shape[::-1]]
    return pl.pallas_call(
        weights_kernel,
        out_shape=[jax.ShapeDtypeStruct(shape, BF16) for shape in outs],
        grid_spec=pltpu.PrefetchScalarGridSpec(
            num_scalar_prefetch=1,
            grid=(width // step_rows,),
            in_specs=[cols, cols, cols, pl.BlockSpec((HD, step_rows), lambda i, p: (p[0], i)),
                      pl.BlockSpec((1, step_rows), lambda i, p: (0, i)), pl.BlockSpec((rank, step_rows), lambda i, p: (0, i)),
                      pl.BlockSpec((step_rows, up_chan), lambda i, p: (i, 0)), pl.BlockSpec(w_conv.shape, lambda i, p: (0, 0))],
            out_specs=[pl.BlockSpec(shape, lambda i, p: (0, 0)) for shape in outs],
            scratch_shapes=[pltpu.VMEM((3, rank, HD), F32), pltpu.VMEM((HD, up_chan), F32),
                            pltpu.VMEM((rank, rank), F32), pltpu.VMEM((rank, up_chan), F32)],
        ),
        compiler_params=pltpu.CompilerParams(vmem_limit_bytes=SMALL_BYTES),
        cost_estimate=pl.CostEstimate(flops=4_000_000_000, bytes_accessed=12 * HD * width, transcendentals=0),
    )(place, wq, wk, wv, wo, gain, w_down, w_up, w_conv)


def pick(rows, total, spot):
    return (iota((total, rows), 0) == iota((total, rows), 1) + spot).astype(BF16)


def gathered(parts, group):
    rows = parts[0].shape[0]
    total = rows * len(parts)
    return sum(dot(pick(rows, total, (group ^ k) * rows), part[...]) for k, part in enumerate(parts))


def text_kernel(count, place, *refs):
    parts = refs[:count]
    gain, wq, wk, wv, _, out, normed, sums = refs[count:]
    step = pl.program_id(0)
    rows = wq.shape[0]

    @pl.when(step == 0)
    def _():
        x = gathered(parts, place[2])
        inverse = lax.rsqrt(jnp.mean(x * x, axis=-1, keepdims=True) + EPSILON)
        whole = (x * inverse * gain[...].astype(F32)).astype(BF16)
        for at in range(normed.shape[0]):
            normed[at] = whole[:, at * rows : (at + 1) * rows]
        sums[...] = jnp.zeros_like(sums)

    here = normed[step]
    for n, w in enumerate((wq, wk, wv)):
        sums[n] += dot(here, w[...])

    @pl.when(step == pl.num_programs(0) - 1)
    def _():
        for h in range(out.shape[0]):
            for n in range(3):
                out[h, :, n * HD : (n + 1) * HD] = sums[n, :, h * HD : (h + 1) * HD].astype(BF16)


def text_heads(place, parts, gain, wq, wk, wv, after):
    rows, width = parts[0].shape
    rows *= len(parts)
    wide = wq.shape[1]
    heads = wide // HD
    step_rows = math.gcd(width, 512)
    strip = pl.BlockSpec((step_rows, wide), lambda i, p: (i, 0))
    whole = lambda a: pl.BlockSpec(a.shape, lambda i, p: (0, 0))
    return pl.pallas_call(
        lambda *refs: text_kernel(len(parts), *refs),
        out_shape=jax.ShapeDtypeStruct((heads, rows, 3 * HD), BF16),
        grid_spec=pltpu.PrefetchScalarGridSpec(
            num_scalar_prefetch=1,
            grid=(width // step_rows,),
            in_specs=[whole(a) for a in parts] + [whole(gain), strip, strip, strip, pl.BlockSpec(memory_space=pl.ANY)],
            out_specs=pl.BlockSpec((heads, rows, 3 * HD), lambda i, p: (0, 0, 0)),
            scratch_shapes=[pltpu.VMEM((width // step_rows, rows, step_rows), BF16), pltpu.VMEM((3, rows, wide), F32)],
        ),
        compiler_params=pltpu.CompilerParams(vmem_limit_bytes=VMEM_BYTES),
        cost_estimate=pl.CostEstimate(
            flops=6 * rows * width * wide, bytes_accessed=6 * width * wide, transcendentals=0
        ),
    )(place, *parts, gain, wq, wk, wv, after)


def text_grad_kernel(count, place, *refs):
    parts = refs[:count]
    wo, mix, _ = refs[count : count + 3]
    outs = refs[count + 3 : -1]
    grad_t = refs[-1]
    step = pl.program_id(0)

    @pl.when(step == 0)
    def _():
        grad_t[...] = gathered(parts, place[2]).T.astype(BF16)

    back = dot(wo[...], grad_t[...]).T.astype(BF16)
    for k, out in enumerate(outs):

        @pl.when(step == k)
        def _():
            out[:, :HD] = back
            out[:, HD:] = mix[...]


def text_grad_heads(place, parts, wo, mix, repeat, after):
    rows, width = parts[0].shape
    rows *= len(parts)
    peers = mix.shape[0] // rows
    return pl.pallas_call(
        lambda *refs: text_grad_kernel(len(parts), *refs),
        out_shape=[jax.ShapeDtypeStruct((rows, 2 * HD), BF16)] * peers,
        grid_spec=pltpu.PrefetchScalarGridSpec(
            num_scalar_prefetch=1,
            grid=(peers,),
            in_specs=[pl.BlockSpec(a.shape, lambda i, p: (0, 0)) for a in parts]
            + [pl.BlockSpec((HD, width), lambda i, p: ((p[5] ^ i) // repeat, 0)),
               pl.BlockSpec((rows, HD), lambda i, p: (p[5] ^ i, 0)), pl.BlockSpec(memory_space=pl.ANY)],
            out_specs=[pl.BlockSpec((rows, 2 * HD), lambda i, p: (0, 0))] * peers,
            scratch_shapes=[pltpu.VMEM((width, rows), BF16)],
        ),
        compiler_params=pltpu.CompilerParams(vmem_limit_bytes=VMEM_BYTES),
        cost_estimate=pl.CostEstimate(
            flops=2 * rows * width * peers * HD, bytes_accessed=2 * width * peers * HD, transcendentals=0
        ),
    )(place, *parts, wo, mix, after)


def text_out_kernel(repeat, peers, place, *refs):
    mixes = refs[:peers]
    wo = refs[peers]
    outs = refs[peers + 1 :]
    total = 0.0
    for k, mix in enumerate(mixes):
        peer = place[5] ^ k
        rows = pl.ds(pl.multiple_of(peer // repeat * HD, HD), HD)
        counts = jnp.where(peer % repeat == 0, 1.0, 0.0)
        total = total + dot(mix[:, HD:], wo[rows, :]) * counts
    whole = total.astype(BF16)
    for k, out in enumerate(outs):
        rows = out.shape[0]
        out[...] = dot(pick(rows, whole.shape[0], (place[2] ^ k) * rows).astype(F32).T.astype(BF16), whole).astype(BF16)


def text_out_parts(place, mixes, wo, repeat, groups):
    rows = mixes[0].shape[0]
    deep, width = wo.shape
    peers = len(mixes)
    few = rows // groups
    step_cols = math.gcd(width, 1024)
    return pl.pallas_call(
        lambda *refs: text_out_kernel(repeat, peers, *refs),
        out_shape=[jax.ShapeDtypeStruct((few, width), BF16)] * groups,
        grid_spec=pltpu.PrefetchScalarGridSpec(
            num_scalar_prefetch=1,
            grid=(width // step_cols,),
            in_specs=[pl.BlockSpec(a.shape, lambda i, p: (0, 0)) for a in mixes]
            + [pl.BlockSpec((deep, step_cols), lambda i, p: (0, i))],
            out_specs=[pl.BlockSpec((few, step_cols), lambda i, p: (0, i))] * groups,
        ),
        compiler_params=pltpu.CompilerParams(vmem_limit_bytes=SMALL_BYTES),
        cost_estimate=pl.CostEstimate(
            flops=2 * rows * width * peers * HD, bytes_accessed=2 * width * peers * HD, transcendentals=0
        ),
    )(place, *mixes, wo)


def turned(values, cos, sin):
    return values * cos + pltpu.roll(values, HD // 2, 1) * sin


def rope_tables(positions):
    half = HD // 2
    freq = np.exp(-(2.0 * np.arange(half) / HD) * math.log(ROPE_BASE)).astype(np.float32)
    angle = np.asarray(positions, np.float64)[:, None] * np.concatenate([freq, freq])[None].astype(np.float64)
    sign = np.where(np.arange(HD) < half, -1.0, 1.0)[None]
    return np.stack([np.cos(angle), np.sin(angle) * sign]).astype(np.float32)


def angles(cos_start, sin_start, steps):
    return cos_start * steps[0] - sin_start * steps[1], sin_start * steps[0] + cos_start * steps[1]


def start_row(starts, thr, b, extra):
    row = pl.ds(thr[b] + b * extra, 1)
    return starts[0, row, :], starts[1, row, :]


def image_kernel(high, wide, width, extra, thr, lat_t, cell, conv_t, proj_t, mapped, gram, starts, steps, steps_t, _,
                 pre_down, act_t, patch_t, q_img, qt, k_img, kt, v_img, vt):
    chan = lat_t.shape[0]
    lat = lat_t[...]
    row = cell[0:1, :]
    col = cell[1:2, :]
    for r in range(3):
        for c in range(3):
            tap = r * 3 + c
            step = (r - 1) * wide + (c - 1)
            moved = pltpu.roll(lat, -step % lat.shape[1], 1) if step else lat
            keep = (row + (r - 1) >= 0) & (row + (r - 1) < high)
            keep &= (col + (c - 1) >= 0) & (col + (c - 1) < wide)
            patch_t[0, tap * chan : (tap + 1) * chan, :] = jnp.where(keep, moved, 0.0).astype(BF16)
    cos_start, sin_start = start_row(starts, thr, pl.program_id(0), extra)
    before_t = dot(conv_t[...], patch_t[0])
    flat_t = silu(before_t).astype(BF16)
    act_t[0] = flat_t
    square = jnp.sum(dot(gram[...], flat_t) * flat_t.astype(F32), axis=0, keepdims=True)
    inv = lax.rsqrt(square * (1.0 / width) + EPSILON)
    heads_t = dot(proj_t[...], flat_t) * inv
    half = HD // 2
    column = lambda values: jnp.broadcast_to(values, (8, HD)).T[half:, :1]
    cos, sin = angles(column(cos_start), column(sin_start), steps_t)
    for at, out, scale in ((0, qt, SCALE * LOG2E), (HD, kt, 1.0)):
        first = heads_t[at : at + half]
        second = heads_t[at + half : at + HD]
        out[0, :half, :] = ((first * cos - second * sin) * scale).astype(BF16)
        out[0, half:, :] = ((second * cos + first * sin) * scale).astype(BF16)
    vt[0] = heads_t[2 * HD :].astype(BF16)
    before = before_t.T
    pre_down[0] = before
    act = silu(before).astype(BF16)
    square = jnp.sum(dot(act, gram[...]) * act.astype(F32), axis=-1, keepdims=True)
    inv = lax.rsqrt(square * (1.0 / width) + EPSILON)
    heads = dot(act, mapped[...])
    cos, sin = angles(cos_start, sin_start, steps)
    cos = cos * inv
    sin = sin * inv
    query = heads[:, :HD] * cos + heads[:, 3 * HD : 4 * HD] * sin
    q_img[0] = (query * (SCALE * LOG2E)).astype(BF16)
    k_img[0] = (heads[:, HD : 2 * HD] * cos + heads[:, 4 * HD :] * sin).astype(BF16)
    v_img[0] = (heads[:, 2 * HD : 3 * HD] * inv).astype(BF16)


def image_rows(sizes, thr, lat_t, cell, conv_t, proj_t, mapped, gram, starts, steps, steps_t, after):
    blocks = thr.shape[0]
    length = steps.shape[1]
    chan = lat_t.shape[0]
    down_chan, taps = conv_t.shape
    whole = lambda a: pl.BlockSpec(a.shape, lambda b: (0,) * len(a.shape))
    outs = [(length, down_chan, F32), (down_chan, length, BF16), (taps, length, BF16), (length, HD, BF16),
            (HD, length, BF16), (length, HD, BF16), (HD, length, BF16), (length, HD, BF16), (HD, length, BF16)]
    return pl.pallas_call(
        lambda *refs: image_kernel(*sizes, *refs),
        out_shape=[jax.ShapeDtypeStruct((blocks, r, c), kind) for r, c, kind in outs],
        grid=(blocks,),
        in_specs=[pl.BlockSpec(memory_space=pltpu.SMEM), pl.BlockSpec((chan, length), lambda b: (0, b))]
        + [whole(a) for a in (cell, conv_t, proj_t, mapped, gram, starts, steps, steps_t)]
        + [pl.BlockSpec(memory_space=pl.ANY)],
        out_specs=[pl.BlockSpec((1, r, c), lambda b: (b, 0, 0)) for r, c, _ in outs],
        compiler_params=pltpu.CompilerParams(vmem_limit_bytes=SMALL_BYTES),
        cost_estimate=pl.CostEstimate(flops=8_000_000_000, bytes_accessed=8_000_000, transcendentals=0),
    )(thr, lat_t, cell, conv_t, proj_t, mapped, gram, starts, steps, steps_t, after)


def attend_kernel(
    head, thr, text, near, far, qt, k_img, vt, u,
    part, q_txt, qt_txt, k_txt, kt_txt, mix_t, mix_txt_t, mix_txt, lse, lse_txt,
    scores, vt_txt, acc, peak, total,
):
    blocks, length, _ = k_img.shape
    text_total = q_txt.shape[0]
    row = iota((text_total, 1), 0)
    rows = text_total // blocks
    shifted = row >= sum(jnp.where(row // rows == b, thr[b], 0) for b in range(blocks))
    cos = jnp.where(shifted, far[0], near[0])
    sin = jnp.where(shifted, far[1], near[1])
    query = turned(text[:, :HD].astype(F32), cos, sin) * (SCALE * LOG2E)
    q_txt[...] = query.astype(BF16)
    qt_txt[...] = query.T.astype(BF16)
    key = turned(text[:, HD : 2 * HD].astype(F32), cos, sin)
    k_txt[...] = key.astype(BF16)
    kt_txt[...] = key.T.astype(BF16)
    vt_txt[...] = flip(text[:, 2 * HD :])

    def pair(j, _):
        mates = (j, blocks - 1 - j)
        seen = [iota((text_total, length), 0) < thr[i] for i in mates]
        for side, i in enumerate(mates):
            s = jnp.where(seen[side], dot(k_txt[...], qt[i]), NEG_SCORE)
            scores[blocks + 1 + side, :text_total, :length] = s
            peak[side] = jnp.max(s, axis=0, keepdims=True)
        turns = []
        for c in range(blocks + 1):
            first = c <= j
            side = jnp.where(first, 0, 1)
            turns.append((side, jnp.where(first, j, blocks - 1 - j), jnp.where(first, c, c - j - 1)))
        for c, (side, i, key) in enumerate(turns):
            s = dot(k_img[key], qt[i])
            scores[c, :length, :length] = s
            peak[side] = jnp.maximum(peak[side], jnp.max(s, axis=0, keepdims=True))
        for side, i in enumerate(mates):
            p = jnp.where(seen[side], jnp.exp2(scores[blocks + 1 + side, :text_total, :length] - peak[side]), 0.0)
            total[side] = jnp.sum(p, axis=0, keepdims=True)
            acc[side] = dot(vt_txt[...], p.astype(BF16))
        for c, (side, i, key) in enumerate(turns):
            p = jnp.exp2(scores[c, :length, :length] - peak[side])
            total[side] = total[side] + jnp.sum(p, axis=0, keepdims=True)
            acc[side] = acc[side] + dot(vt[key], p.astype(BF16))
        for side, i in enumerate(mates):
            mixed = acc[side] / total[side]
            lse[i] = peak[side] + jnp.log2(total[side])
            mix_t[i] = mixed.astype(BF16)
            part[i] = dot(mixed.T.astype(BF16), u[...]).astype(part.dtype)
        return 0

    lax.fori_loop(0, blocks // 2, pair, 0)

    query = qt_txt[...]
    causal = iota((text_total, text_total), 0) <= iota((text_total, text_total), 1)
    lane = iota((1, text_total), 1)
    s = jnp.where(causal, dot(k_txt[...], query), NEG_SCORE)
    s_list = [s]
    top = jnp.max(s, axis=0, keepdims=True)
    for c in range(blocks):
        s = jnp.where(lane >= thr[c], dot(k_img[c], query), NEG_SCORE)
        scores[c, :length, :text_total] = s
        top = jnp.maximum(top, jnp.max(s, axis=0, keepdims=True))
    p = jnp.where(causal, jnp.exp2(s_list[0] - top), 0.0)
    whole = jnp.sum(p, axis=0, keepdims=True)
    mixed = dot(vt_txt[...], p.astype(BF16))
    for c in range(blocks):
        p = jnp.where(lane >= thr[c], jnp.exp2(scores[c, :length, :text_total] - top), 0.0)
        whole = whole + jnp.sum(p, axis=0, keepdims=True)
        mixed = mixed + dot(vt[c], p.astype(BF16))
    mixed = mixed / whole
    lse_txt[...] = top + jnp.log2(whole)
    mix_txt_t[...] = mixed.astype(BF16)
    mix_txt[...] = mixed.T.astype(BF16)


def up_kernel(head, parts, pre_down, z, w_up_out, preds, grad_copies, prediction, grad_out_t):
    act = silu(pre_down[0]).astype(BF16)
    pre_up = dot(act, z[...])
    for p in range(parts.shape[0]):
        pre_up = pre_up + parts[p].astype(F32)
    up_act = silu(pre_up).astype(BF16)
    grad = (dot_nt(preds[...], w_up_out[...]) * silu_slope(pre_up)).astype(BF16)
    for p in range(parts.shape[0]):
        grad_copies[p] = grad
    prediction[...] = dot(up_act, w_up_out[...]).astype(BF16)
    grad_out_t[...] = dot(flip(preds[...]), up_act)


def piece_spot(place, groups, pairs, number):
    group = number // (2 * pairs) ^ place[2]
    pair = number // 2 % pairs ^ place[3]
    return group, pair, number % 2 ^ place[4]


def put_piece(place, lay, number, rows, values):
    _, groups, pairs, _, _ = lay.shape
    group, pair, core = piece_spot(place, groups, pairs, number)
    lay[core, group, pair, rows, :] = values


def hand_out(lay, sems, keep, send):
    moves = [pltpu.make_async_copy(lay.at[n], out, sems.at[n]) for n, out in enumerate((keep, send))]
    for move in moves:
        move.start()
    for move in moves:
        move.wait()


def add_core_kernel(keep, received, *outs):
    for k, out in enumerate(outs):
        out[...] = (keep[k].astype(F32) + received[k].astype(F32)).astype(BF16)


def add_sx_kernel(count, *refs):
    for m, out in enumerate(refs[count:]):
        out[...] = sum(r[m].astype(F32) for r in refs[:count]).astype(BF16)


def add_kernel(*refs):
    refs[-1][...] = sum(r[...].astype(F32) for r in refs[:-1]).astype(BF16)


def unpack_kernel(groups, pairs, own, place, *refs):
    count = 2 * groups
    grad_conv, grad_down, grad_up, grad_out_t, rest = refs[count:]
    few = refs[0].shape[1] - 2 * own
    per = HD // own
    for n, part in enumerate(refs[:count]):
        for m in range(pairs):
            number = ((place[2] ^ n % groups) * pairs + (place[3] ^ m)) * 2 + (place[4] ^ n // groups)
            grad_up[pl.ds(pl.multiple_of(number * own, own), own), :] = part[m, :own, :].astype(F32)
            cols = pl.ds(pl.multiple_of(number // per * HD, HD), HD)
            rows = pl.ds(pl.multiple_of(number % per * own, own), own)
            grad_down[rows, cols] = part[m, own : 2 * own, :].astype(F32)
            rest[pl.ds(pl.multiple_of(number * few, few), few), :] = part[m, 2 * own :, :].astype(F32)
    taps = grad_conv.shape[0]
    grad_conv[...] = rest[:taps, :]
    grad_out_t[...] = rest[taps : taps + grad_out_t.shape[0], :]


def plain(kernel, inputs, outs, after=()):
    whole = lambda a: pl.BlockSpec(a.shape, lambda: (0,) * len(a.shape))
    moved = sum(math.prod(a.shape) * a.dtype.itemsize for a in list(inputs) + list(outs))
    return pl.pallas_call(
        lambda *refs: kernel(*refs[: len(inputs)], *refs[len(inputs) + len(after) :]),
        out_shape=outs,
        in_specs=[whole(a) for a in inputs] + [pl.BlockSpec(memory_space=pl.ANY) for _ in after],
        out_specs=[whole(a) for a in outs],
        compiler_params=pltpu.CompilerParams(vmem_limit_bytes=SMALL_BYTES),
        cost_estimate=pl.CostEstimate(flops=0, bytes_accessed=moved, transcendentals=0),
    )(*inputs, *after)


def backward_kernel(
    share, copies, extra, place, thr, grad_pre, q_img, qt, k_img, kt, v_img, q_txt, qt_txt, k_txt, kt_txt,
    text, mix_t, mix_txt_t, lse, lse_txt, u, proj, gram, z, gain, starts, steps, grad_out_t, *refs,
):
    blocks, length, _ = q_img.shape
    backs = refs[:blocks]
    (pre_down_far, act_t_far, patch_t_far, wq_far, wk_far, wv_far, wo_far, w_up_far, w_down_far,
     keep, send,
     dq, dk, dv, d_out, d_t, dq_t, d_txt, cross_sum, small_sum,
     pre_down, act_t, patch_t, wq, wk, wv, wo, w_up, w_down, lay, sems) = refs[blocks:]
    text_total = q_txt.shape[0]
    width = w_down.shape[1]
    cols = pl.ds(pl.multiple_of(place[0] * HD, HD), HD)
    moves = [(pre_down_far, pre_down), (act_t_far, act_t), (patch_t_far, patch_t), (wq_far.at[:, cols], wq),
             (wk_far.at[:, cols], wk), (wv_far.at[:, cols], wv), (wo_far.at[cols, :], wo), (w_up_far, w_up),
             (w_down_far, w_down)]
    moves = [pltpu.make_async_copy(far, near, sems.at[n]) for n, (far, near) in enumerate(moves)]
    for move in moves:
        move.start()
    cross_sum[...] = jnp.zeros_like(cross_sum)
    small_sum[...] = jnp.zeros_like(small_sum)
    v_txt = text[:, 2 * HD :]
    rows = text_total // blocks
    for k, back in enumerate(backs):
        d_txt[pl.ds(pl.multiple_of((place[5] ^ k) * rows, rows), rows), :] = back[:, :HD]
    d_txt_t = d_txt[...].astype(F32).T
    delta_txt = jnp.sum(d_txt_t * mix_txt_t[...].astype(F32), axis=0, keepdims=True)
    d_txt_t = d_txt_t.astype(BF16)
    lane = iota((1, text_total), 1)
    for c in range(blocks):
        p = jnp.where(lane >= thr[c], jnp.exp2(dot(k_img[c], qt_txt[...]) - lse_txt[...]), 0.0)
        ds = p * (dot(v_img[c], d_txt_t) - delta_txt)
        dk[c] = dot(ds.astype(BF16), q_txt[...])
        dv[c] = dot(p.astype(BF16), d_txt[...])

    def pair(j, _):
        mates = (j, blocks - 1 - j)
        delta = []
        for side, i in enumerate(mates):
            grad = grad_pre[i]
            cross_sum[...] += dot(mix_t[i], grad)
            d_out[side] = dot_nt(grad, u[...]).astype(BF16)
            turned_grad = dot_nt(u[...], grad).astype(BF16)
            d_t[side] = turned_grad
            delta.append(jnp.sum(turned_grad.astype(F32) * mix_t[i].astype(F32), axis=0, keepdims=True))
        for side, i in enumerate(mates):
            seen = iota((text_total, length), 0) < thr[i]
            p = jnp.where(seen, jnp.exp2(dot(k_txt[...], qt[i]) - lse[i]), 0.0)
            ds = p * (dot(v_txt, d_t[side]) - delta[side])
            dq_t[side] = dot(kt_txt[...], ds.astype(BF16))
        for c in range(blocks + 1):
            first = c <= j
            side = jnp.where(first, 0, 1)
            i = jnp.where(first, j, blocks - 1 - j)
            key = jnp.where(first, c, c - j - 1)
            p = jnp.exp2(dot(k_img[key], qt[i]) - lse[i])
            ds = (p * (dot(v_img[key], d_t[side]) - jnp.where(first, delta[0], delta[1]))).astype(BF16)
            dv[key] = dv[key] + dot(p.astype(BF16), d_out[side])
            dk[key] = dk[key] + dot(ds, q_img[i])
            dq_t[side] = dq_t[side] + dot(kt[key], ds)
        for side in range(2):
            dq[mates[side]] = dq_t[side].T
        return 0

    lax.fori_loop(0, blocks // 2, pair, 0)
    for move in moves:
        move.wait()
    taps = patch_t.shape[1]

    def block(b, query):
        cos, sin = angles(*start_row(starts, thr, b, extra), steps)

        def back(values):
            return values * cos - pltpu.roll(values, HD // 2, 1) * sin

        before = pre_down[b]
        act = silu(before).astype(BF16)
        act_wide = act.astype(F32)
        image = dot(act, gram[...])
        square = jnp.sum(image * act_wide, axis=-1, keepdims=True)
        inv = lax.rsqrt(square * (1.0 / width) + EPSILON)
        heads = jnp.concatenate(
            [back(query) * (inv * SCALE), back(dk[b]) * (inv * LN2), dv[b] * inv], axis=1
        ).astype(BF16)
        lift = dot_nt(heads, proj[...])
        crow = inv * inv * (jnp.sum(act_wide * lift, axis=-1, keepdims=True) * (1.0 / width))
        grad = grad_pre[b]
        d_act = (lift - crow * image) * copies + dot_nt(grad, z[...]) * share
        slope = (d_act * silu_slope(before)).astype(BF16)
        flipped = act_t[b]
        return (
            dot(patch_t[b], slope),
            dot(flipped, heads),
            dot(flipped, (act_wide * crow).astype(BF16)),
            dot(flipped, grad),
        )

    def step(n, carry):
        for b in (n, blocks // 2 + n):
            conv, *more = block(b, dq[b])
            small_sum[:taps, :] += conv
            carry = tuple(a + m for a, m in zip(carry, more))
        return carry

    rank = act_t.shape[1]
    spread, pull, inner = lax.fori_loop(
        0, blocks // 2, step,
        (jnp.zeros((rank, 3 * HD), F32), jnp.zeros((rank, rank), F32), jnp.zeros((rank, grad_pre.shape[2]), F32)),
    )
    spread = (spread * copies).astype(BF16)
    pull = (pull * copies).astype(BF16)
    cross = (cross_sum[...] * copies).T.astype(BF16)
    inner_t = (inner * share).T.astype(BF16)
    inner = (inner * share).astype(BF16)
    small_sum[taps : taps + grad_out_t.shape[0], :] = grad_out_t[...]
    _, groups, pairs, rows, _ = lay.shape
    own = width // (2 * groups * pairs)
    few = rows - 2 * own
    for at in range(0, width, HD):
        cols = slice(at, at + HD)
        down = dot_nt(spread[:, :HD], wq[cols, :]) + dot_nt(spread[:, HD : 2 * HD], wk[cols, :])
        down = (down + dot_nt(spread[:, 2 * HD :], wv[cols, :])) * gain[:, cols].astype(F32)
        down = (down - dot(pull, w_down[:, cols]) + dot_nt(inner, w_up[cols, :])).astype(BF16)
        up = (dot(cross, wo[:, cols]) + dot(inner_t, w_down[:, cols])).T.astype(BF16)
        for part in range(0, HD, own):
            put_piece(place, lay, (at + part) // own, slice(0, own), up[part : part + own])
            put_piece(place, lay, (at + part) // own, slice(own, 2 * own), down[part : part + own])
    for number in range(2 * groups * pairs):
        put_piece(place, lay, number, slice(2 * own, rows), small_sum[number * few : (number + 1) * few, :].astype(BF16))
    hand_out(lay, sems, keep, send)


def shards(
    text_tokens,
    latent,
    image_offset,
    norm_gain,
    w_query,
    w_key,
    w_value,
    w_out,
    w_down_conv,
    w_down_proj,
    w_up_proj,
    w_up_out,
    pred_grad,
    text_grad,
):
    axes = ("sy", "sx")
    text_local = text_tokens[0]
    text_rows, width = text_local.shape
    lat_chan = w_up_out.shape[1]
    up_chan = w_up_proj.shape[1]
    down_chan = w_down_conv.shape[1]
    taps = w_down_conv.shape[0]
    tile_rows = latent.shape[1]
    tile_cols = latent.shape[2] // lat_chan
    row_groups = lax.axis_size("sx")
    blocks = lax.axis_size("sy")
    devices = row_groups * blocks
    high = tile_rows * row_groups
    length = high * tile_cols
    text_block = text_rows * row_groups
    text_total = text_block * blocks
    total = length * blocks
    block_len = length + text_block
    heads_here = w_query.shape[1] // HD
    repeat = blocks // heads_here
    assert heads_here * repeat == blocks and blocks % 2 == 0
    own = lax.axis_index("sy")
    share = 1.0 / devices
    copies = 1.0 / repeat

    device = own * row_groups + lax.axis_index("sx").astype(jnp.int32)
    group = lax.axis_index("sx").astype(jnp.int32)
    own = own.astype(jnp.int32)
    head = jnp.stack([own // repeat, device, group, own // 2, own % 2, own])

    def spread_over(values, axis, count):
        return lax.all_to_all(jnp.broadcast_to(values[None], (count,) + values.shape), axis, 0, 0)

    tag = jnp.broadcast_to(image_offset.astype(BF16)[:, None], (tile_rows, HD))
    packed = jnp.concatenate([latent[0], tag], axis=1)
    hop = lambda values, axis, by: lax.ppermute(
        values, axis, [(i, i ^ by) for i in range(row_groups if axis == "sx" else blocks)]
    )
    text_parts = [text_local] + [hop(text_local, "sx", k) for k in range(1, row_groups)]
    text_grad_parts = [text_grad[0]] + [hop(text_grad[0], "sx", k) for k in range(1, row_groups)]
    side = spread_over(packed, axes, devices)

    gain = norm_gain.reshape(1, width)
    small = jax.ShapeDtypeStruct
    square = small((down_chan, down_chan), BF16)
    proj, proj_t, mapped, u, gram, z, conv_t = small_products(
        head, w_query, w_key, w_value, w_out, gain, w_down_proj, w_up_proj, w_down_conv
    )

    def to_heads(values):
        return lax.all_to_all(jnp.repeat(values, repeat, axis=0) if repeat > 1 else values, "sy", 0, 0)

    text_here = text_heads(head, text_parts, gain, w_query, w_key, w_value, proj)
    text = to_heads(text_here).reshape(text_total, 3 * HD)

    side = side.reshape(blocks, row_groups, tile_rows, -1)
    lat_t = side[..., : tile_cols * lat_chan].reshape(total, lat_chan).T.astype(F32)
    offsets = side[:, 0, 0, tile_cols * lat_chan].astype(jnp.int32)
    block_ids = jnp.arange(blocks, dtype=jnp.int32)
    thr = block_ids * text_block + offsets
    ids = np.arange(length, dtype=np.int32)
    cell = np.stack([ids // tile_cols, ids % tile_cols])
    at = np.arange(blocks)[:, None]
    steps = rope_tables(ids)
    steps_t = np.ascontiguousarray(np.swapaxes(steps, 1, 2)[:, HD // 2 :])
    starts = rope_tables((at * block_len + np.arange(text_block + 1)).reshape(-1))
    near = (at * block_len + np.arange(text_block)).reshape(-1)
    near, far = rope_tables(near), rope_tables(near + length)

    chunk = lambda kind, rows=length, cols=HD: small((blocks, rows, cols), kind)
    text_kind = small((text_total, HD), BF16)
    text_flip = small((HD, text_total), BF16)
    side_len = max(length, text_total)
    pre_down, act_t, patch_t, q_img, qt, k_img, kt, v_img, vt = image_rows(
        (high, tile_cols, width, 1), thr, lat_t, cell, conv_t, proj_t, mapped, gram, starts, steps, steps_t, text_here
    )
    part, q_txt, qt_txt, k_txt, kt_txt, mix_t, mix_txt_t, mix_txt, lse, lse_txt = call(
        attend_kernel, head,
        [(thr, "smem"), (text, None), (near, None), (far, None), (qt, None), (k_img, None), (vt, None), (u, None)],
        [chunk(BF16, length, up_chan), text_kind, text_flip, text_kind, text_flip, chunk(BF16, HD, length),
         text_flip, text_kind, small((blocks, 1, length), F32), small((1, text_total), F32)],
        [pltpu.VMEM((blocks + 3, side_len, side_len), F32), pltpu.VMEM((HD, text_total), BF16),
         pltpu.VMEM((2, HD, length), F32), pltpu.VMEM((2, 1, length), F32), pltpu.VMEM((2, 1, length), F32)],
        flops=6_000_000_000,
    )

    own_rows = tile_rows * tile_cols
    part = part if repeat == 1 else part * jnp.asarray(copies, BF16)
    parts = lax.all_to_all(part.reshape(devices, own_rows, up_chan), axes, 0, 0)
    text_back = text_grad_heads(head, text_grad_parts, w_out, mix_txt, repeat, part)
    text_back = [text_back[0]] + [hop(text_back[k], "sy", k) for k in range(1, blocks)]
    grad_copies, prediction, grad_out_t = call(
        up_kernel, head,
        [(parts, None), (pre_down.reshape(devices, own_rows, down_chan), "mine"), (z, None), (w_up_out, None),
         (pred_grad[0].reshape(own_rows, lat_chan), None)],
        [small((devices, own_rows, up_chan), BF16), small((own_rows, lat_chan), BF16), small((lat_chan, up_chan), F32)],
        flops=2_000_000_000,
        after=text_back[:1],
        room=SMALL_BYTES,
    )
    grad_pre = lax.all_to_all(grad_copies, axes, 0, 0).reshape(blocks, length, up_chan)

    mixed = text_out_parts(head, text_back, w_out, repeat, row_groups)
    mixed = [mixed[0]] + [hop(mixed[k], "sx", k) for k in range(1, row_groups)]
    text_out = (text_local.astype(F32) + sum(m.astype(F32) for m in mixed)).astype(BF16)

    pairs = blocks // 2
    own_part = width // devices
    few = -(-(taps + lat_chan) // (16 * devices)) * 16
    piece = lambda rows: small((row_groups, pairs, rows, HD), BF16)
    lump = lambda rows: small((pairs, rows, HD), BF16)
    flat = lambda rows: small((rows, HD), BF16)
    vmem = pltpu.VMEM
    lay = lambda rows: vmem((2, row_groups, pairs, rows, HD), BF16)

    def core_sum(keep, send, rows):
        return plain(add_core_kernel, [keep, hop(send, "sy", 1)], [lump(rows)] * row_groups)

    def sx_sum(sums, rows, after=()):
        sums = [sums[0]] + [hop(sums[k], "sx", k) for k in range(1, row_groups)]
        return plain(lambda *refs: add_sx_kernel(row_groups, *refs), sums, [flat(rows)] * pairs, after)

    def z_sum(sums, rows, after=()):
        sums = [sums[0]] + [hop(sums[m], "sy", 2 * m) for m in range(1, pairs)]
        return plain(add_kernel, sums, [flat(rows)], after)[0]

    def spread_z(mine):
        return jnp.stack([mine] + [hop(mine, "sy", 2 * m) for m in range(1, pairs)])

    def spread_sx(mine):
        near = [mine] + [hop(mine, "sx", k) for k in range(1, row_groups)]
        return near + [hop(values, "sy", 1) for values in near]

    wide = vmem((blocks, length, HD), F32)
    rows = 2 * own_part + few
    keep, send = call(
        lambda *refs: backward_kernel(share, copies, 1, *refs), head,
        [(thr, "smem")] + [(a, None) for a in (
            grad_pre, q_img, qt, k_img, kt, v_img, q_txt, qt_txt, k_txt, kt_txt, text, mix_t, mix_txt_t, lse, lse_txt,
            u, proj, gram, z, gain, starts, steps, grad_out_t, *text_back)]
        + [(a, "any") for a in (
            pre_down, act_t, patch_t, w_query, w_key, w_value, w_out, w_up_proj, w_down_proj)],
        [piece(rows)] * 2,
        [wide, wide, wide, vmem((2, length, HD), BF16), vmem((2, HD, length), BF16), vmem((2, HD, length), F32),
         vmem((text_total, HD), BF16), vmem((HD, up_chan), F32), vmem((devices * few, HD), F32)]
        + [vmem(a.shape, a.dtype) for a in (pre_down, act_t, patch_t)]
        + [vmem((width, HD), BF16)] * 3
        + [vmem((HD, width), BF16), vmem(w_up_proj.shape, BF16), vmem(w_down_proj.shape, BF16), lay(rows),
           pltpu.SemaphoreType.DMA((9,))],
        flops=30_000_000_000,
        after=[text_out],
        out_kind="any",
    )
    mine = spread_z(z_sum(sx_sum(core_sum(keep, send, rows), rows), rows))
    grad_conv, grad_down, grad_up, grad_out_t = call(
        lambda *refs: unpack_kernel(row_groups, pairs, own_part, *refs), head,
        [(a, None) for a in spread_sx(mine)],
        [small((taps, down_chan), F32), small((down_chan, width), F32), small((width, up_chan), F32),
         small((lat_chan, up_chan), F32)],
        [vmem((devices * few, HD), F32)],
        room=2 * SMALL_BYTES,
    )
    return (
        prediction.reshape(1, tile_rows, tile_cols * lat_chan),
        text_out[None],
        grad_conv,
        grad_down,
        grad_up,
        grad_out_t.T,
    )


def solution(mesh):
    placed = (
        P("sy", "sx", None),
        P("sy", "sx", None),
        P("sy"),
        P(),
        P(None, "sx"),
        P(None, "sx"),
        P(None, "sx"),
        P("sx", None),
        P(),
        P(),
        P(),
        P(),
        P("sy", "sx", None),
        P("sy", "sx", None),
    )
    return jax.shard_map(
        shards,
        mesh=mesh,
        in_specs=placed,
        out_specs=(P("sy", "sx", None), P("sy", "sx", None), P(), P(), P(), P()),
        check_vma=False,
    )
```

```python
import math

import jax
import jax.numpy as jnp
import numpy as np
from jax import lax
from jax.experimental import pallas as pl
from jax.experimental.pallas import tpu as pltpu
from jax.sharding import PartitionSpec as P

HD = 128
EPSILON = 1e-05
NEG_SCORE = -1e30
ROPE_BASE = 500000.0
SCALE = HD ** (-0.5)
LOG2E = math.log2(math.e)
LN2 = math.log(2.0)
F32 = jnp.float32
BF16 = jnp.bfloat16
MIB = 1024 * 1024
VMEM_BYTES = 56 * MIB
SMALL_BYTES = 16 * MIB


def dot(left, right):
    return jnp.dot(left, right, preferred_element_type=F32)


def dot_nt(left, right):
    return lax.dot_general(left, right, (((1,), (1,)), ((), ())), preferred_element_type=F32)


def silu_slope(values):
    sigma = jax.nn.sigmoid(values)
    return sigma * (1.0 + values * (1.0 - sigma))


def silu(values):
    return values * jax.nn.sigmoid(values)


def iota(shape, dim):
    return lax.broadcasted_iota(jnp.int32, shape, dim)


def flip(values):
    return values.astype(F32).T.astype(BF16)


def call(kernel, place, inputs, outs, scratch=(), flops=0, after=(), room=VMEM_BYTES):
    inputs = [(place, pltpu.SMEM)] + list(inputs)
    count = len(inputs)
    skip = count + len(after)
    moved = sum(math.prod(a.shape) * a.dtype.itemsize for a in list(outs) + [a for a, space in inputs if space is None])
    return pl.pallas_call(
        lambda *refs: kernel(*refs[:count], *refs[skip:]),
        out_shape=outs,
        in_specs=[pl.BlockSpec(memory_space=pltpu.VMEM if space is None else space) for _, space in inputs]
        + [pl.BlockSpec(memory_space=pl.ANY) for _ in after],
        out_specs=[pl.BlockSpec(memory_space=pltpu.VMEM) for _ in outs],
        scratch_shapes=list(scratch),
        compiler_params=pltpu.CompilerParams(vmem_limit_bytes=room),
        cost_estimate=pl.CostEstimate(flops=flops, bytes_accessed=moved, transcendentals=0),
    )(*[a for a, _ in inputs], *after)


def fetch(moves, sems):
    moves = [pltpu.make_async_copy(far, near, sems.at[n]) for n, (far, near) in enumerate(moves)]
    for move in moves:
        move.start()
    return moves


def whole_row(gain):
    return jnp.concatenate([gain[r : r + 1, :].astype(F32) for r in range(gain.shape[0])], axis=1)


def weights_kernel(
    place, gain, w_conv, w_down_far, wq_far, wk_far, wv_far, w_up_far, wo_far,
    proj, proj_t, mapped, u, gram, z, conv_t,
    w_down, wq, wk, wv, w_up, wo, sems,
):
    cols = pl.ds(pl.multiple_of(place[0] * HD, HD), HD)
    moves = fetch(
        [(w_down_far, w_down), (wq_far.at[:, cols], wq), (wk_far.at[:, cols], wk), (wv_far.at[:, cols], wv),
         (w_up_far, w_up), (wo_far.at[cols, :], wo)],
        sems,
    )
    conv_t[...] = flip(w_conv[...])
    moves[0].wait()
    down = w_down[...]
    scaled = (down.astype(F32) * whole_row(gain)).astype(BF16)
    gram[...] = dot_nt(down, down).astype(BF16)
    for n, w in enumerate((wq, wk, wv)):
        cols = slice(n * HD, (n + 1) * HD)
        moves[1 + n].wait()
        total = dot(scaled, w[...])
        proj[:, cols] = total.astype(BF16)
        proj_t[cols, :] = total.T.astype(BF16)
        mapped[:, cols] = total.astype(BF16)
        if n < 2:
            mapped[:, (3 + n) * HD : (4 + n) * HD] = pltpu.roll(total, HD // 2, 1).astype(BF16)
    moves[4].wait()
    z[...] = dot(down, w_up[...]).astype(BF16)
    moves[5].wait()
    u[...] = dot(wo[...], w_up[...]).astype(BF16)


def pick(rows, total, spot):
    return (iota((total, rows), 0) == iota((total, rows), 1) + spot).astype(BF16)


def gathered(parts, group):
    rows = parts[0].shape[0]
    total = rows * len(parts)
    return sum(dot(pick(rows, total, (group ^ k) * rows), part[...]) for k, part in enumerate(parts))


def text_kernel(count, repeat, place, *refs):
    gain, wq_far, wk_far, wv_far = refs[:4]
    parts = refs[4 : 4 + count]
    outs = refs[4 + count : -4]
    weights, normed, sums, sems = refs[-4:]
    chunks, _, deep, wide = weights.shape
    cols = pl.ds(pl.multiple_of(place[4] * wide, wide), wide)
    moves = fetch(
        [(far.at[c * deep : (c + 1) * deep, cols], weights.at[c, n])
         for c in range(chunks) for n, far in enumerate((wq_far, wk_far, wv_far))],
        sems,
    )
    rows = normed.shape[0] // 2
    row = whole_row(gain)
    for r in range(2):
        x = gathered([part.at[r] for part in parts], place[2])
        inverse = lax.rsqrt(jnp.mean(x * x, axis=-1, keepdims=True) + EPSILON)
        normed[r * rows : (r + 1) * rows, :] = (x * inverse * row).astype(BF16)
    for c in range(chunks):
        here = normed[:, c * deep : (c + 1) * deep]
        for n in range(3):
            moves[3 * c + n].wait()
            term = dot(here, weights[c, n])
            sums[n] = term if c == 0 else sums[n] + term
    for k, out in enumerate(outs):
        head = pl.ds(pl.multiple_of((place[3] ^ k) // repeat * HD, HD), HD)
        for n in range(3):
            out[:, n * HD : (n + 1) * HD] = sums[n, :, head].astype(BF16)


def text_grad_kernel(count, repeat, place, wo_far, mix, *refs):
    parts = refs[:count]
    outs = refs[count : -3]
    wo, total, sems = refs[-3:]
    groups, deep, _ = wo.shape
    moves = fetch([(wo_far.at[g * deep : (g + 1) * deep, :], wo.at[g]) for g in range(groups)], sems)
    grad_t = gathered(parts, place[2]).T.astype(BF16)
    for g in range(groups):
        moves[g].wait()
        total[g * deep : (g + 1) * deep, :] = dot(wo[g], grad_t)
    for k, out in enumerate(outs):
        peer = place[5] ^ k
        rows = out.shape[0]
        out[:, :HD] = total[pl.ds(pl.multiple_of(peer // repeat * HD, HD), HD), :].T.astype(BF16)
        out[:, HD:] = mix[pl.ds(pl.multiple_of(peer * rows, rows), rows), :]


def text_out_kernel(repeat, peers, place, wo_far, *refs):
    mixes = refs[:peers]
    outs = refs[peers:-3]
    wo, mixed, sems = refs[-3:]
    groups, deep, width = wo.shape
    moves = fetch([(wo_far.at[g * deep : (g + 1) * deep, :], wo.at[g]) for g in range(groups)], sems)
    for k, mix in enumerate(mixes):
        peer = place[5] ^ k

        @pl.when(peer % repeat == 0)
        def _():
            mixed[:, pl.ds(pl.multiple_of(peer // repeat * HD, HD), HD)] = mix[:, HD:]

    total = 0.0
    for g in range(groups):
        moves[g].wait()
        total = total + dot(mixed[:, g * deep : (g + 1) * deep], wo[g])
    whole = total.astype(BF16)
    for k, out in enumerate(outs):
        rows = out.shape[0]
        out[...] = dot(pick(rows, whole.shape[0], (place[2] ^ k) * rows).astype(F32).T.astype(BF16), whole).astype(BF16)


def turned(values, cos, sin):
    return values * cos + pltpu.roll(values, HD // 2, 1) * sin


def rope_tables(positions):
    half = HD // 2
    freq = np.exp(-(2.0 * np.arange(half) / HD) * math.log(ROPE_BASE)).astype(np.float32)
    angle = np.asarray(positions, np.float64)[:, None] * np.concatenate([freq, freq])[None].astype(np.float64)
    sign = np.where(np.arange(HD) < half, -1.0, 1.0)[None]
    return np.stack([np.cos(angle), np.sin(angle) * sign]).astype(np.float32)


def angles(cos_start, sin_start, steps):
    return cos_start * steps[0] - sin_start * steps[1], sin_start * steps[0] + cos_start * steps[1]


def start_row(starts, thr, b, extra):
    row = pl.ds(thr[b] + b * extra, 1)
    return starts[0, row, :], starts[1, row, :]


def image_kernel(high, wide, width, extra, thr, lat_t, cell, conv_t, proj_t, mapped, gram, starts, steps, steps_t, *refs):
    pre_down, act_t, patch_t, q_img, qt, k_img, kt, v_img, vt = refs[-9:]
    chan = lat_t.shape[0]
    lat = lat_t[...]
    row = cell[0:1, :]
    col = cell[1:2, :]
    for r in range(3):
        for c in range(3):
            tap = r * 3 + c
            step = (r - 1) * wide + (c - 1)
            moved = pltpu.roll(lat, -step % lat.shape[1], 1) if step else lat
            keep = (row + (r - 1) >= 0) & (row + (r - 1) < high)
            keep &= (col + (c - 1) >= 0) & (col + (c - 1) < wide)
            patch_t[0, tap * chan : (tap + 1) * chan, :] = jnp.where(keep, moved, 0.0).astype(BF16)
    cos_start, sin_start = start_row(starts, thr, pl.program_id(0), extra)
    before_t = dot(conv_t[...], patch_t[0])
    flat_t = silu(before_t).astype(BF16)
    act_t[0] = flat_t
    square = jnp.sum(dot(gram[...], flat_t) * flat_t.astype(F32), axis=0, keepdims=True)
    inv = lax.rsqrt(square * (1.0 / width) + EPSILON)
    heads_t = dot(proj_t[...], flat_t) * inv
    half = HD // 2
    column = lambda values: jnp.broadcast_to(values, (8, HD)).T[half:, :1]
    cos, sin = angles(column(cos_start), column(sin_start), steps_t)
    for at, out, scale in ((0, qt.at[0], SCALE * LOG2E), (HD, kt, 1.0)):
        first = heads_t[at : at + half]
        second = heads_t[at + half : at + HD]
        out[:half, :] = ((first * cos - second * sin) * scale).astype(BF16)
        out[half:, :] = ((second * cos + first * sin) * scale).astype(BF16)
    vt[...] = heads_t[2 * HD :].astype(BF16)
    before = before_t.T
    pre_down[0] = before
    act = silu(before).astype(BF16)
    square = jnp.sum(dot(act, gram[...]) * act.astype(F32), axis=-1, keepdims=True)
    inv = lax.rsqrt(square * (1.0 / width) + EPSILON)
    heads = dot(act, mapped[...])
    cos, sin = angles(cos_start, sin_start, steps)
    cos = cos * inv
    sin = sin * inv
    query = heads[:, :HD] * cos + heads[:, 3 * HD : 4 * HD] * sin
    q_img[0] = (query * (SCALE * LOG2E)).astype(BF16)
    k_img[0] = (heads[:, HD : 2 * HD] * cos + heads[:, 4 * HD :] * sin).astype(BF16)
    v_img[0] = (heads[:, 2 * HD : 3 * HD] * inv).astype(BF16)


def image_rows(sizes, thr, lat_t, cell, conv_t, proj_t, mapped, gram, starts, steps, steps_t, after):
    blocks = thr.shape[0]
    length = steps.shape[1]
    chan = lat_t.shape[0]
    down_chan, taps = conv_t.shape
    whole = lambda a: pl.BlockSpec(a.shape, lambda b: (0,) * len(a.shape))
    outs = [(length, down_chan, F32), (down_chan, length, BF16), (taps, length, BF16), (length, HD, BF16),
            (HD, length, BF16), (length, HD, BF16), None, (length, HD, BF16), None]
    flat = pl.BlockSpec((HD, length), lambda b: (0, b))
    return pl.pallas_call(
        lambda *refs: image_kernel(*sizes, *refs),
        out_shape=[jax.ShapeDtypeStruct((blocks, *o[:2]), o[2]) if o else jax.ShapeDtypeStruct((HD, blocks * length), BF16)
                   for o in outs],
        grid=(blocks,),
        in_specs=[pl.BlockSpec(memory_space=pltpu.SMEM), pl.BlockSpec((chan, length), lambda b: (0, b))]
        + [whole(a) for a in (cell, conv_t, proj_t, mapped, gram, starts, steps, steps_t)]
        + [pl.BlockSpec(memory_space=pl.ANY) for _ in after],
        out_specs=[pl.BlockSpec((1, *o[:2]), lambda b: (b, 0, 0)) if o else flat for o in outs],
        compiler_params=pltpu.CompilerParams(vmem_limit_bytes=VMEM_BYTES),
        cost_estimate=pl.CostEstimate(flops=8_000_000_000, bytes_accessed=8_000_000, transcendentals=0),
    )(thr, lat_t, cell, conv_t, proj_t, mapped, gram, starts, steps, steps_t, *after)


STRIP = 128


def strips(rows):
    return [slice(at, at + STRIP) for at in range(0, rows, STRIP)]


def attend_kernel(
    head, thr, near, far, u, qt_far, k_img_far, vt_far, *refs,
):
    texts = refs[:-18]
    (part, q_txt, qt_txt, k_txt, kt_txt, v_txt, mix_t, mix_txt_t, mix_txt, lse, lse_txt,
     scores, probs, text, qt, keys, vt, sems) = refs[-18:]
    blocks, length, _ = part.shape
    text_total = q_txt.shape[0]
    moves = fetch(
        [(k_img_far, keys.at[text_total:, :]), (qt_far, qt), (vt_far, vt.at[:, text_total:])], sems
    )
    row = iota((text_total, 1), 0)
    rows = text_total // blocks
    core = head[5] // len(texts)
    for k, values in enumerate(texts):
        pair = head[5] % len(texts) ^ k
        for r in range(2):
            spot = pl.ds(pl.multiple_of((2 * pair + (core ^ r)) * rows, rows), rows)
            text[spot, :] = values[r * rows : (r + 1) * rows, :]
    shifted = row >= sum(jnp.where(row // rows == b, thr[b], 0) for b in range(blocks))
    cos = jnp.where(shifted, far[0], near[0])
    sin = jnp.where(shifted, far[1], near[1])
    query = turned(text[:, :HD].astype(F32), cos, sin) * (SCALE * LOG2E)
    q_txt[...] = query.astype(BF16)
    qt_txt[...] = query.T.astype(BF16)
    key = turned(text[:, HD : 2 * HD].astype(F32), cos, sin)
    k_txt[...] = key.astype(BF16)
    keys[:text_total, :] = key.astype(BF16)
    kt_txt[...] = key.T.astype(BF16)
    v_txt[...] = text[:, 2 * HD :]
    vt[:, :text_total] = flip(text[:, 2 * HD :])
    for move in moves:
        move.wait()

    def softmax(turned_query, count, seen):
        wide = turned_query.shape[1]
        scores[:count, :wide] = dot(keys[:count, :], turned_query)
        top = None
        for at in strips(count):
            s = scores[at, :wide]
            mask = seen(at)
            if mask is not None:
                s = jnp.where(mask, s, NEG_SCORE)
                scores[at, :wide] = s
            peak = jnp.max(s, axis=0, keepdims=True)
            top = peak if top is None else jnp.maximum(top, peak)
        whole = 0.0
        for at in strips(count):
            p = jnp.exp2(scores[at, :wide] - top)
            mask = seen(at)
            if mask is not None:
                p = jnp.where(mask, p, 0.0)
            whole = whole + jnp.sum(p, axis=0, keepdims=True)
            probs[at, :wide] = p.astype(BF16)
        return dot(vt[:, :count], probs[:count, :wide]) / whole, top + jnp.log2(whole)

    for i in range(blocks):
        mixed, logs = softmax(
            qt[i], text_total + (i + 1) * length,
            lambda at: iota((STRIP, length), 0) + at.start < thr[i] if at.start < text_total else None,
        )
        lse[i] = logs
        mix_t[i] = mixed.astype(BF16)
        part[i] = dot(mixed.T.astype(BF16), u[...]).astype(part.dtype)
    lane = iota((1, text_total), 1)
    mixed, logs = softmax(
        qt_txt[...], text_total + blocks * length,
        lambda at: iota((STRIP, text_total), 0) + at.start <= lane
        if at.start < text_total else lane >= thr[(at.start - text_total) // length],
    )
    lse_txt[...] = logs
    mix_txt_t[...] = mixed.astype(BF16)
    mix_txt[...] = mixed.T.astype(BF16)


def up_kernel(head, parts, pre_down, z, w_up_out, preds, grad_copies, prediction, grad_out_t):
    act = silu(pre_down[head[1]]).astype(BF16)
    pre_up = dot(act, z[...])
    for p in range(parts.shape[0]):
        pre_up = pre_up + parts[p].astype(F32)
    up_act = silu(pre_up).astype(BF16)
    grad = (dot_nt(preds[...], w_up_out[...]) * silu_slope(pre_up)).astype(BF16)
    for p in range(parts.shape[0]):
        grad_copies[p] = grad
    prediction[...] = dot(up_act, w_up_out[...]).astype(BF16)
    grad_out_t[...] = dot(flip(preds[...]), up_act)


def piece_spot(place, groups, pairs, number):
    group = number // (2 * pairs) ^ place[2]
    pair = number // 2 % pairs ^ place[3]
    return group, pair, number % 2 ^ place[4]


def put_piece(place, pieces, number, rows, values):
    _, groups, pairs, _, _ = pieces.shape
    group, pair, core = piece_spot(place, groups, pairs, number)
    pieces[core, group, pair, rows, :] = values


def add_core_kernel(pieces, received, *outs):
    for k, out in enumerate(outs):
        out[...] = (pieces[0, k].astype(F32) + received[k].astype(F32)).astype(BF16)


def add_sx_kernel(count, *refs):
    for m, out in enumerate(refs[count:]):
        out[...] = sum(r[m].astype(F32) for r in refs[:count]).astype(BF16)


def add_kernel(*refs):
    refs[-1][...] = sum(r[...].astype(F32) for r in refs[:-1]).astype(BF16)


def unpack_kernel(groups, pairs, own, place, *refs):
    count = 2 * groups
    grad_conv, grad_down, grad_up, grad_out_t, rest = refs[count:]
    few = refs[0].shape[1] - 2 * own
    per = HD // own
    for n, part in enumerate(refs[:count]):
        for m in range(pairs):
            number = ((place[2] ^ n % groups) * pairs + (place[3] ^ m)) * 2 + (place[4] ^ n // groups)
            grad_up[pl.ds(pl.multiple_of(number * own, own), own), :] = part[m, :own, :].astype(F32)
            cols = pl.ds(pl.multiple_of(number // per * HD, HD), HD)
            rows = pl.ds(pl.multiple_of(number % per * own, own), own)
            grad_down[rows, cols] = part[m, own : 2 * own, :].astype(F32)
            rest[pl.ds(pl.multiple_of(number * few, few), few), :] = part[m, 2 * own :, :].astype(F32)
    taps = grad_conv.shape[0]
    grad_conv[...] = rest[:taps, :]
    grad_out_t[...] = rest[taps : taps + grad_out_t.shape[0], :]


def plain(kernel, inputs, outs, after=()):
    whole = lambda a: pl.BlockSpec(a.shape, lambda: (0,) * len(a.shape))
    moved = sum(math.prod(a.shape) * a.dtype.itemsize for a in list(inputs) + list(outs))
    return pl.pallas_call(
        lambda *refs: kernel(*refs[: len(inputs)], *refs[len(inputs) + len(after) :]),
        out_shape=outs,
        in_specs=[whole(a) for a in inputs] + [pl.BlockSpec(memory_space=pl.ANY) for _ in after],
        out_specs=[whole(a) for a in outs],
        compiler_params=pltpu.CompilerParams(vmem_limit_bytes=SMALL_BYTES),
        cost_estimate=pl.CostEstimate(flops=0, bytes_accessed=moved, transcendentals=0),
    )(*inputs, *after)


def backward_kernel(
    share, copies, extra, place, thr, grad_pre, q_txt, qt_txt, k_txt, kt_txt, v_txt, mix_txt_t, lse, lse_txt,
    u, proj, gram, z, gain, starts, steps, grad_out_t, *refs,
):
    blocks, length, _ = grad_pre.shape
    backs = refs[:blocks]
    (k_img_far, v_img_far, qt_far, kt_far, q_img_far, mix_t_far, pre_down_far, act_t_far, patch_t_far,
     wq_far, wk_far, wv_far, wo_far, w_up_far, w_down_far,
     pieces,
     dq, dk, dv, d_txt, cross_sum, small_sum, scores, pulls, probs, slopes,
     keys, values, qt, kt, q_img, mix_t, pre_down, act_t, patch_t, wq, wk, wv, wo, w_up, w_down,
     sems) = refs[blocks:]
    text_total = q_txt.shape[0]
    width = w_down.shape[1]
    cols = pl.ds(pl.multiple_of(place[0] * HD, HD), HD)
    moves = fetch(
        [(k_img_far, keys.at[text_total:, :]), (v_img_far, values.at[text_total:, :]), (qt_far, qt),
         (kt_far, kt.at[:, text_total:]), (q_img_far, q_img), (mix_t_far, mix_t),
         (pre_down_far, pre_down), (act_t_far, act_t), (patch_t_far, patch_t),
         (wq_far.at[:, cols], wq), (wk_far.at[:, cols], wk), (wv_far.at[:, cols], wv), (wo_far.at[cols, :], wo),
         (w_up_far, w_up), (w_down_far, w_down)],
        sems,
    )
    cross_sum[...] = jnp.zeros_like(cross_sum)
    small_sum[...] = jnp.zeros_like(small_sum)
    keys[:text_total, :] = k_txt[...]
    values[:text_total, :] = v_txt[...]
    kt[:, :text_total] = kt_txt[...]
    rows = text_total // blocks
    for k, back in enumerate(backs):
        d_txt[pl.ds(pl.multiple_of((place[5] ^ k) * rows, rows), rows), :] = back[:, :HD]
    d_txt_t = d_txt[...].astype(F32).T
    delta_txt = jnp.sum(d_txt_t * mix_txt_t[...].astype(F32), axis=0, keepdims=True)

    def score_grads(first, last, turned_query, turned_grad, logs, delta, seen):
        wide = turned_query.shape[1]
        scores[first:last, :wide] = dot(keys[first:last, :], turned_query)
        pulls[first:last, :wide] = dot(values[first:last, :], turned_grad)
        for at in strips(last)[first // STRIP :]:
            p = jnp.exp2(scores[at, :wide] - logs)
            mask = seen(at)
            if mask is not None:
                p = jnp.where(mask, p, 0.0)
            probs[at, :wide] = p.astype(BF16)
            slopes[at, :wide] = (p * (pulls[at, :wide] - delta)).astype(BF16)

    for move in moves[:2]:
        move.wait()
    lane = iota((1, text_total), 1)
    end = text_total + blocks * length
    score_grads(
        text_total, end, qt_txt[...], d_txt_t.astype(BF16), lse_txt[...], delta_txt,
        lambda at: lane >= thr[(at.start - text_total) // length],
    )
    dk[...] = dot(slopes[text_total:end, :text_total], q_txt[...])
    dv[...] = dot(probs[text_total:end, :text_total], d_txt[...])
    for move in moves[2:6]:
        move.wait()
    for i in range(blocks):
        grad = grad_pre[i]
        cross_sum[...] += dot(mix_t[i], grad)
        d_out = dot_nt(grad, u[...]).astype(BF16)
        d_t = dot_nt(u[...], grad).astype(BF16)
        delta = jnp.sum(d_t.astype(F32) * mix_t[i].astype(F32), axis=0, keepdims=True)
        count = (i + 1) * length
        end = text_total + count
        score_grads(
            0, end, qt[i], d_t, lse[i], delta,
            lambda at: iota((STRIP, length), 0) + at.start < thr[i] if at.start < text_total else None,
        )
        dv[:count, :] += dot(probs[text_total:end, :length], d_out)
        dk[:count, :] += dot(slopes[text_total:end, :length], q_img[i])
        dq[i] = dot(kt[:, :end], slopes[:end, :length]).T
    for move in moves[6:9]:
        move.wait()
    taps = patch_t.shape[1]

    def block(b, query):
        cos, sin = angles(*start_row(starts, thr, b, extra), steps)
        own_rows = pl.ds(pl.multiple_of(b * length, length), length)

        def back(values):
            return values * cos - pltpu.roll(values, HD // 2, 1) * sin

        before = pre_down[b]
        act = silu(before).astype(BF16)
        act_wide = act.astype(F32)
        image = dot(act, gram[...])
        square = jnp.sum(image * act_wide, axis=-1, keepdims=True)
        inv = lax.rsqrt(square * (1.0 / width) + EPSILON)
        heads = jnp.concatenate(
            [back(query) * (inv * SCALE), back(dk[own_rows, :]) * (inv * LN2), dv[own_rows, :] * inv], axis=1
        ).astype(BF16)
        lift = dot_nt(heads, proj[...])
        crow = inv * inv * (jnp.sum(act_wide * lift, axis=-1, keepdims=True) * (1.0 / width))
        grad = grad_pre[b]
        d_act = (lift - crow * image) * copies + dot_nt(grad, z[...]) * share
        slope = (d_act * silu_slope(before)).astype(BF16)
        flipped = act_t[b]
        return (
            dot(patch_t[b], slope),
            dot(flipped, heads),
            dot(flipped, (act_wide * crow).astype(BF16)),
            dot(flipped, grad),
        )

    def step(n, carry):
        for b in (n, blocks // 2 + n):
            conv, *more = block(b, dq[b])
            small_sum[:taps, :] += conv
            carry = tuple(a + m for a, m in zip(carry, more))
        return carry

    rank = act_t.shape[1]
    spread, pull, inner = lax.fori_loop(
        0, blocks // 2, step,
        (jnp.zeros((rank, 3 * HD), F32), jnp.zeros((rank, rank), F32), jnp.zeros((rank, grad_pre.shape[2]), F32)),
    )
    for move in moves[9:]:
        move.wait()
    spread = (spread * copies).astype(BF16)
    pull = (pull * copies).astype(BF16)
    cross = (cross_sum[...] * copies).T.astype(BF16)
    inner_t = (inner * share).T.astype(BF16)
    inner = (inner * share).astype(BF16)
    small_sum[taps : taps + grad_out_t.shape[0], :] = grad_out_t[...]
    _, groups, pairs, rows, _ = pieces.shape
    own = width // (2 * groups * pairs)
    few = rows - 2 * own
    for at in range(0, width, HD):
        cols = slice(at, at + HD)
        down = dot_nt(spread[:, :HD], wq[cols, :]) + dot_nt(spread[:, HD : 2 * HD], wk[cols, :])
        down = (down + dot_nt(spread[:, 2 * HD :], wv[cols, :])) * gain[at // HD : at // HD + 1, :].astype(F32)
        down = (down - dot(pull, w_down[:, cols]) + dot_nt(inner, w_up[cols, :])).astype(BF16)
        up = (dot(cross, wo[:, cols]) + dot(inner_t, w_down[:, cols])).T.astype(BF16)
        for part in range(0, HD, own):
            put_piece(place, pieces, (at + part) // own, slice(0, own), up[part : part + own])
            put_piece(place, pieces, (at + part) // own, slice(own, 2 * own), down[part : part + own])
    for number in range(2 * groups * pairs):
        put_piece(place, pieces, number, slice(2 * own, rows), small_sum[number * few : (number + 1) * few, :].astype(BF16))


def shards(
    text_tokens,
    latent,
    image_offset,
    norm_gain,
    w_query,
    w_key,
    w_value,
    w_out,
    w_down_conv,
    w_down_proj,
    w_up_proj,
    w_up_out,
    pred_grad,
    text_grad,
):
    axes = ("sy", "sx")
    text_local = text_tokens[0]
    text_rows, width = text_local.shape
    lat_chan = w_up_out.shape[1]
    up_chan = w_up_proj.shape[1]
    down_chan = w_down_conv.shape[1]
    taps = w_down_conv.shape[0]
    tile_rows = latent.shape[1]
    tile_cols = latent.shape[2] // lat_chan
    row_groups = lax.axis_size("sx")
    blocks = lax.axis_size("sy")
    devices = row_groups * blocks
    high = tile_rows * row_groups
    length = high * tile_cols
    text_block = text_rows * row_groups
    text_total = text_block * blocks
    total = length * blocks
    block_len = length + text_block
    heads_here = w_query.shape[1] // HD
    repeat = blocks // heads_here
    assert heads_here * repeat == blocks and blocks % 2 == 0
    own = lax.axis_index("sy")
    share = 1.0 / devices
    copies = 1.0 / repeat

    device = own * row_groups + lax.axis_index("sx").astype(jnp.int32)
    group = lax.axis_index("sx").astype(jnp.int32)
    own = own.astype(jnp.int32)
    head = jnp.stack([own // repeat, device, group, own // 2, own % 2, own])

    def spread_over(values, axis, count):
        return lax.all_to_all(jnp.broadcast_to(values[None], (count,) + values.shape), axis, 0, 0)

    tag = jnp.broadcast_to(image_offset.astype(BF16)[:, None], (tile_rows, HD))
    packed = jnp.concatenate([latent[0], tag], axis=1)
    hop = lambda values, axis, by: lax.ppermute(
        values, axis, [(i, i ^ by) for i in range(row_groups if axis == "sx" else blocks)]
    )
    pair = jnp.stack([text_local, hop(text_local, "sy", 1)])
    text_parts = [pair] + [hop(pair, "sx", k) for k in range(1, row_groups)]
    text_grad_parts = [text_grad[0]] + [hop(text_grad[0], "sx", k) for k in range(1, row_groups)]
    side = spread_over(packed, axes, devices)

    gain = norm_gain.reshape(width // HD, HD)
    small = jax.ShapeDtypeStruct
    square = small((down_chan, down_chan), BF16)
    pairs = blocks // 2
    vmem = pltpu.VMEM
    dma = lambda count: pltpu.SemaphoreType.DMA((count,))
    bf = lambda *shape: small(shape, BF16)
    proj, proj_t, mapped, u, gram, z, conv_t = call(
        weights_kernel, head,
        [(gain, None), (w_down_conv, None)]
        + [(a, pl.ANY) for a in (w_down_proj, w_query, w_key, w_value, w_up_proj, w_out)],
        [bf(down_chan, 3 * HD), bf(3 * HD, down_chan), bf(down_chan, 5 * HD), bf(HD, up_chan),
         bf(down_chan, down_chan), bf(down_chan, up_chan), bf(down_chan, taps)],
        [vmem((down_chan, width), BF16)] + [vmem((width, HD), BF16)] * 3
        + [vmem((width, up_chan), BF16), vmem((HD, width), BF16), dma(6)],
        flops=4_000_000_000,
    )
    both = 2 * text_block
    chunks = 8
    wide = heads_here * HD // 2
    text_here = call(
        lambda *refs: text_kernel(row_groups, repeat, *refs), head,
        [(gain, None)] + [(a, pl.ANY) for a in (w_query, w_key, w_value)] + [(a, None) for a in text_parts],
        [bf(both, 3 * HD)] * pairs,
        [vmem((chunks, 3, width // chunks, wide), BF16), vmem((both, width), BF16), vmem((3, both, wide), F32),
         dma(3 * chunks)],
        flops=6 * both * width * wide,
        after=[proj],
    )
    texts = [
        lax.ppermute(values, "sy", [(2 * z + c, c * pairs + (z ^ k)) for z in range(pairs) for c in range(2)])
        for k, values in enumerate(text_here)
    ]

    side = side.reshape(blocks, row_groups, tile_rows, -1)
    lat_t = side[..., : tile_cols * lat_chan].reshape(total, lat_chan).T.astype(F32)
    offsets = side[:, 0, 0, tile_cols * lat_chan].astype(jnp.int32)
    block_ids = jnp.arange(blocks, dtype=jnp.int32)
    thr = block_ids * text_block + offsets
    ids = np.arange(length, dtype=np.int32)
    cell = np.stack([ids // tile_cols, ids % tile_cols])
    at = np.arange(blocks)[:, None]
    steps = rope_tables(ids)
    steps_t = np.ascontiguousarray(np.swapaxes(steps, 1, 2)[:, HD // 2 :])
    starts = rope_tables((at * block_len + np.arange(text_block + 1)).reshape(-1))
    near = (at * block_len + np.arange(text_block)).reshape(-1)
    near, far = rope_tables(near), rope_tables(near + length)

    chunk = lambda kind, rows=length, cols=HD: small((blocks, rows, cols), kind)
    text_kind = small((text_total, HD), BF16)
    text_flip = small((HD, text_total), BF16)
    side_len = max(length, text_total)
    seq = text_total + total
    pre_down, act_t, patch_t, q_img, qt, k_img, kt, v_img, vt = image_rows(
        (high, tile_cols, width, 1), thr, lat_t, cell, conv_t, proj_t, mapped, gram, starts, steps, steps_t,
        [text_here[0], *text_grad_parts]
    )
    part, q_txt, qt_txt, k_txt, kt_txt, v_txt, mix_t, mix_txt_t, mix_txt, lse, lse_txt = call(
        attend_kernel, head,
        [(thr, pltpu.SMEM), (near, None), (far, None), (u, None), (qt, pl.ANY), (k_img.reshape(total, HD), pl.ANY),
         (vt, pl.ANY)]
        + [(a, None) for a in texts],
        [chunk(BF16, length, up_chan), text_kind, text_flip, text_kind, text_flip, text_kind, chunk(BF16, HD, length),
         text_flip, text_kind, small((blocks, 1, length), F32), small((1, text_total), F32)],
        [vmem((seq, side_len), F32), vmem((seq, side_len), BF16), vmem((text_total, 3 * HD), BF16),
         vmem(qt.shape, BF16), vmem((seq, HD), BF16), vmem((HD, seq), BF16), dma(3)],
        flops=6_000_000_000,
    )

    own_rows = tile_rows * tile_cols
    part = part if repeat == 1 else part * jnp.asarray(copies, BF16)
    parts = lax.all_to_all(part.reshape(devices, own_rows, up_chan), axes, 0, 0)
    wo_room = [vmem((4, heads_here * HD // 4, width), BF16)]
    text_back = call(
        lambda *refs: text_grad_kernel(row_groups, repeat, *refs), head,
        [(w_out, pl.ANY), (mix_txt, None)] + [(a, None) for a in text_grad_parts],
        [bf(text_block, 2 * HD)] * blocks,
        wo_room + [vmem((heads_here * HD, text_block), F32), dma(4)],
        flops=2 * text_block * width * heads_here * HD,
        after=[part],
    )
    text_back = [text_back[0]] + [hop(text_back[k], "sy", k) for k in range(1, blocks)]
    grad_copies, prediction, grad_out_t = call(
        up_kernel, head,
        [(parts, None), (pre_down.reshape(devices, own_rows, down_chan), None), (z, None), (w_up_out, None),
         (pred_grad[0].reshape(own_rows, lat_chan), None)],
        [small((devices, own_rows, up_chan), BF16), small((own_rows, lat_chan), BF16), small((lat_chan, up_chan), F32)],
        flops=2_000_000_000,
        after=text_back[:1],
        room=SMALL_BYTES,
    )
    grad_pre = lax.all_to_all(grad_copies, axes, 0, 0).reshape(blocks, length, up_chan)

    own_part = width // devices
    few = -(-(taps + lat_chan) // (16 * devices)) * 16
    lump = lambda rows: small((pairs, rows, HD), BF16)
    flat = lambda rows: small((rows, HD), BF16)
    vmem = pltpu.VMEM
    def core_sum(pieces, rows):
        return plain(add_core_kernel, [pieces, hop(pieces[1], "sy", 1)], [lump(rows)] * row_groups)

    def sx_sum(sums, rows, after=()):
        sums = [sums[0]] + [hop(sums[k], "sx", k) for k in range(1, row_groups)]
        return plain(lambda *refs: add_sx_kernel(row_groups, *refs), sums, [flat(rows)] * pairs, after)

    def z_sum(sums, rows, after=()):
        sums = [sums[0]] + [hop(sums[m], "sy", 2 * m) for m in range(1, pairs)]
        return plain(add_kernel, sums, [flat(rows)], after)[0]

    def spread_z(mine):
        return jnp.stack([mine] + [hop(mine, "sy", 2 * m) for m in range(1, pairs)])

    def spread_sx(mine):
        near = [mine] + [hop(mine, "sx", k) for k in range(1, row_groups)]
        return near + [hop(values, "sy", 1) for values in near]

    rows = 2 * own_part + few
    near_arrays = (k_img.reshape(total, HD), v_img.reshape(total, HD), qt, kt, q_img, mix_t, pre_down, act_t, patch_t)
    far_arrays = near_arrays + (w_query, w_key, w_value, w_out, w_up_proj, w_down_proj)
    pieces = call(
        lambda *refs: backward_kernel(share, copies, 1, *refs), head,
        [(thr, pltpu.SMEM)] + [(a, None) for a in (
            grad_pre, q_txt, qt_txt, k_txt, kt_txt, v_txt, mix_txt_t, lse, lse_txt,
            u, proj, gram, z, gain, starts, steps, grad_out_t, *text_back)]
        + [(a, pl.ANY) for a in far_arrays],
        [small((2, row_groups, pairs, rows, HD), BF16)],
        [vmem((blocks, length, HD), F32), vmem((total, HD), F32), vmem((total, HD), F32), vmem((text_total, HD), BF16),
         vmem((HD, up_chan), F32), vmem((devices * few, HD), F32)]
        + [vmem((seq, side_len), F32)] * 2 + [vmem((seq, side_len), BF16)] * 2
        + [vmem((seq, HD), BF16)] * 2 + [vmem(qt.shape, BF16), vmem((HD, seq), BF16)]
        + [vmem(a.shape, a.dtype) for a in near_arrays[4:]]
        + [vmem((width, HD), BF16)] * 3
        + [vmem((HD, width), BF16), vmem(w_up_proj.shape, BF16), vmem(w_down_proj.shape, BF16),
           pltpu.SemaphoreType.DMA((len(far_arrays),))],
        flops=30_000_000_000,
    )[0]
    pieces = core_sum(pieces, rows)
    mixed = call(
        lambda *refs: text_out_kernel(repeat, blocks, *refs), head,
        [(w_out, pl.ANY)] + [(a, None) for a in text_back],
        [bf(text_rows, width)] * row_groups,
        wo_room + [vmem((text_block, heads_here * HD), BF16), dma(4)],
        flops=2 * text_block * width * heads_here * HD,
        after=pieces[:1],
    )
    pieces = sx_sum(pieces, rows, mixed[:1])
    mixed = [mixed[0]] + [hop(mixed[k], "sx", k) for k in range(1, row_groups)]
    text_out = (text_local.astype(F32) + sum(m.astype(F32) for m in mixed)).astype(BF16)
    mine = spread_z(z_sum(pieces, rows))
    grad_conv, grad_down, grad_up, grad_out_t = call(
        lambda *refs: unpack_kernel(row_groups, pairs, own_part, *refs), head,
        [(a, None) for a in spread_sx(mine)],
        [small((taps, down_chan), F32), small((down_chan, width), F32), small((width, up_chan), F32),
         small((lat_chan, up_chan), F32)],
        [vmem((devices * few, HD), F32)],
        room=2 * SMALL_BYTES,
    )
    return (
        prediction.reshape(1, tile_rows, tile_cols * lat_chan),
        text_out[None],
        grad_conv,
        grad_down,
        grad_up,
        grad_out_t.T,
    )


def solution(mesh):
    placed = (
        P("sy", "sx", None),
        P("sy", "sx", None),
        P("sy"),
        P(),
        P(None, "sx"),
        P(None, "sx"),
        P(None, "sx"),
        P("sx", None),
        P(),
        P(),
        P(),
        P(),
        P("sy", "sx", None),
        P("sy", "sx", None),
    )
    return jax.shard_map(
        shards,
        mesh=mesh,
        in_specs=placed,
        out_specs=(P("sy", "sx", None), P("sy", "sx", None), P(), P(), P(), P()),
        check_vma=False,
    )
```

```python
import math

import jax
import jax.numpy as jnp
import numpy as np
from jax import lax
from jax.experimental import pallas as pl
from jax.experimental.pallas import tpu as pltpu
from jax.sharding import PartitionSpec as P

HD = 128
EPSILON = 1e-05
NEG_SCORE = -1e30
ROPE_BASE = 500000.0
SCALE = HD ** (-0.5)
LOG2E = math.log2(math.e)
LN2 = math.log(2.0)
F32 = jnp.float32
BF16 = jnp.bfloat16
MIB = 1024 * 1024
VMEM_BYTES = 56 * MIB
SMALL_BYTES = 16 * MIB


def dot(left, right):
    return jnp.dot(left, right, preferred_element_type=F32)


def dot_nt(left, right):
    return lax.dot_general(left, right, (((1,), (1,)), ((), ())), preferred_element_type=F32)


def silu_slope(values):
    sigma = jax.nn.sigmoid(values)
    return sigma * (1.0 + values * (1.0 - sigma))


def silu(values):
    return values * jax.nn.sigmoid(values)


def iota(shape, dim):
    return lax.broadcasted_iota(jnp.int32, shape, dim)


def flip(values):
    return values.astype(F32).T.astype(BF16)


def call(kernel, place, inputs, outs, scratch=(), flops=0, after=(), room=VMEM_BYTES):
    inputs = [(place, pltpu.SMEM)] + list(inputs)
    count = len(inputs)
    skip = count + len(after)
    moved = sum(math.prod(a.shape) * a.dtype.itemsize for a in list(outs) + [a for a, space in inputs if space is None])
    return pl.pallas_call(
        lambda *refs: kernel(*refs[:count], *refs[skip:]),
        out_shape=outs,
        in_specs=[pl.BlockSpec(memory_space=pltpu.VMEM if space is None else space) for _, space in inputs]
        + [pl.BlockSpec(memory_space=pl.ANY) for _ in after],
        out_specs=[pl.BlockSpec(memory_space=pltpu.VMEM) for _ in outs],
        scratch_shapes=list(scratch),
        compiler_params=pltpu.CompilerParams(vmem_limit_bytes=room),
        cost_estimate=pl.CostEstimate(flops=flops, bytes_accessed=moved, transcendentals=0),
    )(*[a for a, _ in inputs], *after)


def fetch(moves, sems):
    moves = [pltpu.make_async_copy(far, near, sems.at[n]) for n, (far, near) in enumerate(moves)]
    for move in moves:
        move.start()
    return moves


def whole_row(gain):
    return jnp.concatenate([gain[r : r + 1, :].astype(F32) for r in range(gain.shape[0])], axis=1)


def weights_kernel(
    place, gain, w_conv, w_down_far, wq_far, wk_far, wv_far, w_up_far, wo_far,
    proj, proj_t, mapped, u, gram, z, conv_t,
    w_down, wq, wk, wv, w_up, wo, sems,
):
    cols = pl.ds(pl.multiple_of(place[0] * HD, HD), HD)
    moves = fetch(
        [(w_down_far, w_down), (wq_far.at[:, cols], wq), (wk_far.at[:, cols], wk), (wv_far.at[:, cols], wv),
         (w_up_far, w_up), (wo_far.at[cols, :], wo)],
        sems,
    )
    conv_t[...] = flip(w_conv[...])
    moves[0].wait()
    down = w_down[...]
    scaled = (down.astype(F32) * whole_row(gain)).astype(BF16)
    gram[...] = dot_nt(down, down).astype(BF16)
    for n, w in enumerate((wq, wk, wv)):
        cols = slice(n * HD, (n + 1) * HD)
        moves[1 + n].wait()
        total = dot(scaled, w[...])
        proj[:, cols] = total.astype(BF16)
        proj_t[cols, :] = total.T.astype(BF16)
        mapped[:, cols] = total.astype(BF16)
        if n < 2:
            mapped[:, (3 + n) * HD : (4 + n) * HD] = pltpu.roll(total, HD // 2, 1).astype(BF16)
    moves[4].wait()
    z[...] = dot(down, w_up[...]).astype(BF16)
    moves[5].wait()
    u[...] = dot(wo[...], w_up[...]).astype(BF16)


def pick(rows, total, spot):
    return (iota((total, rows), 0) == iota((total, rows), 1) + spot).astype(BF16)


def gathered(parts, group):
    rows = parts[0].shape[0]
    total = rows * len(parts)
    return sum(dot(pick(rows, total, (group ^ k) * rows), part[...]) for k, part in enumerate(parts))


def text_kernel(count, repeat, place, *refs):
    gain, wq_far, wk_far, wv_far = refs[:4]
    parts = refs[4 : 4 + count]
    outs = refs[4 + count : -4]
    weights, normed, sums, sems = refs[-4:]
    chunks, _, deep, wide = weights.shape
    cols = pl.ds(pl.multiple_of(place[4] * wide, wide), wide)
    moves = fetch(
        [(far.at[c * deep : (c + 1) * deep, cols], weights.at[c, n])
         for c in range(chunks) for n, far in enumerate((wq_far, wk_far, wv_far))],
        sems,
    )
    rows = normed.shape[0] // 2
    row = whole_row(gain)
    for r in range(2):
        x = gathered([part.at[r] for part in parts], place[2])
        inverse = lax.rsqrt(jnp.mean(x * x, axis=-1, keepdims=True) + EPSILON)
        normed[r * rows : (r + 1) * rows, :] = (x * inverse * row).astype(BF16)
    for c in range(chunks):
        here = normed[:, c * deep : (c + 1) * deep]
        for n in range(3):
            moves[3 * c + n].wait()
            term = dot(here, weights[c, n])
            sums[n] = term if c == 0 else sums[n] + term
    for k, out in enumerate(outs):
        head = pl.ds(pl.multiple_of((place[3] ^ k) // repeat * HD, HD), HD)
        for n in range(3):
            out[:, n * HD : (n + 1) * HD] = sums[n, :, head].astype(BF16)


def text_grad_kernel(count, repeat, place, wo_far, mix, *refs):
    parts = refs[:count]
    outs = refs[count : -3]
    wo, total, sems = refs[-3:]
    groups, deep, _ = wo.shape
    moves = fetch([(wo_far.at[g * deep : (g + 1) * deep, :], wo.at[g]) for g in range(groups)], sems)
    grad_t = gathered(parts, place[2]).T.astype(BF16)
    for g in range(groups):
        moves[g].wait()
        total[g * deep : (g + 1) * deep, :] = dot(wo[g], grad_t)
    for k, out in enumerate(outs):
        peer = place[5] ^ k
        rows = out.shape[0]
        out[:, :HD] = total[pl.ds(pl.multiple_of(peer // repeat * HD, HD), HD), :].T.astype(BF16)
        out[:, HD:] = mix[pl.ds(pl.multiple_of(peer * rows, rows), rows), :]


def text_out_kernel(repeat, peers, place, wo_far, *refs):
    mixes = refs[:peers]
    outs = refs[peers:-3]
    wo, mixed, sems = refs[-3:]
    groups, deep, width = wo.shape
    moves = fetch([(wo_far.at[g * deep : (g + 1) * deep, :], wo.at[g]) for g in range(groups)], sems)
    for k, mix in enumerate(mixes):
        peer = place[5] ^ k

        @pl.when(peer % repeat == 0)
        def _():
            mixed[:, pl.ds(pl.multiple_of(peer // repeat * HD, HD), HD)] = mix[:, HD:]

    total = 0.0
    for g in range(groups):
        moves[g].wait()
        total = total + dot(mixed[:, g * deep : (g + 1) * deep], wo[g])
    whole = total.astype(BF16)
    for k, out in enumerate(outs):
        rows = out.shape[0]
        out[...] = dot(pick(rows, whole.shape[0], (place[2] ^ k) * rows).astype(F32).T.astype(BF16), whole).astype(BF16)


def turned(values, cos, sin):
    return values * cos + pltpu.roll(values, HD // 2, 1) * sin


def rope_tables(positions):
    half = HD // 2
    freq = np.exp(-(2.0 * np.arange(half) / HD) * math.log(ROPE_BASE)).astype(np.float32)
    angle = np.asarray(positions, np.float64)[:, None] * np.concatenate([freq, freq])[None].astype(np.float64)
    sign = np.where(np.arange(HD) < half, -1.0, 1.0)[None]
    return np.stack([np.cos(angle), np.sin(angle) * sign]).astype(np.float32)


def angles(cos_start, sin_start, steps):
    return cos_start * steps[0] - sin_start * steps[1], sin_start * steps[0] + cos_start * steps[1]


def start_row(starts, thr, b, extra):
    row = pl.ds(thr[b] + b * extra, 1)
    return starts[0, row, :], starts[1, row, :]


def image_kernel(high, wide, width, extra, thr, lat_all, cell, conv_t, proj_t, mapped, gram, starts, steps, steps_t, *refs):
    pre_down, act_t, patch_t, q_img, qt, k_img, kt, v_img, vt = refs[-9:]
    images, length, _ = pre_down.shape
    for n in range(images):
        number = pl.program_id(0) * images + n
        lanes = slice(n * length, (n + 1) * length)
        lat = lat_all[:, n * length : (n + 1) * length]
        chan = lat.shape[0]
        row = cell[0:1, :]
        col = cell[1:2, :]
        for r in range(3):
            for c in range(3):
                tap = r * 3 + c
                step = (r - 1) * wide + (c - 1)
                moved = pltpu.roll(lat, -step % lat.shape[1], 1) if step else lat
                keep = (row + (r - 1) >= 0) & (row + (r - 1) < high)
                keep &= (col + (c - 1) >= 0) & (col + (c - 1) < wide)
                patch_t[n, tap * chan : (tap + 1) * chan, :] = jnp.where(keep, moved, 0.0).astype(BF16)
        cos_start, sin_start = start_row(starts, thr, number, extra)
        before_t = dot(conv_t[...], patch_t[n])
        flat_t = silu(before_t).astype(BF16)
        act_t[n] = flat_t
        square = jnp.sum(dot(gram[...], flat_t) * flat_t.astype(F32), axis=0, keepdims=True)
        inv = lax.rsqrt(square * (1.0 / width) + EPSILON)
        heads_t = dot(proj_t[...], flat_t) * inv
        half = HD // 2
        column = lambda values: jnp.broadcast_to(values, (8, HD)).T[half:, :1]
        cos, sin = angles(column(cos_start), column(sin_start), steps_t)
        for at, out, scale in ((0, qt.at[n], SCALE * LOG2E), (HD, kt.at[:, lanes], 1.0)):
            first = heads_t[at : at + half]
            second = heads_t[at + half : at + HD]
            out[:half, :] = ((first * cos - second * sin) * scale).astype(BF16)
            out[half:, :] = ((second * cos + first * sin) * scale).astype(BF16)
        vt[:, lanes] = heads_t[2 * HD :].astype(BF16)
        before = before_t.T
        pre_down[n] = before
        act = silu(before).astype(BF16)
        square = jnp.sum(dot(act, gram[...]) * act.astype(F32), axis=-1, keepdims=True)
        inv = lax.rsqrt(square * (1.0 / width) + EPSILON)
        heads = dot(act, mapped[...])
        cos, sin = angles(cos_start, sin_start, steps)
        cos = cos * inv
        sin = sin * inv
        query = heads[:, :HD] * cos + heads[:, 3 * HD : 4 * HD] * sin
        q_img[n] = (query * (SCALE * LOG2E)).astype(BF16)
        k_img[n] = (heads[:, HD : 2 * HD] * cos + heads[:, 4 * HD :] * sin).astype(BF16)
        v_img[n] = (heads[:, 2 * HD : 3 * HD] * inv).astype(BF16)


def image_rows(sizes, thr, lat_t, cell, conv_t, proj_t, mapped, gram, starts, steps, steps_t, after):
    blocks = thr.shape[0]
    length = steps.shape[1]
    chan = lat_t.shape[0]
    down_chan, taps = conv_t.shape
    whole = lambda a: pl.BlockSpec(a.shape, lambda b: (0,) * len(a.shape))
    outs = [(length, down_chan, F32), (down_chan, length, BF16), (taps, length, BF16), (length, HD, BF16),
            (HD, length, BF16), (length, HD, BF16), None, (length, HD, BF16), None]
    per = 2
    flat = pl.BlockSpec((HD, per * length), lambda b: (0, b))
    return pl.pallas_call(
        lambda *refs: image_kernel(*sizes, *refs),
        out_shape=[jax.ShapeDtypeStruct((blocks, *o[:2]), o[2]) if o else jax.ShapeDtypeStruct((HD, blocks * length), BF16)
                   for o in outs],
        grid=(blocks // per,),
        in_specs=[pl.BlockSpec(memory_space=pltpu.SMEM), pl.BlockSpec((chan, per * length), lambda b: (0, b))]
        + [whole(a) for a in (cell, conv_t, proj_t, mapped, gram, starts, steps, steps_t)]
        + [pl.BlockSpec(memory_space=pl.ANY) for _ in after],
        out_specs=[pl.BlockSpec((per, *o[:2]), lambda b: (b, 0, 0)) if o else flat for o in outs],
        compiler_params=pltpu.CompilerParams(vmem_limit_bytes=VMEM_BYTES),
        cost_estimate=pl.CostEstimate(flops=8_000_000_000, bytes_accessed=8_000_000, transcendentals=0),
    )(thr, lat_t, cell, conv_t, proj_t, mapped, gram, starts, steps, steps_t, *after)


STRIP = 128


def strips(rows):
    return [slice(at, at + STRIP) for at in range(0, rows, STRIP)]


def attend_kernel(
    head, thr, near, far, u, qt_far, k_img_far, vt_far, *refs,
):
    texts = refs[:-18]
    (part, q_txt, qt_txt, k_txt, kt_txt, v_txt, mix_t, mix_txt_t, mix_txt, lse, lse_txt,
     scores, probs, text, qt, keys, vt, sems) = refs[-18:]
    blocks, length, _ = part.shape
    text_total = q_txt.shape[0]
    moves = fetch(
        [(k_img_far, keys.at[text_total:, :]), (qt_far, qt), (vt_far, vt.at[:HD, text_total:])], sems
    )
    row = iota((text_total, 1), 0)
    rows = text_total // blocks
    core = head[5] // len(texts)
    for k, values in enumerate(texts):
        pair = head[5] % len(texts) ^ k
        for r in range(2):
            spot = pl.ds(pl.multiple_of((2 * pair + (core ^ r)) * rows, rows), rows)
            text[spot, :] = values[r * rows : (r + 1) * rows, :]
    shifted = row >= sum(jnp.where(row // rows == b, thr[b], 0) for b in range(blocks))
    cos = jnp.where(shifted, far[0], near[0])
    sin = jnp.where(shifted, far[1], near[1])
    query = turned(text[:, :HD].astype(F32), cos, sin) * (SCALE * LOG2E)
    q_txt[...] = query.astype(BF16)
    qt_txt[...] = query.T.astype(BF16)
    key = turned(text[:, HD : 2 * HD].astype(F32), cos, sin)
    k_txt[...] = key.astype(BF16)
    keys[:text_total, :] = key.astype(BF16)
    kt_txt[...] = key.T.astype(BF16)
    v_txt[...] = text[:, 2 * HD :]
    vt[:HD, :text_total] = flip(text[:, 2 * HD :])
    vt[HD:, :] = jnp.ones((vt.shape[0] - HD, vt.shape[1]), BF16)
    for move in moves:
        move.wait()

    def softmax(turned_query, count, seen):
        wide = turned_query.shape[1]
        scores[:count, :wide] = dot(keys[:count, :], turned_query)
        fold = lambda values: values.reshape(STRIP // 8, 8, wide)
        top = None
        for at in strips(count):
            s = scores[at, :wide]
            mask = seen(at)
            if mask is not None:
                s = jnp.where(mask, s, NEG_SCORE)
                scores[at, :wide] = s
            peak = jnp.max(fold(s), axis=0)
            top = peak if top is None else jnp.maximum(top, peak)
        top = jnp.max(top, axis=0, keepdims=True)
        for at in strips(count):
            p = jnp.exp2(scores[at, :wide] - top)
            mask = seen(at)
            if mask is not None:
                p = jnp.where(mask, p, 0.0)
            probs[at, :wide] = p.astype(BF16)
        mixed = dot(vt[:, :count], probs[:count, :wide])
        whole = mixed[HD : HD + 1, :]
        return mixed[:HD] / whole, top + jnp.log2(whole)

    for i in range(blocks):
        mixed, logs = softmax(
            qt[i], text_total + (i + 1) * length,
            lambda at: iota((STRIP, length), 0) + at.start < thr[i] if at.start < text_total else None,
        )
        lse[i] = logs
        mix_t[i] = mixed.astype(BF16)
        part[i] = dot(mixed.T.astype(BF16), u[...]).astype(part.dtype)
    lane = iota((1, text_total), 1)
    mixed, logs = softmax(
        qt_txt[...], text_total + blocks * length,
        lambda at: iota((STRIP, text_total), 0) + at.start <= lane
        if at.start < text_total else lane >= thr[(at.start - text_total) // length],
    )
    lse_txt[...] = logs
    mix_txt_t[...] = mixed.astype(BF16)
    mix_txt[...] = mixed.T.astype(BF16)


def up_kernel(head, parts, pre_down, z, w_up_out, preds, grad_copies, prediction, grad_out_t):
    act = silu(pre_down[head[1]]).astype(BF16)
    pre_up = dot(act, z[...])
    for p in range(parts.shape[0]):
        pre_up = pre_up + parts[p].astype(F32)
    up_act = silu(pre_up).astype(BF16)
    grad = (dot_nt(preds[...], w_up_out[...]) * silu_slope(pre_up)).astype(BF16)
    for p in range(parts.shape[0]):
        grad_copies[p] = grad
    prediction[...] = dot(up_act, w_up_out[...]).astype(BF16)
    grad_out_t[...] = dot(flip(preds[...]), up_act)


def piece_spot(place, groups, pairs, number):
    group = number // (2 * pairs) ^ place[2]
    pair = number // 2 % pairs ^ place[3]
    return group, pair, number % 2 ^ place[4]


def put_piece(place, pieces, number, rows, values):
    _, groups, pairs, _, _ = pieces.shape
    group, pair, core = piece_spot(place, groups, pairs, number)
    pieces[core, group, pair, rows, :] = values


def add_core_kernel(keep, received, *outs):
    for k, out in enumerate(outs):
        out[...] = (keep[k].astype(F32) + received[k].astype(F32)).astype(BF16)


def add_sx_kernel(count, *refs):
    for m, out in enumerate(refs[count:]):
        out[...] = sum(r[m].astype(F32) for r in refs[:count]).astype(BF16)


def add_kernel(*refs):
    refs[-1][...] = sum(r[...].astype(F32) for r in refs[:-1]).astype(BF16)


def unpack_kernel(groups, pairs, own, place, *refs):
    count = 2 * groups
    grad_conv, grad_down, grad_up, grad_out_t, rest = refs[count:]
    few = refs[0].shape[1] - 2 * own
    per = HD // own
    for n, part in enumerate(refs[:count]):
        for m in range(pairs):
            number = ((place[2] ^ n % groups) * pairs + (place[3] ^ m)) * 2 + (place[4] ^ n // groups)
            grad_up[pl.ds(pl.multiple_of(number * own, own), own), :] = part[m, :own, :].astype(F32)
            cols = pl.ds(pl.multiple_of(number // per * HD, HD), HD)
            rows = pl.ds(pl.multiple_of(number % per * own, own), own)
            grad_down[rows, cols] = part[m, own : 2 * own, :].astype(F32)
            rest[pl.ds(pl.multiple_of(number * few, few), few), :] = part[m, 2 * own :, :].astype(F32)
    taps = grad_conv.shape[0]
    grad_conv[...] = rest[:taps, :]
    grad_out_t[...] = rest[taps : taps + grad_out_t.shape[0], :]


def plain(kernel, inputs, outs, after=()):
    whole = lambda a: pl.BlockSpec(a.shape, lambda: (0,) * len(a.shape))
    moved = sum(math.prod(a.shape) * a.dtype.itemsize for a in list(inputs) + list(outs))
    return pl.pallas_call(
        lambda *refs: kernel(*refs[: len(inputs)], *refs[len(inputs) + len(after) :]),
        out_shape=outs,
        in_specs=[whole(a) for a in inputs] + [pl.BlockSpec(memory_space=pl.ANY) for _ in after],
        out_specs=[whole(a) for a in outs],
        compiler_params=pltpu.CompilerParams(vmem_limit_bytes=SMALL_BYTES),
        cost_estimate=pl.CostEstimate(flops=0, bytes_accessed=moved, transcendentals=0),
    )(*inputs, *after)


def score_grads(keys, values, room, first, last, turned_query, turned_grad, logs, delta, seen):
    scores, pulls, probs, slopes = room
    wide = turned_query.shape[1]
    scores[first:last, :wide] = dot(keys[first:last, :], turned_query)
    pulls[first:last, :wide] = dot(values[first:last, :], turned_grad)
    for at in strips(last)[first // STRIP :]:
        p = jnp.exp2(scores[at, :wide] - logs)
        mask = seen(at)
        if mask is not None:
            p = jnp.where(mask, p, 0.0)
        probs[at, :wide] = p.astype(BF16)
        slopes[at, :wide] = (p * (pulls[at, :wide] - delta)).astype(BF16)


def text_backward_kernel(place, thr, k_img, v_img, q_txt, qt_txt, mix_txt_t, lse_txt, *refs):
    backs = refs[:-7]
    dk, dv, d_txt, *room = refs[-7:]
    text_total = q_txt.shape[0]
    total = k_img.shape[0]
    blocks = thr.shape[0]
    rows = text_total // blocks
    for k, back in enumerate(backs):
        d_txt[pl.ds(pl.multiple_of((place[5] ^ k) * rows, rows), rows), :] = back[:, :HD]
    d_txt_t = d_txt[...].astype(F32).T
    delta = jnp.sum(d_txt_t * mix_txt_t[...].astype(F32), axis=0, keepdims=True)
    lane = iota((1, text_total), 1)
    score_grads(
        k_img, v_img, room, 0, total, qt_txt[...], d_txt_t.astype(BF16), lse_txt[...], delta,
        lambda at: lane >= thr[at.start // (total // blocks)],
    )
    probs, slopes = room[2:]
    dk[...] = dot(slopes[...], q_txt[...])
    dv[...] = dot(probs[...], d_txt[...])


def backward_kernel(
    share, copies, extra, place, thr, grad_pre, k_txt, kt_txt, v_txt, lse, u, proj, gram, z, gain, starts, steps, grad_out_t, *refs,
):
    blocks, length, _ = grad_pre.shape
    (k_img_far, v_img_far, qt_far, kt_far, q_img_far, mix_t_far, dk_far, dv_far, pre_down_far, act_t_far, patch_t_far,
     wq_far, wk_far, wv_far, wo_far, w_up_far, w_down_far,
     keep, send,
     pieces, dq, dk, dv, cross_sum, small_sum, scores, pulls, probs, slopes,
     keys, values, qt, kt, q_img, mix_t, pre_down, act_t, patch_t, wq, wk, wv, wo, w_up, w_down,
     sems) = refs
    text_total = k_txt.shape[0]
    width = w_down.shape[1]
    cols = pl.ds(pl.multiple_of(place[0] * HD, HD), HD)
    moves = fetch(
        [(k_img_far, keys.at[text_total:, :]), (v_img_far, values.at[text_total:, :]), (qt_far, qt),
         (kt_far, kt.at[:, text_total:]), (q_img_far, q_img), (mix_t_far, mix_t), (dk_far, dk), (dv_far, dv),
         (pre_down_far, pre_down), (act_t_far, act_t), (patch_t_far, patch_t),
         (wq_far.at[:, cols], wq), (wk_far.at[:, cols], wk), (wv_far.at[:, cols], wv), (wo_far.at[cols, :], wo),
         (w_up_far, w_up), (w_down_far, w_down)],
        sems,
    )
    cross_sum[...] = jnp.zeros_like(cross_sum)
    small_sum[...] = jnp.zeros_like(small_sum)
    keys[:text_total, :] = k_txt[...]
    values[:text_total, :] = v_txt[...]
    kt[:, :text_total] = kt_txt[...]
    room = (scores, pulls, probs, slopes)
    for move in moves[:8]:
        move.wait()
    for i in range(blocks):
        grad = grad_pre[i]
        cross_sum[...] += dot(mix_t[i], grad)
        d_out = dot_nt(grad, u[...]).astype(BF16)
        d_t = dot_nt(u[...], grad).astype(BF16)
        delta = jnp.sum(d_t.astype(F32) * mix_t[i].astype(F32), axis=0, keepdims=True)
        count = (i + 1) * length
        end = text_total + count
        score_grads(
            keys, values, room, 0, end, qt[i], d_t, lse[i], delta,
            lambda at: iota((STRIP, length), 0) + at.start < thr[i] if at.start < text_total else None,
        )
        dv[:count, :] += dot(probs[text_total:end, :length], d_out)
        dk[:count, :] += dot(slopes[text_total:end, :length], q_img[i])
        dq[i] = dot(kt[:, :end], slopes[:end, :length]).T
    for move in moves[8:11]:
        move.wait()
    taps = patch_t.shape[1]

    def block(b, query):
        cos, sin = angles(*start_row(starts, thr, b, extra), steps)
        own_rows = pl.ds(pl.multiple_of(b * length, length), length)

        def back(values):
            return values * cos - pltpu.roll(values, HD // 2, 1) * sin

        before = pre_down[b]
        act = silu(before).astype(BF16)
        act_wide = act.astype(F32)
        image = dot(act, gram[...])
        square = jnp.sum(image * act_wide, axis=-1, keepdims=True)
        inv = lax.rsqrt(square * (1.0 / width) + EPSILON)
        heads = jnp.concatenate(
            [back(query) * (inv * SCALE), back(dk[own_rows, :]) * (inv * LN2), dv[own_rows, :] * inv], axis=1
        ).astype(BF16)
        lift = dot_nt(heads, proj[...])
        crow = inv * inv * (jnp.sum(act_wide * lift, axis=-1, keepdims=True) * (1.0 / width))
        grad = grad_pre[b]
        d_act = (lift - crow * image) * copies + dot_nt(grad, z[...]) * share
        slope = (d_act * silu_slope(before)).astype(BF16)
        flipped = act_t[b]
        return (
            dot(patch_t[b], slope),
            dot(flipped, heads),
            dot(flipped, (act_wide * crow).astype(BF16)),
            dot(flipped, grad),
        )

    def step(n, carry):
        for b in (n, blocks // 2 + n):
            conv, *more = block(b, dq[b])
            small_sum[:taps, :] += conv
            carry = tuple(a + m for a, m in zip(carry, more))
        return carry

    rank = act_t.shape[1]
    spread, pull, inner = lax.fori_loop(
        0, blocks // 2, step,
        (jnp.zeros((rank, 3 * HD), F32), jnp.zeros((rank, rank), F32), jnp.zeros((rank, grad_pre.shape[2]), F32)),
    )
    for move in moves[11:]:
        move.wait()
    spread = (spread * copies).astype(BF16)
    pull = (pull * copies).astype(BF16)
    cross = (cross_sum[...] * copies).T.astype(BF16)
    inner_t = (inner * share).T.astype(BF16)
    inner = (inner * share).astype(BF16)
    small_sum[taps : taps + grad_out_t.shape[0], :] = grad_out_t[...]
    _, groups, pairs, rows, _ = pieces.shape
    own = width // (2 * groups * pairs)
    few = rows - 2 * own
    for at in range(0, width, HD):
        cols = slice(at, at + HD)
        down = dot_nt(spread[:, :HD], wq[cols, :]) + dot_nt(spread[:, HD : 2 * HD], wk[cols, :])
        down = (down + dot_nt(spread[:, 2 * HD :], wv[cols, :])) * gain[at // HD : at // HD + 1, :].astype(F32)
        down = (down - dot(pull, w_down[:, cols]) + dot_nt(inner, w_up[cols, :])).astype(BF16)
        up = (dot(cross, wo[:, cols]) + dot(inner_t, w_down[:, cols])).T.astype(BF16)
        for part in range(0, HD, own):
            put_piece(place, pieces, (at + part) // own, slice(0, own), up[part : part + own])
            put_piece(place, pieces, (at + part) // own, slice(own, 2 * own), down[part : part + own])
    for number in range(2 * groups * pairs):
        put_piece(place, pieces, number, slice(2 * own, rows), small_sum[number * few : (number + 1) * few, :].astype(BF16))
    for move in fetch([(pieces.at[0], keep), (pieces.at[1], send)], sems):
        move.wait()


def shards(
    text_tokens,
    latent,
    image_offset,
    norm_gain,
    w_query,
    w_key,
    w_value,
    w_out,
    w_down_conv,
    w_down_proj,
    w_up_proj,
    w_up_out,
    pred_grad,
    text_grad,
):
    axes = ("sy", "sx")
    text_local = text_tokens[0]
    text_rows, width = text_local.shape
    lat_chan = w_up_out.shape[1]
    up_chan = w_up_proj.shape[1]
    down_chan = w_down_conv.shape[1]
    taps = w_down_conv.shape[0]
    tile_rows = latent.shape[1]
    tile_cols = latent.shape[2] // lat_chan
    row_groups = lax.axis_size("sx")
    blocks = lax.axis_size("sy")
    devices = row_groups * blocks
    high = tile_rows * row_groups
    length = high * tile_cols
    text_block = text_rows * row_groups
    text_total = text_block * blocks
    total = length * blocks
    block_len = length + text_block
    heads_here = w_query.shape[1] // HD
    repeat = blocks // heads_here
    assert heads_here * repeat == blocks and blocks % 2 == 0
    own = lax.axis_index("sy")
    share = 1.0 / devices
    copies = 1.0 / repeat

    device = own * row_groups + lax.axis_index("sx").astype(jnp.int32)
    group = lax.axis_index("sx").astype(jnp.int32)
    own = own.astype(jnp.int32)
    head = jnp.stack([own // repeat, device, group, own // 2, own % 2, own])

    def spread_over(values, axis, count):
        return lax.all_to_all(jnp.broadcast_to(values[None], (count,) + values.shape), axis, 0, 0)

    tag = jnp.broadcast_to(image_offset.astype(BF16)[:, None], (tile_rows, HD))
    packed = jnp.concatenate([latent[0], tag], axis=1)
    hop = lambda values, axis, by: lax.ppermute(
        values, axis, [(i, i ^ by) for i in range(row_groups if axis == "sx" else blocks)]
    )
    pair = jnp.stack([text_local, hop(text_local, "sy", 1)])
    text_parts = [pair] + [hop(pair, "sx", k) for k in range(1, row_groups)]
    text_grad_parts = [text_grad[0]] + [hop(text_grad[0], "sx", k) for k in range(1, row_groups)]
    side = spread_over(packed, axes, devices)

    gain = norm_gain.reshape(width // HD, HD)
    small = jax.ShapeDtypeStruct
    square = small((down_chan, down_chan), BF16)
    pairs = blocks // 2
    vmem = pltpu.VMEM
    dma = lambda count: pltpu.SemaphoreType.DMA((count,))
    bf = lambda *shape: small(shape, BF16)
    proj, proj_t, mapped, u, gram, z, conv_t = call(
        weights_kernel, head,
        [(gain, None), (w_down_conv, None)]
        + [(a, pl.ANY) for a in (w_down_proj, w_query, w_key, w_value, w_up_proj, w_out)],
        [bf(down_chan, 3 * HD), bf(3 * HD, down_chan), bf(down_chan, 5 * HD), bf(HD, up_chan),
         bf(down_chan, down_chan), bf(down_chan, up_chan), bf(down_chan, taps)],
        [vmem((down_chan, width), BF16)] + [vmem((width, HD), BF16)] * 3
        + [vmem((width, up_chan), BF16), vmem((HD, width), BF16), dma(6)],
        flops=4_000_000_000,
    )
    both = 2 * text_block
    chunks = 8
    wide = heads_here * HD // 2
    text_here = call(
        lambda *refs: text_kernel(row_groups, repeat, *refs), head,
        [(gain, None)] + [(a, pl.ANY) for a in (w_query, w_key, w_value)] + [(a, None) for a in text_parts],
        [bf(both, 3 * HD)] * pairs,
        [vmem((chunks, 3, width // chunks, wide), BF16), vmem((both, width), BF16), vmem((3, both, wide), F32),
         dma(3 * chunks)],
        flops=6 * both * width * wide,
        after=[proj],
    )
    texts = [
        lax.ppermute(values, "sy", [(2 * z + c, c * pairs + (z ^ k)) for z in range(pairs) for c in range(2)])
        for k, values in enumerate(text_here)
    ]

    side = side.reshape(blocks, row_groups, tile_rows, -1)
    lat_t = side[..., : tile_cols * lat_chan].reshape(total, lat_chan).T.astype(F32)
    offsets = side[:, 0, 0, tile_cols * lat_chan].astype(jnp.int32)
    block_ids = jnp.arange(blocks, dtype=jnp.int32)
    thr = block_ids * text_block + offsets
    ids = np.arange(length, dtype=np.int32)
    cell = np.stack([ids // tile_cols, ids % tile_cols])
    at = np.arange(blocks)[:, None]
    steps = rope_tables(ids)
    steps_t = np.ascontiguousarray(np.swapaxes(steps, 1, 2)[:, HD // 2 :])
    starts = rope_tables((at * block_len + np.arange(text_block + 1)).reshape(-1))
    near = (at * block_len + np.arange(text_block)).reshape(-1)
    near, far = rope_tables(near), rope_tables(near + length)

    chunk = lambda kind, rows=length, cols=HD: small((blocks, rows, cols), kind)
    text_kind = small((text_total, HD), BF16)
    text_flip = small((HD, text_total), BF16)
    side_len = max(length, text_total)
    seq = text_total + total
    pre_down, act_t, patch_t, q_img, qt, k_img, kt, v_img, vt = image_rows(
        (high, tile_cols, width, 1), thr, lat_t, cell, conv_t, proj_t, mapped, gram, starts, steps, steps_t,
        [text_here[0], *text_grad_parts]
    )
    part, q_txt, qt_txt, k_txt, kt_txt, v_txt, mix_t, mix_txt_t, mix_txt, lse, lse_txt = call(
        attend_kernel, head,
        [(thr, pltpu.SMEM), (near, None), (far, None), (u, None), (qt, pl.ANY), (k_img.reshape(total, HD), pl.ANY),
         (vt, pl.ANY)]
        + [(a, None) for a in texts],
        [chunk(BF16, length, up_chan), text_kind, text_flip, text_kind, text_flip, text_kind, chunk(BF16, HD, length),
         text_flip, text_kind, small((blocks, 1, length), F32), small((1, text_total), F32)],
        [vmem((seq, side_len), F32), vmem((seq, side_len), BF16), vmem((text_total, 3 * HD), BF16),
         vmem(qt.shape, BF16), vmem((seq, HD), BF16), vmem((HD + 16, seq), BF16), dma(3)],
        flops=6_000_000_000,
    )

    own_rows = tile_rows * tile_cols
    part = part if repeat == 1 else part * jnp.asarray(copies, BF16)
    parts = lax.all_to_all(part.reshape(devices, own_rows, up_chan), axes, 0, 0)
    wo_room = [vmem((4, heads_here * HD // 4, width), BF16)]
    text_back = call(
        lambda *refs: text_grad_kernel(row_groups, repeat, *refs), head,
        [(w_out, pl.ANY), (mix_txt, None)] + [(a, None) for a in text_grad_parts],
        [bf(text_block, 2 * HD)] * blocks,
        wo_room + [vmem((heads_here * HD, text_block), F32), dma(4)],
        flops=2 * text_block * width * heads_here * HD,
        after=[part],
    )
    text_back = [text_back[0]] + [hop(text_back[k], "sy", k) for k in range(1, blocks)]
    grad_copies, prediction, grad_out_t = call(
        up_kernel, head,
        [(parts, None), (pre_down.reshape(devices, own_rows, down_chan), None), (z, None), (w_up_out, None),
         (pred_grad[0].reshape(own_rows, lat_chan), None)],
        [small((devices, own_rows, up_chan), BF16), small((own_rows, lat_chan), BF16), small((lat_chan, up_chan), F32)],
        flops=2_000_000_000,
        after=text_back[1:],
        room=SMALL_BYTES,
    )
    grad_pre = lax.all_to_all(grad_copies, axes, 0, 0).reshape(blocks, length, up_chan)

    own_part = width // devices
    few = -(-(taps + lat_chan) // (16 * devices)) * 16
    lump = lambda rows: small((pairs, rows, HD), BF16)
    flat = lambda rows: small((rows, HD), BF16)
    vmem = pltpu.VMEM
    def core_sum(keep, send, rows):
        return plain(add_core_kernel, [keep, hop(send, "sy", 1)], [lump(rows)] * row_groups)

    def sx_sum(sums, rows, after=()):
        sums = [sums[0]] + [hop(sums[k], "sx", k) for k in range(1, row_groups)]
        return plain(lambda *refs: add_sx_kernel(row_groups, *refs), sums, [flat(rows)] * pairs, after)

    def z_sum(sums, rows, after=()):
        sums = [sums[0]] + [hop(sums[m], "sy", 2 * m) for m in range(1, pairs)]
        return plain(add_kernel, sums, [flat(rows)], after)[0]

    def spread_z(mine):
        return jnp.stack([mine] + [hop(mine, "sy", 2 * m) for m in range(1, pairs)])

    def spread_sx(mine):
        near = [mine] + [hop(mine, "sx", k) for k in range(1, row_groups)]
        return near + [hop(values, "sy", 1) for values in near]

    mixed = call(
        lambda *refs: text_out_kernel(repeat, blocks, *refs), head,
        [(w_out, pl.ANY)] + [(a, None) for a in text_back],
        [bf(text_rows, width)] * row_groups,
        wo_room + [vmem((text_block, heads_here * HD), BF16), dma(4)],
        flops=2 * text_block * width * heads_here * HD,
        after=[grad_copies],
    )
    mixed = [mixed[0]] + [hop(mixed[k], "sx", k) for k in range(1, row_groups)]
    text_out = (text_local.astype(F32) + sum(m.astype(F32) for m in mixed)).astype(BF16)
    k_rows, v_rows = k_img.reshape(total, HD), v_img.reshape(total, HD)
    strip_room = lambda rows: [vmem((rows, side_len), F32)] * 2 + [vmem((rows, side_len), BF16)] * 2
    dk, dv = call(
        text_backward_kernel, head,
        [(thr, pltpu.SMEM)] + [(a, None) for a in (k_rows, v_rows, q_txt, qt_txt, mix_txt_t, lse_txt, *text_back)],
        [small((total, HD), F32)] * 2,
        [vmem((text_total, HD), BF16)] + [vmem((total, text_total), kind) for kind in (F32, F32, BF16, BF16)],
        flops=2_000_000_000,
        after=mixed[:1] + [grad_copies],
    )
    rows = 2 * own_part + few
    near_arrays = (k_rows, v_rows, qt, kt, q_img, mix_t, dk, dv, pre_down, act_t, patch_t)
    far_arrays = near_arrays + (w_query, w_key, w_value, w_out, w_up_proj, w_down_proj)
    keep, send = call(
        lambda *refs: backward_kernel(share, copies, 1, *refs), head,
        [(thr, pltpu.SMEM)] + [(a, None) for a in (
            grad_pre, k_txt, kt_txt, v_txt, lse, u, proj, gram, z, gain, starts, steps, grad_out_t)]
        + [(a, pl.ANY) for a in far_arrays],
        [small((row_groups, pairs, rows, HD), BF16)] * 2,
        [vmem((2, row_groups, pairs, rows, HD), BF16), vmem((blocks, length, HD), F32), vmem((total, HD), F32),
         vmem((total, HD), F32), vmem((HD, up_chan), F32), vmem((devices * few, HD), F32)]
        + strip_room(seq)
        + [vmem((seq, HD), BF16)] * 2 + [vmem(qt.shape, BF16), vmem((HD, seq), BF16)]
        + [vmem(a.shape, a.dtype) for a in (q_img, mix_t, pre_down, act_t, patch_t)]
        + [vmem((width, HD), BF16)] * 3
        + [vmem((HD, width), BF16), vmem(w_up_proj.shape, BF16), vmem(w_down_proj.shape, BF16),
           pltpu.SemaphoreType.DMA((len(far_arrays),))],
        flops=30_000_000_000,
        after=mixed[1:],
    )
    mine = spread_z(z_sum(sx_sum(core_sum(keep, send, rows), rows), rows))
    grad_conv, grad_down, grad_up, grad_out_t = call(
        lambda *refs: unpack_kernel(row_groups, pairs, own_part, *refs), head,
        [(a, None) for a in spread_sx(mine)],
        [small((taps, down_chan), F32), small((down_chan, width), F32), small((width, up_chan), F32),
         small((lat_chan, up_chan), F32)],
        [vmem((devices * few, HD), F32)],
        room=2 * SMALL_BYTES,
    )
    return (
        prediction.reshape(1, tile_rows, tile_cols * lat_chan),
        text_out[None],
        grad_conv,
        grad_down,
        grad_up,
        grad_out_t.T,
    )


def solution(mesh):
    placed = (
        P("sy", "sx", None),
        P("sy", "sx", None),
        P("sy"),
        P(),
        P(None, "sx"),
        P(None, "sx"),
        P(None, "sx"),
        P("sx", None),
        P(),
        P(),
        P(),
        P(),
        P("sy", "sx", None),
        P("sy", "sx", None),
    )
    return jax.shard_map(
        shards,
        mesh=mesh,
        in_specs=placed,
        out_specs=(P("sy", "sx", None), P("sy", "sx", None), P(), P(), P(), P()),
        check_vma=False,
    )
```

```python
import math

import jax
import jax.numpy as jnp
import numpy as np
from jax import lax
from jax.experimental import pallas as pl
from jax.experimental.pallas import tpu as pltpu
from jax.sharding import PartitionSpec as P

HD = 128
EPSILON = 1e-05
NEG_SCORE = -1e30
ROPE_BASE = 500000.0
SCALE = HD ** (-0.5)
LOG2E = math.log2(math.e)
LN2 = math.log(2.0)
F32 = jnp.float32
BF16 = jnp.bfloat16
MIB = 1024 * 1024
VMEM_BYTES = 56 * MIB
SMALL_BYTES = 16 * MIB


def dot(left, right):
    return jnp.dot(left, right, preferred_element_type=F32)


def dot_nt(left, right):
    return lax.dot_general(left, right, (((1,), (1,)), ((), ())), preferred_element_type=F32)


def silu_slope(values):
    sigma = jax.nn.sigmoid(values)
    return sigma * (1.0 + values * (1.0 - sigma))


def silu(values):
    return values * jax.nn.sigmoid(values)


def iota(shape, dim):
    return lax.broadcasted_iota(jnp.int32, shape, dim)


def flip(values):
    return values.astype(F32).T.astype(BF16)


def call(kernel, place, inputs, outs, scratch=(), flops=0, after=(), room=VMEM_BYTES):
    inputs = [(place, pltpu.SMEM)] + list(inputs)
    count = len(inputs)
    skip = count + len(after)
    moved = sum(math.prod(a.shape) * a.dtype.itemsize for a in list(outs) + [a for a, space in inputs if space is None])
    return pl.pallas_call(
        lambda *refs: kernel(*refs[:count], *refs[skip:]),
        out_shape=outs,
        in_specs=[pl.BlockSpec(memory_space=pltpu.VMEM if space is None else space) for _, space in inputs]
        + [pl.BlockSpec(memory_space=pl.ANY) for _ in after],
        out_specs=[pl.BlockSpec(memory_space=pltpu.VMEM) for _ in outs],
        scratch_shapes=list(scratch),
        compiler_params=pltpu.CompilerParams(vmem_limit_bytes=room),
        cost_estimate=pl.CostEstimate(flops=flops, bytes_accessed=moved, transcendentals=0),
    )(*[a for a, _ in inputs], *after)


def fetch(moves, sems):
    moves = [pltpu.make_async_copy(far, near, sems.at[n]) for n, (far, near) in enumerate(moves)]
    for move in moves:
        move.start()
    return moves


def whole_row(gain):
    return jnp.concatenate([gain[r : r + 1, :].astype(F32) for r in range(gain.shape[0])], axis=1)


def weights_kernel(
    place, gain, w_conv, w_down_far, wq_far, wk_far, wv_far, w_up_far, wo_far,
    proj, proj_t, mapped, u, gram, z, conv_t,
    w_down, wq, wk, wv, w_up, wo, sems,
):
    cols = pl.ds(pl.multiple_of(place[0] * HD, HD), HD)
    moves = fetch(
        [(w_down_far, w_down), (wq_far.at[:, cols], wq), (wk_far.at[:, cols], wk), (wv_far.at[:, cols], wv),
         (w_up_far, w_up), (wo_far.at[cols, :], wo)],
        sems,
    )
    conv_t[...] = flip(w_conv[...])
    moves[0].wait()
    down = w_down[...]
    scaled = (down.astype(F32) * whole_row(gain)).astype(BF16)
    gram[...] = dot_nt(down, down).astype(BF16)
    for n, w in enumerate((wq, wk, wv)):
        cols = slice(n * HD, (n + 1) * HD)
        moves[1 + n].wait()
        total = dot(scaled, w[...])
        proj[:, cols] = total.astype(BF16)
        proj_t[cols, :] = total.T.astype(BF16)
        mapped[:, cols] = total.astype(BF16)
        if n < 2:
            mapped[:, (3 + n) * HD : (4 + n) * HD] = pltpu.roll(total, HD // 2, 1).astype(BF16)
    moves[4].wait()
    z[...] = dot(down, w_up[...]).astype(BF16)
    moves[5].wait()
    u[...] = dot(wo[...], w_up[...]).astype(BF16)


def pick(rows, total, spot):
    return (iota((total, rows), 0) == iota((total, rows), 1) + spot).astype(BF16)


def gathered(parts, group):
    rows = parts[0].shape[0]
    total = rows * len(parts)
    return sum(dot(pick(rows, total, (group ^ k) * rows), part[...]) for k, part in enumerate(parts))


def text_kernel(count, repeat, place, *refs):
    gain, wq_far, wk_far, wv_far = refs[:4]
    parts = refs[4 : 4 + count]
    outs = refs[4 + count : -4]
    weights, normed, sums, sems = refs[-4:]
    chunks, _, deep, wide = weights.shape
    cols = pl.ds(pl.multiple_of(place[4] * wide, wide), wide)
    moves = fetch(
        [(far.at[c * deep : (c + 1) * deep, cols], weights.at[c, n])
         for c in range(chunks) for n, far in enumerate((wq_far, wk_far, wv_far))],
        sems,
    )
    rows = normed.shape[0] // 2
    row = whole_row(gain)
    for r in range(2):
        x = gathered([part.at[r] for part in parts], place[2])
        inverse = lax.rsqrt(jnp.mean(x * x, axis=-1, keepdims=True) + EPSILON)
        normed[r * rows : (r + 1) * rows, :] = (x * inverse * row).astype(BF16)
    for c in range(chunks):
        here = normed[:, c * deep : (c + 1) * deep]
        for n in range(3):
            moves[3 * c + n].wait()
            term = dot(here, weights[c, n])
            sums[n] = term if c == 0 else sums[n] + term
    for k, out in enumerate(outs):
        head = pl.ds(pl.multiple_of((place[3] ^ k) // repeat * HD, HD), HD)
        for n in range(3):
            out[:, n * HD : (n + 1) * HD] = sums[n, :, head].astype(BF16)


def text_grad_kernel(count, repeat, place, wo_far, mix, *refs):
    parts = refs[:count]
    outs = refs[count : -3]
    wo, total, sems = refs[-3:]
    groups, deep, _ = wo.shape
    moves = fetch([(wo_far.at[g * deep : (g + 1) * deep, :], wo.at[g]) for g in range(groups)], sems)
    grad_t = gathered([part.at[2] for part in parts], place[2]).T.astype(BF16)
    for g in range(groups):
        moves[g].wait()
        total[g * deep : (g + 1) * deep, :] = dot(wo[g], grad_t)
    for k, out in enumerate(outs):
        peer = place[5] ^ k
        rows = out.shape[0]
        out[:, :HD] = total[pl.ds(pl.multiple_of(peer // repeat * HD, HD), HD), :].T.astype(BF16)
        out[:, HD:] = mix[pl.ds(pl.multiple_of(peer * rows, rows), rows), :]


def text_out_kernel(repeat, peers, place, wo_far, *refs):
    mixes = refs[:peers]
    outs = refs[peers:-3]
    wo, mixed, sems = refs[-3:]
    groups, deep, width = wo.shape
    moves = fetch([(wo_far.at[g * deep : (g + 1) * deep, :], wo.at[g]) for g in range(groups)], sems)
    for k, mix in enumerate(mixes):
        peer = place[5] ^ k

        @pl.when(peer % repeat == 0)
        def _():
            mixed[:, pl.ds(pl.multiple_of(peer // repeat * HD, HD), HD)] = mix[:, HD:]

    total = 0.0
    for g in range(groups):
        moves[g].wait()
        total = total + dot(mixed[:, g * deep : (g + 1) * deep], wo[g])
    whole = total.astype(BF16)
    for k, out in enumerate(outs):
        rows = out.shape[0]
        out[...] = dot(pick(rows, whole.shape[0], (place[2] ^ k) * rows).astype(F32).T.astype(BF16), whole).astype(BF16)


def turned(values, cos, sin):
    return values * cos + pltpu.roll(values, HD // 2, 1) * sin


def rope_tables(positions):
    half = HD // 2
    freq = np.exp(-(2.0 * np.arange(half) / HD) * math.log(ROPE_BASE)).astype(np.float32)
    angle = np.asarray(positions, np.float64)[:, None] * np.concatenate([freq, freq])[None].astype(np.float64)
    sign = np.where(np.arange(HD) < half, -1.0, 1.0)[None]
    return np.stack([np.cos(angle), np.sin(angle) * sign]).astype(np.float32)


def angles(cos_start, sin_start, steps):
    return cos_start * steps[0] - sin_start * steps[1], sin_start * steps[0] + cos_start * steps[1]


def start_row(starts, thr, b, extra):
    row = pl.ds(thr[b] + b * extra, 1)
    return starts[0, row, :], starts[1, row, :]


def image_kernel(high, wide, width, extra, thr, lat_all, cell, conv_t, proj_t, mapped, gram, starts, steps, steps_t, *refs):
    pre_down, act_t, patch_t, q_img, qt, k_img, kt, v_img, vt = refs[-9:]
    images, length, _ = pre_down.shape
    for n in range(images):
        number = pl.program_id(0) * images + n
        lanes = slice(n * length, (n + 1) * length)
        lat = lat_all[:, n * length : (n + 1) * length]
        chan = lat.shape[0]
        row = cell[0:1, :]
        col = cell[1:2, :]
        for r in range(3):
            for c in range(3):
                tap = r * 3 + c
                step = (r - 1) * wide + (c - 1)
                moved = pltpu.roll(lat, -step % lat.shape[1], 1) if step else lat
                keep = (row + (r - 1) >= 0) & (row + (r - 1) < high)
                keep &= (col + (c - 1) >= 0) & (col + (c - 1) < wide)
                patch_t[n, tap * chan : (tap + 1) * chan, :] = jnp.where(keep, moved, 0.0).astype(BF16)
        cos_start, sin_start = start_row(starts, thr, number, extra)
        before_t = dot(conv_t[...], patch_t[n])
        flat_t = silu(before_t).astype(BF16)
        act_t[n] = flat_t
        square = jnp.sum(dot(gram[...], flat_t) * flat_t.astype(F32), axis=0, keepdims=True)
        inv = lax.rsqrt(square * (1.0 / width) + EPSILON)
        heads_t = dot(proj_t[...], flat_t) * inv
        half = HD // 2
        column = lambda values: jnp.broadcast_to(values, (8, HD)).T[half:, :1]
        cos, sin = angles(column(cos_start), column(sin_start), steps_t)
        for at, out, scale in ((0, qt.at[n], SCALE * LOG2E), (HD, kt.at[:, lanes], 1.0)):
            first = heads_t[at : at + half]
            second = heads_t[at + half : at + HD]
            out[:half, :] = ((first * cos - second * sin) * scale).astype(BF16)
            out[half:, :] = ((second * cos + first * sin) * scale).astype(BF16)
        vt[:, lanes] = heads_t[2 * HD :].astype(BF16)
        before = before_t.T
        pre_down[n] = before
        act = silu(before).astype(BF16)
        square = jnp.sum(dot(act, gram[...]) * act.astype(F32), axis=-1, keepdims=True)
        inv = lax.rsqrt(square * (1.0 / width) + EPSILON)
        heads = dot(act, mapped[...])
        cos, sin = angles(cos_start, sin_start, steps)
        cos = cos * inv
        sin = sin * inv
        query = heads[:, :HD] * cos + heads[:, 3 * HD : 4 * HD] * sin
        q_img[n] = (query * (SCALE * LOG2E)).astype(BF16)
        k_img[n] = (heads[:, HD : 2 * HD] * cos + heads[:, 4 * HD :] * sin).astype(BF16)
        v_img[n] = (heads[:, 2 * HD : 3 * HD] * inv).astype(BF16)


def image_rows(sizes, thr, lat_t, cell, conv_t, proj_t, mapped, gram, starts, steps, steps_t, after):
    blocks = thr.shape[0]
    length = steps.shape[1]
    chan = lat_t.shape[0]
    down_chan, taps = conv_t.shape
    whole = lambda a: pl.BlockSpec(a.shape, lambda b: (0,) * len(a.shape))
    outs = [(length, down_chan, F32), (down_chan, length, BF16), (taps, length, BF16), (length, HD, BF16),
            (HD, length, BF16), (length, HD, BF16), None, (length, HD, BF16), None]
    per = 2
    flat = pl.BlockSpec((HD, per * length), lambda b: (0, b))
    return pl.pallas_call(
        lambda *refs: image_kernel(*sizes, *refs),
        out_shape=[jax.ShapeDtypeStruct((blocks, *o[:2]), o[2]) if o else jax.ShapeDtypeStruct((HD, blocks * length), BF16)
                   for o in outs],
        grid=(blocks // per,),
        in_specs=[pl.BlockSpec(memory_space=pltpu.SMEM), pl.BlockSpec((chan, per * length), lambda b: (0, b))]
        + [whole(a) for a in (cell, conv_t, proj_t, mapped, gram, starts, steps, steps_t)]
        + [pl.BlockSpec(memory_space=pl.ANY) for _ in after],
        out_specs=[pl.BlockSpec((per, *o[:2]), lambda b: (b, 0, 0)) if o else flat for o in outs],
        compiler_params=pltpu.CompilerParams(vmem_limit_bytes=VMEM_BYTES),
        cost_estimate=pl.CostEstimate(flops=8_000_000_000, bytes_accessed=8_000_000, transcendentals=0),
    )(thr, lat_t, cell, conv_t, proj_t, mapped, gram, starts, steps, steps_t, *after)


STRIP = 128


def strips(rows):
    return [slice(at, at + STRIP) for at in range(0, rows, STRIP)]


def attend_kernel(
    head, thr, near, far, u, qt_far, k_img_far, vt_far, *refs,
):
    texts = refs[:-18]
    (part, q_txt, qt_txt, k_txt, kt_txt, v_txt, mix_t, mix_txt_t, mix_txt, lse, lse_txt,
     scores, probs, text, qt, keys, vt, sems) = refs[-18:]
    blocks, length, _ = part.shape
    text_total = q_txt.shape[0]
    moves = fetch(
        [(k_img_far, keys.at[text_total:, :]), (qt_far, qt), (vt_far, vt.at[:HD, text_total:])], sems
    )
    row = iota((text_total, 1), 0)
    rows = text_total // blocks
    core = head[5] // len(texts)
    for k, values in enumerate(texts):
        pair = head[5] % len(texts) ^ k
        for r in range(2):
            spot = pl.ds(pl.multiple_of((2 * pair + (core ^ r)) * rows, rows), rows)
            text[spot, :] = values[r * rows : (r + 1) * rows, :]
    shifted = row >= sum(jnp.where(row // rows == b, thr[b], 0) for b in range(blocks))
    cos = jnp.where(shifted, far[0], near[0])
    sin = jnp.where(shifted, far[1], near[1])
    query = turned(text[:, :HD].astype(F32), cos, sin) * (SCALE * LOG2E)
    q_txt[...] = query.astype(BF16)
    qt_txt[...] = query.T.astype(BF16)
    key = turned(text[:, HD : 2 * HD].astype(F32), cos, sin)
    k_txt[...] = key.astype(BF16)
    keys[:text_total, :] = key.astype(BF16)
    kt_txt[...] = key.T.astype(BF16)
    v_txt[...] = text[:, 2 * HD :]
    vt[:HD, :text_total] = flip(text[:, 2 * HD :])
    vt[HD:, :] = jnp.ones((vt.shape[0] - HD, vt.shape[1]), BF16)
    for move in moves:
        move.wait()

    def begin(n):
        turned_query, count, _ = jobs[n]
        scores[n % 2, :count, : turned_query.shape[1]] = dot(keys[:count, :], turned_query)

    def softmax(n):
        turned_query, count, seen = jobs[n]
        wide = turned_query.shape[1]
        here = scores.at[n % 2]
        weights = probs.at[n % 2]
        fold = lambda values: values.reshape(STRIP // 8, 8, wide)
        top = None
        for at in strips(count):
            s = here[at, :wide]
            mask = seen(at)
            if mask is not None:
                s = jnp.where(mask, s, NEG_SCORE)
                here[at, :wide] = s
            peak = jnp.max(fold(s), axis=0)
            top = peak if top is None else jnp.maximum(top, peak)
        top = jnp.max(top, axis=0, keepdims=True)
        for at in strips(count):
            p = jnp.exp2(here[at, :wide] - top)
            mask = seen(at)
            if mask is not None:
                p = jnp.where(mask, p, 0.0)
            weights[at, :wide] = p.astype(BF16)
        mixed = dot(vt[:, :count], weights[:count, :wide])
        whole = mixed[HD : HD + 1, :]
        return mixed[:HD] / whole, top + jnp.log2(whole)

    def image_seen(i):
        return lambda at: iota((STRIP, length), 0) + at.start < thr[i] if at.start < text_total else None

    lane = iota((1, text_total), 1)
    jobs = [(qt[i], text_total + (i + 1) * length, image_seen(i)) for i in range(blocks)]
    jobs.append((
        qt_txt[...], text_total + blocks * length,
        lambda at: iota((STRIP, text_total), 0) + at.start <= lane
        if at.start < text_total else lane >= thr[(at.start - text_total) // length],
    ))
    begin(0)
    for i in range(blocks):
        begin(i + 1)
        mixed, logs = softmax(i)
        lse[i] = logs
        mix_t[i] = mixed.astype(BF16)
        part[i] = dot(mixed.T.astype(BF16), u[...]).astype(part.dtype)
    mixed, logs = softmax(blocks)
    lse_txt[...] = logs
    mix_txt_t[...] = mixed.astype(BF16)
    mix_txt[...] = mixed.T.astype(BF16)


def up_kernel(head, parts, pre_down, z, w_up_out, preds, grad_copies, prediction, grad_out_t):
    act = silu(pre_down[head[1]]).astype(BF16)
    pre_up = dot(act, z[...])
    for p in range(parts.shape[0]):
        pre_up = pre_up + parts[p].astype(F32)
    up_act = silu(pre_up).astype(BF16)
    grad = (dot_nt(preds[...], w_up_out[...]) * silu_slope(pre_up)).astype(BF16)
    for p in range(parts.shape[0]):
        grad_copies[p] = grad
    prediction[...] = dot(up_act, w_up_out[...]).astype(BF16)
    grad_out_t[...] = dot(flip(preds[...]), up_act)


def piece_spot(place, groups, pairs, number):
    group = number // (2 * pairs) ^ place[2]
    pair = number // 2 % pairs ^ place[3]
    return group, pair, number % 2 ^ place[4]


def put_piece(place, pieces, number, rows, values):
    _, groups, pairs, _, _ = pieces.shape
    group, pair, core = piece_spot(place, groups, pairs, number)
    pieces[core, group, pair, rows, :] = values


def add_core_kernel(keep, received, *outs):
    for k, out in enumerate(outs):
        out[...] = (keep[k].astype(F32) + received[k].astype(F32)).astype(BF16)


def add_sx_kernel(count, *refs):
    for m, out in enumerate(refs[count:]):
        out[...] = sum(r[m].astype(F32) for r in refs[:count]).astype(BF16)


def add_kernel(*refs):
    refs[-1][...] = sum(r[...].astype(F32) for r in refs[:-1]).astype(BF16)


def unpack_kernel(groups, pairs, own, place, *refs):
    count = 2 * groups
    grad_conv, grad_down, grad_up, grad_out_t, rest = refs[count:]
    few = refs[0].shape[1] - 2 * own
    per = HD // own
    for n, part in enumerate(refs[:count]):
        for m in range(pairs):
            number = ((place[2] ^ n % groups) * pairs + (place[3] ^ m)) * 2 + (place[4] ^ n // groups)
            grad_up[pl.ds(pl.multiple_of(number * own, own), own), :] = part[m, :own, :].astype(F32)
            cols = pl.ds(pl.multiple_of(number // per * HD, HD), HD)
            rows = pl.ds(pl.multiple_of(number % per * own, own), own)
            grad_down[rows, cols] = part[m, own : 2 * own, :].astype(F32)
            rest[pl.ds(pl.multiple_of(number * few, few), few), :] = part[m, 2 * own :, :].astype(F32)
    taps = grad_conv.shape[0]
    grad_conv[...] = rest[:taps, :]
    grad_out_t[...] = rest[taps : taps + grad_out_t.shape[0], :]


def plain(kernel, inputs, outs, after=()):
    whole = lambda a: pl.BlockSpec(a.shape, lambda: (0,) * len(a.shape))
    moved = sum(math.prod(a.shape) * a.dtype.itemsize for a in list(inputs) + list(outs))
    return pl.pallas_call(
        lambda *refs: kernel(*refs[: len(inputs)], *refs[len(inputs) + len(after) :]),
        out_shape=outs,
        in_specs=[whole(a) for a in inputs] + [pl.BlockSpec(memory_space=pl.ANY) for _ in after],
        out_specs=[whole(a) for a in outs],
        compiler_params=pltpu.CompilerParams(vmem_limit_bytes=SMALL_BYTES),
        cost_estimate=pl.CostEstimate(flops=0, bytes_accessed=moved, transcendentals=0),
    )(*inputs, *after)


def score_products(keys, values, room, first, last, turned_query, turned_grad):
    scores, pulls = room[:2]
    wide = turned_query.shape[1]
    scores[first:last, :wide] = dot(keys[first:last, :], turned_query)
    pulls[first:last, :wide] = dot(values[first:last, :], turned_grad)


def score_grads(room, first, last, logs, delta, seen):
    scores, pulls, probs, slopes = room
    wide = logs.shape[1]
    for at in strips(last)[first // STRIP :]:
        p = jnp.exp2(scores[at, :wide] - logs)
        mask = seen(at)
        if mask is not None:
            p = jnp.where(mask, p, 0.0)
        probs[at, :wide] = p.astype(BF16)
        slopes[at, :wide] = (p * (pulls[at, :wide] - delta)).astype(BF16)


def text_backward_kernel(place, thr, k_img, v_img, q_txt, qt_txt, mix_txt_t, lse_txt, *refs):
    backs = refs[:-7]
    dk, dv, d_txt, *room = refs[-7:]
    text_total = q_txt.shape[0]
    total = k_img.shape[0]
    blocks = thr.shape[0]
    rows = text_total // blocks
    for k, back in enumerate(backs):
        d_txt[pl.ds(pl.multiple_of((place[5] ^ k) * rows, rows), rows), :] = back[:, :HD]
    d_txt_t = d_txt[...].astype(F32).T
    delta = jnp.sum(d_txt_t * mix_txt_t[...].astype(F32), axis=0, keepdims=True)
    lane = iota((1, text_total), 1)
    score_products(k_img, v_img, room, 0, total, qt_txt[...], d_txt_t.astype(BF16))
    score_grads(
        room, 0, total, lse_txt[...], delta,
        lambda at: lane >= thr[at.start // (total // blocks)],
    )
    probs, slopes = room[2:]
    dk[...] = dot(slopes[...], q_txt[...])
    dv[...] = dot(probs[...], d_txt[...])


def backward_kernel(
    share, copies, extra, place, thr, grad_pre, k_txt, kt_txt, v_txt, lse, u, proj, gram, z, gain, starts, steps, grad_out_t, *refs,
):
    blocks, length, _ = grad_pre.shape
    (k_img_far, v_img_far, qt_far, kt_far, q_img_far, mix_t_far, dk_far, dv_far, pre_down_far, act_t_far, patch_t_far,
     wq_far, wk_far, wv_far, wo_far, w_up_far, w_down_far,
     keep, send,
     pieces, dq, dk, dv, cross_sum, small_sum, scores, pulls, probs, slopes,
     keys, values, qt, kt, q_img, mix_t, dk_text, dv_text, pre_down, act_t, patch_t, wq, wk, wv, wo, w_up, w_down,
     sems) = refs
    text_total = k_txt.shape[0]
    width = w_down.shape[1]
    cols = pl.ds(pl.multiple_of(place[0] * HD, HD), HD)
    moves = fetch(
        [(k_img_far, keys.at[text_total:, :]), (v_img_far, values.at[text_total:, :]), (qt_far, qt),
         (kt_far, kt.at[:, text_total:]), (q_img_far, q_img), (mix_t_far, mix_t), (dk_far, dk_text), (dv_far, dv_text),
         (pre_down_far, pre_down), (act_t_far, act_t), (patch_t_far, patch_t),
         (wq_far.at[:, cols], wq), (wk_far.at[:, cols], wk), (wv_far.at[:, cols], wv), (wo_far.at[cols, :], wo),
         (w_up_far, w_up), (w_down_far, w_down)],
        sems,
    )
    cross_sum[...] = jnp.zeros_like(cross_sum)
    small_sum[...] = jnp.zeros_like(small_sum)
    keys[:text_total, :] = k_txt[...]
    values[:text_total, :] = v_txt[...]
    kt[:, :text_total] = kt_txt[...]
    for move in moves[:6]:
        move.wait()

    def begin(i):
        grad = grad_pre[i]
        cross_sum[...] += dot(mix_t[i], grad)
        d_t = dot_nt(u[...], grad).astype(BF16)
        delta = jnp.sum(d_t.astype(F32) * mix_t[i].astype(F32), axis=0, keepdims=True)
        room = [ref.at[i % 2] for ref in (scores, pulls, probs, slopes)]
        score_products(keys, values, room, 0, text_total + (i + 1) * length, qt[i], d_t)
        return room, delta, dot_nt(grad, u[...]).astype(BF16)

    def add(total, before, values):
        if before:
            total[:before, :] += values[:before]
        total[before : before + length, :] = values[before:]

    ahead = begin(0)
    for i in range(blocks):
        room, delta, d_out = ahead
        if i + 1 < blocks:
            ahead = begin(i + 1)
        before = i * length
        end = text_total + before + length
        score_grads(
            room, 0, end, lse[i], delta,
            lambda at: iota((STRIP, length), 0) + at.start < thr[i] if at.start < text_total else None,
        )
        add(dv, before, dot(room[2][text_total:end, :length], d_out))
        add(dk, before, dot(room[3][text_total:end, :length], q_img[i]))
        dq[i] = dot(kt[:, :end], room[3][:end, :length]).T
    for move in moves[6:11]:
        move.wait()
    taps = patch_t.shape[1]

    def block(b, query):
        cos, sin = angles(*start_row(starts, thr, b, extra), steps)
        own_rows = pl.ds(pl.multiple_of(b * length, length), length)

        def back(values):
            return values * cos - pltpu.roll(values, HD // 2, 1) * sin

        before = pre_down[b]
        act = silu(before).astype(BF16)
        act_wide = act.astype(F32)
        image = dot(act, gram[...])
        square = jnp.sum(image * act_wide, axis=-1, keepdims=True)
        inv = lax.rsqrt(square * (1.0 / width) + EPSILON)
        heads = jnp.concatenate(
            [back(query) * (inv * SCALE), back(dk[own_rows, :] + dk_text[own_rows, :]) * (inv * LN2),
             (dv[own_rows, :] + dv_text[own_rows, :]) * inv], axis=1
        ).astype(BF16)
        lift = dot_nt(heads, proj[...])
        crow = inv * inv * (jnp.sum(act_wide * lift, axis=-1, keepdims=True) * (1.0 / width))
        grad = grad_pre[b]
        d_act = (lift - crow * image) * copies + dot_nt(grad, z[...]) * share
        slope = (d_act * silu_slope(before)).astype(BF16)
        flipped = act_t[b]
        return (
            dot(patch_t[b], slope),
            dot(flipped, heads),
            dot(flipped, (act_wide * crow).astype(BF16)),
            dot(flipped, grad),
        )

    def step(n, carry):
        for b in (n, blocks // 2 + n):
            conv, *more = block(b, dq[b])
            small_sum[:taps, :] += conv
            carry = tuple(a + m for a, m in zip(carry, more))
        return carry

    rank = act_t.shape[1]
    spread, pull, inner = lax.fori_loop(
        0, blocks // 2, step,
        (jnp.zeros((rank, 3 * HD), F32), jnp.zeros((rank, rank), F32), jnp.zeros((rank, grad_pre.shape[2]), F32)),
    )
    for move in moves[11:]:
        move.wait()
    spread = (spread * copies).astype(BF16)
    pull = (pull * copies).astype(BF16)
    cross = (cross_sum[...] * copies).T.astype(BF16)
    inner_t = (inner * share).T.astype(BF16)
    inner = (inner * share).astype(BF16)
    small_sum[taps : taps + grad_out_t.shape[0], :] = grad_out_t[...]
    _, groups, pairs, rows, _ = pieces.shape
    own = width // (2 * groups * pairs)
    few = rows - 2 * own
    for at in range(0, width, HD):
        cols = slice(at, at + HD)
        down = dot_nt(spread[:, :HD], wq[cols, :]) + dot_nt(spread[:, HD : 2 * HD], wk[cols, :])
        down = (down + dot_nt(spread[:, 2 * HD :], wv[cols, :])) * gain[at // HD : at // HD + 1, :].astype(F32)
        down = (down - dot(pull, w_down[:, cols]) + dot_nt(inner, w_up[cols, :])).astype(BF16)
        up = (dot(cross, wo[:, cols]) + dot(inner_t, w_down[:, cols])).T.astype(BF16)
        for part in range(0, HD, own):
            put_piece(place, pieces, (at + part) // own, slice(0, own), up[part : part + own])
            put_piece(place, pieces, (at + part) // own, slice(own, 2 * own), down[part : part + own])
    for number in range(2 * groups * pairs):
        put_piece(place, pieces, number, slice(2 * own, rows), small_sum[number * few : (number + 1) * few, :].astype(BF16))
    for move in fetch([(pieces.at[0], keep), (pieces.at[1], send)], sems):
        move.wait()


def shards(
    text_tokens,
    latent,
    image_offset,
    norm_gain,
    w_query,
    w_key,
    w_value,
    w_out,
    w_down_conv,
    w_down_proj,
    w_up_proj,
    w_up_out,
    pred_grad,
    text_grad,
):
    axes = ("sy", "sx")
    text_local = text_tokens[0]
    text_rows, width = text_local.shape
    lat_chan = w_up_out.shape[1]
    up_chan = w_up_proj.shape[1]
    down_chan = w_down_conv.shape[1]
    taps = w_down_conv.shape[0]
    tile_rows = latent.shape[1]
    tile_cols = latent.shape[2] // lat_chan
    row_groups = lax.axis_size("sx")
    blocks = lax.axis_size("sy")
    devices = row_groups * blocks
    high = tile_rows * row_groups
    length = high * tile_cols
    text_block = text_rows * row_groups
    text_total = text_block * blocks
    total = length * blocks
    block_len = length + text_block
    heads_here = w_query.shape[1] // HD
    repeat = blocks // heads_here
    assert heads_here * repeat == blocks and blocks % 2 == 0
    own = lax.axis_index("sy")
    share = 1.0 / devices
    copies = 1.0 / repeat

    device = own * row_groups + lax.axis_index("sx").astype(jnp.int32)
    group = lax.axis_index("sx").astype(jnp.int32)
    own = own.astype(jnp.int32)
    head = jnp.stack([own // repeat, device, group, own // 2, own % 2, own])

    def spread_over(values, axis, count):
        return lax.all_to_all(jnp.broadcast_to(values[None], (count,) + values.shape), axis, 0, 0)

    tag = jnp.broadcast_to(image_offset.astype(BF16)[:, None], (tile_rows, HD))
    packed = jnp.concatenate([latent[0], tag], axis=1)
    hop = lambda values, axis, by: lax.ppermute(
        values, axis, [(i, i ^ by) for i in range(row_groups if axis == "sx" else blocks)]
    )
    trio = jnp.stack([text_local, hop(text_local, "sy", 1), text_grad[0]])
    text_parts = [trio] + [hop(trio, "sx", k) for k in range(1, row_groups)]
    side = spread_over(packed, axes, devices)

    gain = norm_gain.reshape(width // HD, HD)
    small = jax.ShapeDtypeStruct
    square = small((down_chan, down_chan), BF16)
    pairs = blocks // 2
    vmem = pltpu.VMEM
    dma = lambda count: pltpu.SemaphoreType.DMA((count,))
    bf = lambda *shape: small(shape, BF16)
    proj, proj_t, mapped, u, gram, z, conv_t = call(
        weights_kernel, head,
        [(gain, None), (w_down_conv, None)]
        + [(a, pl.ANY) for a in (w_down_proj, w_query, w_key, w_value, w_up_proj, w_out)],
        [bf(down_chan, 3 * HD), bf(3 * HD, down_chan), bf(down_chan, 5 * HD), bf(HD, up_chan),
         bf(down_chan, down_chan), bf(down_chan, up_chan), bf(down_chan, taps)],
        [vmem((down_chan, width), BF16)] + [vmem((width, HD), BF16)] * 3
        + [vmem((width, up_chan), BF16), vmem((HD, width), BF16), dma(6)],
        flops=4_000_000_000,
    )
    both = 2 * text_block
    chunks = 8
    wide = heads_here * HD // 2
    text_here = call(
        lambda *refs: text_kernel(row_groups, repeat, *refs), head,
        [(gain, None)] + [(a, pl.ANY) for a in (w_query, w_key, w_value)] + [(a, None) for a in text_parts],
        [bf(both, 3 * HD)] * pairs,
        [vmem((chunks, 3, width // chunks, wide), BF16), vmem((both, width), BF16), vmem((3, both, wide), F32),
         dma(3 * chunks)],
        flops=6 * both * width * wide,
        after=[proj],
    )
    texts = [
        lax.ppermute(values, "sy", [(2 * z + c, c * pairs + (z ^ k)) for z in range(pairs) for c in range(2)])
        for k, values in enumerate(text_here)
    ]

    side = side.reshape(blocks, row_groups, tile_rows, -1)
    lat_t = side[..., : tile_cols * lat_chan].reshape(total, lat_chan).T.astype(F32)
    offsets = side[:, 0, 0, tile_cols * lat_chan].astype(jnp.int32)
    block_ids = jnp.arange(blocks, dtype=jnp.int32)
    thr = block_ids * text_block + offsets
    ids = np.arange(length, dtype=np.int32)
    cell = np.stack([ids // tile_cols, ids % tile_cols])
    at = np.arange(blocks)[:, None]
    steps = rope_tables(ids)
    steps_t = np.ascontiguousarray(np.swapaxes(steps, 1, 2)[:, HD // 2 :])
    starts = rope_tables((at * block_len + np.arange(text_block + 1)).reshape(-1))
    near = (at * block_len + np.arange(text_block)).reshape(-1)
    near, far = rope_tables(near), rope_tables(near + length)

    chunk = lambda kind, rows=length, cols=HD: small((blocks, rows, cols), kind)
    text_kind = small((text_total, HD), BF16)
    text_flip = small((HD, text_total), BF16)
    side_len = max(length, text_total)
    seq = text_total + total
    pre_down, act_t, patch_t, q_img, qt, k_img, kt, v_img, vt = image_rows(
        (high, tile_cols, width, 1), thr, lat_t, cell, conv_t, proj_t, mapped, gram, starts, steps, steps_t,
        text_here[:1]
    )
    part, q_txt, qt_txt, k_txt, kt_txt, v_txt, mix_t, mix_txt_t, mix_txt, lse, lse_txt = call(
        attend_kernel, head,
        [(thr, pltpu.SMEM), (near, None), (far, None), (u, None), (qt, pl.ANY), (k_img.reshape(total, HD), pl.ANY),
         (vt, pl.ANY)]
        + [(a, None) for a in texts],
        [chunk(BF16, length, up_chan), text_kind, text_flip, text_kind, text_flip, text_kind, chunk(BF16, HD, length),
         text_flip, text_kind, small((blocks, 1, length), F32), small((1, text_total), F32)],
        [vmem((2, seq, side_len), F32), vmem((2, seq, side_len), BF16), vmem((text_total, 3 * HD), BF16),
         vmem(qt.shape, BF16), vmem((seq, HD), BF16), vmem((HD + 16, seq), BF16), dma(3)],
        flops=6_000_000_000,
    )

    own_rows = tile_rows * tile_cols
    part = part if repeat == 1 else part * jnp.asarray(copies, BF16)
    parts = lax.all_to_all(part.reshape(devices, own_rows, up_chan), axes, 0, 0)
    wo_room = [vmem((4, heads_here * HD // 4, width), BF16)]
    text_back = call(
        lambda *refs: text_grad_kernel(row_groups, repeat, *refs), head,
        [(w_out, pl.ANY), (mix_txt, None)] + [(a, None) for a in text_parts],
        [bf(text_block, 2 * HD)] * blocks,
        wo_room + [vmem((heads_here * HD, text_block), F32), dma(4)],
        flops=2 * text_block * width * heads_here * HD,
        after=[part],
    )
    text_back = [text_back[0]] + [hop(text_back[k], "sy", k) for k in range(1, blocks)]
    grad_copies, prediction, grad_out_t = call(
        up_kernel, head,
        [(parts, None), (pre_down.reshape(devices, own_rows, down_chan), None), (z, None), (w_up_out, None),
         (pred_grad[0].reshape(own_rows, lat_chan), None)],
        [small((devices, own_rows, up_chan), BF16), small((own_rows, lat_chan), BF16), small((lat_chan, up_chan), F32)],
        flops=2_000_000_000,
        after=text_back[1:],
        room=SMALL_BYTES,
    )
    grad_pre = lax.all_to_all(grad_copies, axes, 0, 0).reshape(blocks, length, up_chan)

    own_part = width // devices
    few = -(-(taps + lat_chan) // (16 * devices)) * 16
    lump = lambda rows: small((pairs, rows, HD), BF16)
    flat = lambda rows: small((rows, HD), BF16)
    vmem = pltpu.VMEM
    def core_sum(keep, send, rows):
        return plain(add_core_kernel, [keep, hop(send, "sy", 1)], [lump(rows)] * row_groups)

    def sx_sum(sums, rows, after=()):
        sums = [sums[0]] + [hop(sums[k], "sx", k) for k in range(1, row_groups)]
        return plain(lambda *refs: add_sx_kernel(row_groups, *refs), sums, [flat(rows)] * pairs, after)

    def z_sum(sums, rows, after=()):
        sums = [sums[0]] + [hop(sums[m], "sy", 2 * m) for m in range(1, pairs)]
        return plain(add_kernel, sums, [flat(rows)], after)[0]

    def spread_z(mine):
        return jnp.stack([mine] + [hop(mine, "sy", 2 * m) for m in range(1, pairs)])

    def spread_sx(mine):
        near = [mine] + [hop(mine, "sx", k) for k in range(1, row_groups)]
        return near + [hop(values, "sy", 1) for values in near]

    mixed = call(
        lambda *refs: text_out_kernel(repeat, blocks, *refs), head,
        [(w_out, pl.ANY)] + [(a, None) for a in text_back],
        [bf(text_rows, width)] * row_groups,
        wo_room + [vmem((text_block, heads_here * HD), BF16), dma(4)],
        flops=2 * text_block * width * heads_here * HD,
        after=[grad_copies],
    )
    mixed = [mixed[0]] + [hop(mixed[k], "sx", k) for k in range(1, row_groups)]
    text_out = (text_local.astype(F32) + sum(m.astype(F32) for m in mixed)).astype(BF16)
    k_rows, v_rows = k_img.reshape(total, HD), v_img.reshape(total, HD)
    strip_room = lambda *lead: [vmem((*lead, side_len), F32)] * 2 + [vmem((*lead, side_len), BF16)] * 2
    dk, dv = call(
        text_backward_kernel, head,
        [(thr, pltpu.SMEM)] + [(a, None) for a in (k_rows, v_rows, q_txt, qt_txt, mix_txt_t, lse_txt, *text_back)],
        [small((total, HD), F32)] * 2,
        [vmem((text_total, HD), BF16)] + [vmem((total, text_total), kind) for kind in (F32, F32, BF16, BF16)],
        flops=2_000_000_000,
        after=mixed[:1] + [grad_copies],
    )
    rows = 2 * own_part + few
    near_arrays = (k_rows, v_rows, qt, kt, q_img, mix_t, dk, dv, pre_down, act_t, patch_t)
    far_arrays = near_arrays + (w_query, w_key, w_value, w_out, w_up_proj, w_down_proj)
    keep, send = call(
        lambda *refs: backward_kernel(share, copies, 1, *refs), head,
        [(thr, pltpu.SMEM)] + [(a, None) for a in (
            grad_pre, k_txt, kt_txt, v_txt, lse, u, proj, gram, z, gain, starts, steps, grad_out_t)]
        + [(a, pl.ANY) for a in far_arrays],
        [small((row_groups, pairs, rows, HD), BF16)] * 2,
        [vmem((2, row_groups, pairs, rows, HD), BF16), vmem((blocks, length, HD), F32), vmem((total, HD), F32),
         vmem((total, HD), F32), vmem((HD, up_chan), F32), vmem((devices * few, HD), F32)]
        + strip_room(2, seq)
        + [vmem((seq, HD), BF16)] * 2 + [vmem(qt.shape, BF16), vmem((HD, seq), BF16)]
        + [vmem(a.shape, a.dtype) for a in (q_img, mix_t, dk, dv, pre_down, act_t, patch_t)]
        + [vmem((width, HD), BF16)] * 3
        + [vmem((HD, width), BF16), vmem(w_up_proj.shape, BF16), vmem(w_down_proj.shape, BF16),
           pltpu.SemaphoreType.DMA((len(far_arrays),))],
        flops=30_000_000_000,
        after=mixed[1:],
    )
    mine = spread_z(z_sum(sx_sum(core_sum(keep, send, rows), rows), rows))
    grad_conv, grad_down, grad_up, grad_out_t = call(
        lambda *refs: unpack_kernel(row_groups, pairs, own_part, *refs), head,
        [(a, None) for a in spread_sx(mine)],
        [small((taps, down_chan), F32), small((down_chan, width), F32), small((width, up_chan), F32),
         small((lat_chan, up_chan), F32)],
        [vmem((devices * few, HD), F32)],
        room=2 * SMALL_BYTES,
    )
    return (
        prediction.reshape(1, tile_rows, tile_cols * lat_chan),
        text_out[None],
        grad_conv,
        grad_down,
        grad_up,
        grad_out_t.T,
    )


def solution(mesh):
    placed = (
        P("sy", "sx", None),
        P("sy", "sx", None),
        P("sy"),
        P(),
        P(None, "sx"),
        P(None, "sx"),
        P(None, "sx"),
        P("sx", None),
        P(),
        P(),
        P(),
        P(),
        P("sy", "sx", None),
        P("sy", "sx", None),
    )
    return jax.shard_map(
        shards,
        mesh=mesh,
        in_specs=placed,
        out_specs=(P("sy", "sx", None), P("sy", "sx", None), P(), P(), P(), P()),
        check_vma=False,
    )
```

```python
import math

import jax
import jax.numpy as jnp
import numpy as np
from jax import lax
from jax.experimental import pallas as pl
from jax.experimental.pallas import tpu as pltpu
from jax.sharding import PartitionSpec as P

HD = 128
EPSILON = 1e-05
NEG_SCORE = -1e30
ROPE_BASE = 500000.0
SCALE = HD ** (-0.5)
LOG2E = math.log2(math.e)
LN2 = math.log(2.0)
F32 = jnp.float32
BF16 = jnp.bfloat16
MIB = 1024 * 1024
VMEM_BYTES = 56 * MIB
SMALL_BYTES = 16 * MIB


def dot(left, right):
    return jnp.dot(left, right, preferred_element_type=F32)


def dot_nt(left, right):
    return lax.dot_general(left, right, (((1,), (1,)), ((), ())), preferred_element_type=F32)


def silu_slope(values):
    sigma = jax.nn.sigmoid(values)
    return sigma * (1.0 + values * (1.0 - sigma))


def silu(values):
    return values * jax.nn.sigmoid(values)


def iota(shape, dim):
    return lax.broadcasted_iota(jnp.int32, shape, dim)


def flip(values):
    return values.astype(F32).T.astype(BF16)


def call(kernel, place, inputs, outs, scratch=(), flops=0, after=(), room=VMEM_BYTES):
    inputs = [(place, pltpu.SMEM)] + list(inputs)
    count = len(inputs)
    skip = count + len(after)
    moved = sum(math.prod(a.shape) * a.dtype.itemsize for a in list(outs) + [a for a, space in inputs if space is None])
    return pl.pallas_call(
        lambda *refs: kernel(*refs[:count], *refs[skip:]),
        out_shape=outs,
        in_specs=[pl.BlockSpec(memory_space=pltpu.VMEM if space is None else space) for _, space in inputs]
        + [pl.BlockSpec(memory_space=pl.ANY) for _ in after],
        out_specs=[pl.BlockSpec(memory_space=pltpu.VMEM) for _ in outs],
        scratch_shapes=list(scratch),
        compiler_params=pltpu.CompilerParams(vmem_limit_bytes=room),
        cost_estimate=pl.CostEstimate(flops=flops, bytes_accessed=moved, transcendentals=0),
    )(*[a for a, _ in inputs], *after)


def fetch(moves, sems):
    moves = [pltpu.make_async_copy(far, near, sems.at[n]) for n, (far, near) in enumerate(moves)]
    for move in moves:
        move.start()
    return moves


def whole_row(gain):
    return jnp.concatenate([gain[r : r + 1, :].astype(F32) for r in range(gain.shape[0])], axis=1)


def pick(rows, total, spot):
    return (iota((total, rows), 0) == iota((total, rows), 1) + spot).astype(BF16)


def gathered(parts, group):
    rows = parts[0].shape[0]
    total = rows * len(parts)
    return sum(dot(pick(rows, total, (group ^ k) * rows), part[...]) for k, part in enumerate(parts))


def front_kernel(count, repeat, place, gain, w_conv, w_down_far, wq_far, wk_far, wv_far, w_up_far, wo_far, *refs):
    parts = refs[:count]
    proj, proj_t, mapped, u, gram, z, conv_t = refs[count : count + 7]
    outs = refs[count + 7 : -10]
    w_down, wq, wk, wv, w_up, wo, weights, normed, sums, sems = refs[-10:]
    chunks, _, deep, wide = weights.shape
    cols = pl.ds(pl.multiple_of(place[0] * HD, HD), HD)
    half = pl.ds(pl.multiple_of(place[4] * wide, wide), wide)
    moves = fetch(
        [(w_down_far, w_down), (wq_far.at[:, cols], wq), (wk_far.at[:, cols], wk), (wv_far.at[:, cols], wv),
         (w_up_far, w_up), (wo_far.at[cols, :], wo)]
        + [(far.at[c * deep : (c + 1) * deep, half], weights.at[c, n])
           for c in range(chunks) for n, far in enumerate((wq_far, wk_far, wv_far))],
        sems,
    )
    conv_t[...] = flip(w_conv[...])
    rows = normed.shape[0] // 2
    row = whole_row(gain)
    for r in range(2):
        x = gathered([part.at[r] for part in parts], place[2])
        inverse = lax.rsqrt(jnp.mean(x * x, axis=-1, keepdims=True) + EPSILON)
        normed[r * rows : (r + 1) * rows, :] = (x * inverse * row).astype(BF16)
    moves[0].wait()
    down = w_down[...]
    scaled = (down.astype(F32) * row).astype(BF16)
    gram[...] = dot_nt(down, down).astype(BF16)
    for n, w in enumerate((wq, wk, wv)):
        cols = slice(n * HD, (n + 1) * HD)
        moves[1 + n].wait()
        total = dot(scaled, w[...])
        proj[:, cols] = total.astype(BF16)
        proj_t[cols, :] = total.T.astype(BF16)
        mapped[:, cols] = total.astype(BF16)
        if n < 2:
            mapped[:, (3 + n) * HD : (4 + n) * HD] = pltpu.roll(total, HD // 2, 1).astype(BF16)
    moves[4].wait()
    z[...] = dot(down, w_up[...]).astype(BF16)
    moves[5].wait()
    u[...] = dot(wo[...], w_up[...]).astype(BF16)
    for c in range(chunks):
        here = normed[:, c * deep : (c + 1) * deep]
        for n in range(3):
            moves[6 + 3 * c + n].wait()
            term = dot(here, weights[c, n])
            sums[n] = term if c == 0 else sums[n] + term
    for k, out in enumerate(outs):
        head = pl.ds(pl.multiple_of((place[3] ^ k) // repeat * HD, HD), HD)
        for n in range(3):
            out[:, n * HD : (n + 1) * HD] = sums[n, :, head].astype(BF16)


def text_grad_kernel(count, repeat, place, wo_far, mix, *refs):
    parts = refs[:count]
    outs = refs[count : -3]
    wo, total, sems = refs[-3:]
    groups, deep, _ = wo.shape
    moves = fetch([(wo_far.at[g * deep : (g + 1) * deep, :], wo.at[g]) for g in range(groups)], sems)
    grad = gathered([part.at[2] for part in parts], place[2]).astype(BF16)
    for g in range(groups):
        moves[g].wait()
        total[:, g * deep : (g + 1) * deep] = dot_nt(grad, wo[g])
    for k, out in enumerate(outs):
        peer = place[5] ^ k
        rows = out.shape[0]
        out[:, :HD] = total[:, pl.ds(pl.multiple_of(peer // repeat * HD, HD), HD)].astype(BF16)
        out[:, HD:] = mix[pl.ds(pl.multiple_of(peer * rows, rows), rows), :]


def text_out_kernel(repeat, peers, place, wo_far, *refs):
    mixes = refs[:peers]
    outs = refs[peers:-3]
    wo, mixed, sems = refs[-3:]
    groups, deep, width = wo.shape
    moves = fetch([(wo_far.at[g * deep : (g + 1) * deep, :], wo.at[g]) for g in range(groups)], sems)
    for k, mix in enumerate(mixes):
        peer = place[5] ^ k

        @pl.when(peer % repeat == 0)
        def _():
            mixed[:, pl.ds(pl.multiple_of(peer // repeat * HD, HD), HD)] = mix[:, HD:]

    total = 0.0
    for g in range(groups):
        moves[g].wait()
        total = total + dot(mixed[:, g * deep : (g + 1) * deep], wo[g])
    whole = total.astype(BF16)
    for k, out in enumerate(outs):
        rows = out.shape[0]
        out[...] = dot(pick(rows, whole.shape[0], (place[2] ^ k) * rows).astype(F32).T.astype(BF16), whole).astype(BF16)


def turned(values, cos, sin):
    return values * cos + pltpu.roll(values, HD // 2, 1) * sin


def rope_tables(positions):
    half = HD // 2
    freq = np.exp(-(2.0 * np.arange(half) / HD) * math.log(ROPE_BASE)).astype(np.float32)
    angle = np.asarray(positions, np.float64)[:, None] * np.concatenate([freq, freq])[None].astype(np.float64)
    sign = np.where(np.arange(HD) < half, -1.0, 1.0)[None]
    return np.stack([np.cos(angle), np.sin(angle) * sign]).astype(np.float32)


def angles(cos_start, sin_start, steps):
    return cos_start * steps[0] - sin_start * steps[1], sin_start * steps[0] + cos_start * steps[1]


def start_row(starts, thr, b, extra):
    row = pl.ds(thr[b] + b * extra, 1)
    return starts[0, row, :], starts[1, row, :]


def image_kernel(high, wide, width, extra, thr, lat_all, cell, conv_t, proj_t, mapped, gram, starts, steps, steps_t, *refs):
    pre_down, act_t, patch_t, q_img, qt, k_img, kt, v_img, vt = refs[-9:]
    images, length, _ = pre_down.shape
    for n in range(images):
        number = pl.program_id(0) * images + n
        lanes = slice(n * length, (n + 1) * length)
        lat = lat_all[:, n * length : (n + 1) * length]
        chan = lat.shape[0]
        row = cell[0:1, :]
        col = cell[1:2, :]
        for r in range(3):
            for c in range(3):
                tap = r * 3 + c
                step = (r - 1) * wide + (c - 1)
                moved = pltpu.roll(lat, -step % lat.shape[1], 1) if step else lat
                keep = (row + (r - 1) >= 0) & (row + (r - 1) < high)
                keep &= (col + (c - 1) >= 0) & (col + (c - 1) < wide)
                patch_t[n, tap * chan : (tap + 1) * chan, :] = jnp.where(keep, moved, 0.0).astype(BF16)
        cos_start, sin_start = start_row(starts, thr, number, extra)
        before_t = dot(conv_t[...], patch_t[n])
        flat_t = silu(before_t).astype(BF16)
        act_t[n] = flat_t
        square = jnp.sum(dot(gram[...], flat_t) * flat_t.astype(F32), axis=0, keepdims=True)
        inv = lax.rsqrt(square * (1.0 / width) + EPSILON)
        heads_t = dot(proj_t[...], flat_t) * inv
        half = HD // 2
        column = lambda values: jnp.broadcast_to(values, (8, HD)).T[half:, :1]
        cos, sin = angles(column(cos_start), column(sin_start), steps_t)
        for at, out, scale in ((0, qt.at[n], SCALE * LOG2E), (HD, kt.at[:, lanes], 1.0)):
            first = heads_t[at : at + half]
            second = heads_t[at + half : at + HD]
            out[:half, :] = ((first * cos - second * sin) * scale).astype(BF16)
            out[half:, :] = ((second * cos + first * sin) * scale).astype(BF16)
        vt[:, lanes] = heads_t[2 * HD :].astype(BF16)
        before = before_t.T
        pre_down[n] = before
        act = silu(before).astype(BF16)
        square = jnp.sum(dot(act, gram[...]) * act.astype(F32), axis=-1, keepdims=True)
        inv = lax.rsqrt(square * (1.0 / width) + EPSILON)
        heads = dot(act, mapped[...])
        cos, sin = angles(cos_start, sin_start, steps)
        cos = cos * inv
        sin = sin * inv
        query = heads[:, :HD] * cos + heads[:, 3 * HD : 4 * HD] * sin
        q_img[n] = (query * (SCALE * LOG2E)).astype(BF16)
        k_img[n] = (heads[:, HD : 2 * HD] * cos + heads[:, 4 * HD :] * sin).astype(BF16)
        v_img[n] = (heads[:, 2 * HD : 3 * HD] * inv).astype(BF16)


def image_rows(sizes, thr, lat_t, cell, conv_t, proj_t, mapped, gram, starts, steps, steps_t, after):
    blocks = thr.shape[0]
    length = steps.shape[1]
    chan = lat_t.shape[0]
    down_chan, taps = conv_t.shape
    whole = lambda a: pl.BlockSpec(a.shape, lambda b: (0,) * len(a.shape))
    outs = [(length, down_chan, F32), (down_chan, length, BF16), (taps, length, BF16), (length, HD, BF16),
            (HD, length, BF16), (length, HD, BF16), None, (length, HD, BF16), None]
    per = 2
    flat = pl.BlockSpec((HD, per * length), lambda b: (0, b))
    return pl.pallas_call(
        lambda *refs: image_kernel(*sizes, *refs),
        out_shape=[jax.ShapeDtypeStruct((blocks, *o[:2]), o[2]) if o else jax.ShapeDtypeStruct((HD, blocks * length), BF16)
                   for o in outs],
        grid=(blocks // per,),
        in_specs=[pl.BlockSpec(memory_space=pltpu.SMEM), pl.BlockSpec((chan, per * length), lambda b: (0, b))]
        + [whole(a) for a in (cell, conv_t, proj_t, mapped, gram, starts, steps, steps_t)]
        + [pl.BlockSpec(memory_space=pl.ANY) for _ in after],
        out_specs=[pl.BlockSpec((per, *o[:2]), lambda b: (b, 0, 0)) if o else flat for o in outs],
        compiler_params=pltpu.CompilerParams(vmem_limit_bytes=VMEM_BYTES),
        cost_estimate=pl.CostEstimate(flops=8_000_000_000, bytes_accessed=8_000_000, transcendentals=0),
    )(thr, lat_t, cell, conv_t, proj_t, mapped, gram, starts, steps, steps_t, *after)


STRIP = 128


def strips(rows):
    return [slice(at, at + STRIP) for at in range(0, rows, STRIP)]


def attend_kernel(
    head, thr, near, far, u, qt_far, k_img_far, vt_far, *refs,
):
    texts = refs[:-18]
    (part, q_txt, qt_txt, k_txt, kt_txt, v_txt, mix_t, mix_txt_t, mix_txt, lse, lse_txt,
     scores, probs, text, qt, keys, vt, sems) = refs[-18:]
    blocks, length, _ = part.shape
    text_total = q_txt.shape[0]
    moves = fetch(
        [(k_img_far, keys.at[text_total:, :]), (qt_far, qt), (vt_far, vt.at[:HD, text_total:])], sems
    )
    row = iota((text_total, 1), 0)
    rows = text_total // blocks
    core = head[5] // len(texts)
    for k, values in enumerate(texts):
        pair = head[5] % len(texts) ^ k
        for r in range(2):
            spot = pl.ds(pl.multiple_of((2 * pair + (core ^ r)) * rows, rows), rows)
            text[spot, :] = values[r * rows : (r + 1) * rows, :]
    shifted = row >= sum(jnp.where(row // rows == b, thr[b], 0) for b in range(blocks))
    cos = jnp.where(shifted, far[0], near[0])
    sin = jnp.where(shifted, far[1], near[1])
    query = turned(text[:, :HD].astype(F32), cos, sin) * (SCALE * LOG2E)
    q_txt[...] = query.astype(BF16)
    qt_txt[...] = query.T.astype(BF16)
    key = turned(text[:, HD : 2 * HD].astype(F32), cos, sin)
    k_txt[...] = key.astype(BF16)
    keys[:text_total, :] = key.astype(BF16)
    kt_txt[...] = key.T.astype(BF16)
    v_txt[...] = text[:, 2 * HD :]
    vt[:HD, :text_total] = flip(text[:, 2 * HD :])
    vt[HD:, :] = jnp.ones((vt.shape[0] - HD, vt.shape[1]), BF16)
    for move in moves:
        move.wait()

    def begin(n):
        turned_query, count, _ = jobs[n]
        scores[n % 2, :count, : turned_query.shape[1]] = dot(keys[:count, :], turned_query)

    def softmax(n):
        turned_query, count, seen = jobs[n]
        wide = turned_query.shape[1]
        here = scores.at[n % 2]
        weights = probs.at[n % 2]
        fold = lambda values: values.reshape(STRIP // 8, 8, wide)
        top = None
        for at in strips(count):
            s = here[at, :wide]
            mask = seen(at)
            if mask is not None:
                s = jnp.where(mask, s, NEG_SCORE)
                here[at, :wide] = s
            peak = jnp.max(fold(s), axis=0)
            top = peak if top is None else jnp.maximum(top, peak)
        top = jnp.max(top, axis=0, keepdims=True)
        for at in strips(count):
            p = jnp.exp2(here[at, :wide] - top)
            mask = seen(at)
            if mask is not None:
                p = jnp.where(mask, p, 0.0)
            weights[at, :wide] = p.astype(BF16)
        mixed = dot(vt[:, :count], weights[:count, :wide])
        whole = mixed[HD : HD + 1, :]
        return mixed[:HD] / whole, top + jnp.log2(whole)

    def image_seen(i):
        return lambda at: iota((STRIP, length), 0) + at.start < thr[i] if at.start < text_total else None

    lane = iota((1, text_total), 1)
    jobs = [(qt[i], text_total + (i + 1) * length, image_seen(i)) for i in range(blocks)]
    jobs.append((
        qt_txt[...], text_total + blocks * length,
        lambda at: iota((STRIP, text_total), 0) + at.start <= lane
        if at.start < text_total else lane >= thr[(at.start - text_total) // length],
    ))
    begin(0)
    for i in range(blocks):
        begin(i + 1)
        mixed, logs = softmax(i)
        lse[i] = logs
        mix_t[i] = mixed.astype(BF16)
        part[i] = dot(mixed.T.astype(BF16), u[...]).astype(part.dtype)
    mixed, logs = softmax(blocks)
    lse_txt[...] = logs
    mix_txt_t[...] = mixed.astype(BF16)
    mix_txt[...] = mixed.T.astype(BF16)


def up_kernel(head, parts, pre_down, z, w_up_out, preds, grad_copies, prediction, grad_out_t):
    act = silu(pre_down[head[1]]).astype(BF16)
    pre_up = dot(act, z[...])
    for p in range(parts.shape[0]):
        pre_up = pre_up + parts[p].astype(F32)
    up_act = silu(pre_up).astype(BF16)
    grad = (dot_nt(preds[...], w_up_out[...]) * silu_slope(pre_up)).astype(BF16)
    for p in range(parts.shape[0]):
        grad_copies[p] = grad
    prediction[...] = dot(up_act, w_up_out[...]).astype(BF16)
    grad_out_t[...] = dot(flip(preds[...]), up_act)


def piece_spot(place, groups, pairs, number):
    group = number // (2 * pairs) ^ place[2]
    pair = number // 2 % pairs ^ place[3]
    return group, pair, number % 2 ^ place[4]


def put_piece(place, pieces, number, rows, values):
    _, groups, pairs, _, _ = pieces.shape
    group, pair, core = piece_spot(place, groups, pairs, number)
    pieces[core, group, pair, rows, :] = values


def add_core_kernel(keep, received, *outs):
    for k, out in enumerate(outs):
        out[...] = (keep[k].astype(F32) + received[k].astype(F32)).astype(BF16)


def add_sx_kernel(count, *refs):
    for m, out in enumerate(refs[count:]):
        out[...] = sum(r[m].astype(F32) for r in refs[:count]).astype(BF16)


def add_kernel(*refs):
    refs[-1][...] = sum(r[...].astype(F32) for r in refs[:-1]).astype(BF16)


def unpack_kernel(groups, pairs, own, place, *refs):
    count = 2 * groups
    grad_conv, grad_down, grad_up, grad_out_t, rest = refs[count:]
    few = refs[0].shape[1] - 2 * own
    per = HD // own
    for n, part in enumerate(refs[:count]):
        for m in range(pairs):
            number = ((place[2] ^ n % groups) * pairs + (place[3] ^ m)) * 2 + (place[4] ^ n // groups)
            grad_up[pl.ds(pl.multiple_of(number * own, own), own), :] = part[m, :own, :].astype(F32)
            cols = pl.ds(pl.multiple_of(number // per * HD, HD), HD)
            rows = pl.ds(pl.multiple_of(number % per * own, own), own)
            grad_down[rows, cols] = part[m, own : 2 * own, :].astype(F32)
            rest[pl.ds(pl.multiple_of(number * few, few), few), :] = part[m, 2 * own :, :].astype(F32)
    taps = grad_conv.shape[0]
    grad_conv[...] = rest[:taps, :]
    grad_out_t[...] = rest[taps : taps + grad_out_t.shape[0], :]


def plain(kernel, inputs, outs, after=()):
    whole = lambda a: pl.BlockSpec(a.shape, lambda: (0,) * len(a.shape))
    moved = sum(math.prod(a.shape) * a.dtype.itemsize for a in list(inputs) + list(outs))
    return pl.pallas_call(
        lambda *refs: kernel(*refs[: len(inputs)], *refs[len(inputs) + len(after) :]),
        out_shape=outs,
        in_specs=[whole(a) for a in inputs] + [pl.BlockSpec(memory_space=pl.ANY) for _ in after],
        out_specs=[whole(a) for a in outs],
        compiler_params=pltpu.CompilerParams(vmem_limit_bytes=SMALL_BYTES),
        cost_estimate=pl.CostEstimate(flops=0, bytes_accessed=moved, transcendentals=0),
    )(*inputs, *after)


def score_products(keys, values, room, first, last, turned_query, turned_grad):
    scores, pulls = room[:2]
    wide = turned_query.shape[1]
    scores[first:last, :wide] = dot(keys[first:last, :], turned_query)
    pulls[first:last, :wide] = dot(values[first:last, :], turned_grad)


def score_grads(room, first, last, logs, delta, seen):
    scores, pulls, probs, slopes = room
    wide = logs.shape[1]
    for at in strips(last)[first // STRIP :]:
        p = jnp.exp2(scores[at, :wide] - logs)
        mask = seen(at)
        if mask is not None:
            p = jnp.where(mask, p, 0.0)
        probs[at, :wide] = p.astype(BF16)
        slopes[at, :wide] = (p * (pulls[at, :wide] - delta)).astype(BF16)


def text_backward_kernel(place, thr, k_img, v_img, q_txt, qt_txt, mix_txt_t, lse_txt, *refs):
    backs = refs[:-7]
    dk, dv, d_txt, *room = refs[-7:]
    text_total = q_txt.shape[0]
    total = k_img.shape[0]
    blocks = thr.shape[0]
    rows = text_total // blocks
    for k, back in enumerate(backs):
        d_txt[pl.ds(pl.multiple_of((place[5] ^ k) * rows, rows), rows), :] = back[:, :HD]
    d_txt_t = d_txt[...].astype(F32).T
    delta = jnp.sum(d_txt_t * mix_txt_t[...].astype(F32), axis=0, keepdims=True)
    lane = iota((1, text_total), 1)
    score_products(k_img, v_img, room, 0, total, qt_txt[...], d_txt_t.astype(BF16))
    score_grads(
        room, 0, total, lse_txt[...], delta,
        lambda at: lane >= thr[at.start // (total // blocks)],
    )
    probs, slopes = room[2:]
    dk[...] = dot(slopes[...], q_txt[...])
    dv[...] = dot(probs[...], d_txt[...])


def backward_kernel(
    share, copies, extra, place, thr, grad_pre, k_txt, kt_txt, v_txt, lse, u, proj, gram, z, gain, starts, steps, grad_out_t, *refs,
):
    blocks, length, _ = grad_pre.shape
    (k_img_far, v_img_far, qt_far, kt_far, q_img_far, mix_t_far, dk_far, dv_far, pre_down_far, act_t_far, patch_t_far,
     wq_far, wk_far, wv_far, wo_far, w_up_far, w_down_far,
     keep, send,
     pieces, dq, dk, dv, cross_sum, small_sum, scores, pulls, probs, slopes,
     keys, values, qt, kt, q_img, mix_t, dk_text, dv_text, pre_down, act_t, patch_t, w_cols, w_rows, w_up,
     sems) = refs
    text_total = k_txt.shape[0]
    width = w_up.shape[0]
    cols = pl.ds(pl.multiple_of(place[0] * HD, HD), HD)
    moves = fetch(
        [(k_img_far, keys.at[text_total:, :]), (v_img_far, values.at[text_total:, :]), (qt_far, qt),
         (kt_far, kt.at[:, text_total:]), (q_img_far, q_img), (mix_t_far, mix_t), (dk_far, dk_text), (dv_far, dv_text),
         (pre_down_far, pre_down), (act_t_far, act_t), (patch_t_far, patch_t),
         (wq_far.at[:, cols], w_cols.at[:, :HD]), (wk_far.at[:, cols], w_cols.at[:, HD : 2 * HD]),
         (wv_far.at[:, cols], w_cols.at[:, 2 * HD :]), (wo_far.at[cols, :], w_rows.at[:HD, :]),
         (w_up_far, w_up), (w_down_far, w_rows.at[HD:, :])],
        sems,
    )
    cross_sum[...] = jnp.zeros_like(cross_sum)
    small_sum[...] = jnp.zeros_like(small_sum)
    keys[:text_total, :] = k_txt[...]
    values[:text_total, :] = v_txt[...]
    kt[:, :text_total] = kt_txt[...]
    for move in moves[:6]:
        move.wait()

    def begin(i):
        grad = grad_pre[i]
        cross_sum[...] += dot(mix_t[i], grad)
        d_t = dot_nt(u[...], grad).astype(BF16)
        delta = jnp.sum(d_t.astype(F32) * mix_t[i].astype(F32), axis=0, keepdims=True)
        room = [ref.at[i % 2] for ref in (scores, pulls, probs, slopes)]
        score_products(keys, values, room, 0, text_total + (i + 1) * length, qt[i], d_t)
        return room, delta, dot_nt(grad, u[...]).astype(BF16)

    def add(total, before, values):
        if before:
            total[:before, :] += values[:before]
        total[before : before + length, :] = values[before:]

    ahead = begin(0)
    for i in range(blocks):
        room, delta, d_out = ahead
        if i + 1 < blocks:
            ahead = begin(i + 1)
        before = i * length
        end = text_total + before + length
        score_grads(
            room, 0, end, lse[i], delta,
            lambda at: iota((STRIP, length), 0) + at.start < thr[i] if at.start < text_total else None,
        )
        add(dv, before, dot(room[2][text_total:end, :length], d_out))
        add(dk, before, dot(room[3][text_total:end, :length], q_img[i]))
        dq[i] = dot(kt[:, :end], room[3][:end, :length]).T
    for move in moves[6:11]:
        move.wait()
    taps = patch_t.shape[1]

    def block(b, query):
        cos, sin = angles(*start_row(starts, thr, b, extra), steps)
        own_rows = pl.ds(pl.multiple_of(b * length, length), length)

        def back(values):
            return values * cos - pltpu.roll(values, HD // 2, 1) * sin

        before = pre_down[b]
        act = silu(before).astype(BF16)
        act_wide = act.astype(F32)
        image = dot(act, gram[...])
        square = jnp.sum(image * act_wide, axis=-1, keepdims=True)
        inv = lax.rsqrt(square * (1.0 / width) + EPSILON)
        heads = jnp.concatenate(
            [back(query) * (inv * SCALE), back(dk[own_rows, :] + dk_text[own_rows, :]) * (inv * LN2),
             (dv[own_rows, :] + dv_text[own_rows, :]) * inv], axis=1
        ).astype(BF16)
        lift = dot_nt(heads, proj[...])
        crow = inv * inv * (jnp.sum(act_wide * lift, axis=-1, keepdims=True) * (1.0 / width))
        grad = grad_pre[b]
        d_act = (lift - crow * image) * copies + dot_nt(grad, z[...]) * share
        slope = (d_act * silu_slope(before)).astype(BF16)
        flipped = act_t[b]
        return (
            dot(patch_t[b], slope),
            dot(flipped, heads),
            dot(flipped, (act_wide * crow).astype(BF16)),
            dot(flipped, grad),
        )

    def step(n, carry):
        for b in (n, blocks // 2 + n):
            conv, *more = block(b, dq[b])
            small_sum[:taps, :] += conv
            carry = tuple(a + m for a, m in zip(carry, more))
        return carry

    rank = act_t.shape[1]
    spread, pull, inner = lax.fori_loop(
        0, blocks // 2, step,
        (jnp.zeros((rank, 3 * HD), F32), jnp.zeros((rank, rank), F32), jnp.zeros((rank, grad_pre.shape[2]), F32)),
    )
    for move in moves[11:]:
        move.wait()
    spread = (spread * copies).astype(BF16)
    pull = (pull * copies).astype(BF16)
    cross = (cross_sum[...] * copies).T.astype(BF16)
    inner_t = (inner * share).T.astype(BF16)
    inner = (inner * share).astype(BF16)
    small_sum[taps : taps + grad_out_t.shape[0], :] = grad_out_t[...]
    _, groups, pairs, rows, _ = pieces.shape
    own = width // (2 * groups * pairs)
    few = rows - 2 * own
    both_t = jnp.concatenate([cross, inner_t], axis=1)
    for at in range(0, width, 2 * HD):
        cols = slice(at, at + 2 * HD)
        scale = whole_row(gain[at // HD : at // HD + 2, :])
        down = dot_nt(spread, w_cols[cols, :]) * scale
        down = (down - dot(pull, w_rows[HD:, cols]) + dot_nt(inner, w_up[cols, :])).astype(BF16)
        up = dot(both_t, w_rows[:, cols]).T.astype(BF16)
        for part in range(0, 2 * HD, own):
            number = (at + part) // own
            tile = part // HD * HD
            put_piece(place, pieces, number, slice(0, own), up[part : part + own])
            put_piece(place, pieces, number, slice(own, 2 * own), down[part - tile : part - tile + own, tile : tile + HD])
    for number in range(2 * groups * pairs):
        put_piece(place, pieces, number, slice(2 * own, rows), small_sum[number * few : (number + 1) * few, :].astype(BF16))
    for move in fetch([(pieces.at[0], keep), (pieces.at[1], send)], sems):
        move.wait()


def shards(
    text_tokens,
    latent,
    image_offset,
    norm_gain,
    w_query,
    w_key,
    w_value,
    w_out,
    w_down_conv,
    w_down_proj,
    w_up_proj,
    w_up_out,
    pred_grad,
    text_grad,
):
    axes = ("sy", "sx")
    text_local = text_tokens[0]
    text_rows, width = text_local.shape
    lat_chan = w_up_out.shape[1]
    up_chan = w_up_proj.shape[1]
    down_chan = w_down_conv.shape[1]
    taps = w_down_conv.shape[0]
    tile_rows = latent.shape[1]
    tile_cols = latent.shape[2] // lat_chan
    row_groups = lax.axis_size("sx")
    blocks = lax.axis_size("sy")
    devices = row_groups * blocks
    high = tile_rows * row_groups
    length = high * tile_cols
    text_block = text_rows * row_groups
    text_total = text_block * blocks
    total = length * blocks
    block_len = length + text_block
    heads_here = w_query.shape[1] // HD
    repeat = blocks // heads_here
    assert heads_here * repeat == blocks and blocks % 2 == 0
    own = lax.axis_index("sy")
    share = 1.0 / devices
    copies = 1.0 / repeat

    device = own * row_groups + lax.axis_index("sx").astype(jnp.int32)
    group = lax.axis_index("sx").astype(jnp.int32)
    own = own.astype(jnp.int32)
    head = jnp.stack([own // repeat, device, group, own // 2, own % 2, own])

    def spread_over(values, axis, count):
        return lax.all_to_all(jnp.broadcast_to(values[None], (count,) + values.shape), axis, 0, 0)

    tag = jnp.broadcast_to(image_offset.astype(BF16)[:, None], (tile_rows, HD))
    packed = jnp.concatenate([latent[0], tag], axis=1)
    hop = lambda values, axis, by: lax.ppermute(
        values, axis, [(i, i ^ by) for i in range(row_groups if axis == "sx" else blocks)]
    )
    trio = jnp.stack([text_local, hop(text_local, "sy", 1), text_grad[0]])
    packed, trio = lax.optimization_barrier((packed, trio))
    text_parts = [trio] + [hop(trio, "sx", k) for k in range(1, row_groups)]
    side = spread_over(packed, axes, devices)

    gain = norm_gain.reshape(width // HD, HD)
    small = jax.ShapeDtypeStruct
    square = small((down_chan, down_chan), BF16)
    pairs = blocks // 2
    vmem = pltpu.VMEM
    dma = lambda count: pltpu.SemaphoreType.DMA((count,))
    bf = lambda *shape: small(shape, BF16)
    both = 2 * text_block
    chunks = 8
    wide = heads_here * HD // 2
    proj, proj_t, mapped, u, gram, z, conv_t, *text_here = call(
        lambda *refs: front_kernel(row_groups, repeat, *refs), head,
        [(gain, None), (w_down_conv, None)]
        + [(a, pl.ANY) for a in (w_down_proj, w_query, w_key, w_value, w_up_proj, w_out)]
        + [(a, None) for a in text_parts],
        [bf(down_chan, 3 * HD), bf(3 * HD, down_chan), bf(down_chan, 5 * HD), bf(HD, up_chan),
         bf(down_chan, down_chan), bf(down_chan, up_chan), bf(down_chan, taps)] + [bf(both, 3 * HD)] * pairs,
        [vmem((down_chan, width), BF16)] + [vmem((width, HD), BF16)] * 3
        + [vmem((width, up_chan), BF16), vmem((HD, width), BF16),
           vmem((chunks, 3, width // chunks, wide), BF16), vmem((both, width), BF16), vmem((3, both, wide), F32),
           dma(6 + 3 * chunks)],
        flops=4_000_000_000 + 6 * both * width * wide,
    )
    texts = [
        lax.ppermute(values, "sy", [(2 * z + c, c * pairs + (z ^ k)) for z in range(pairs) for c in range(2)])
        for k, values in enumerate(text_here)
    ]

    side = side.reshape(blocks, row_groups, tile_rows, -1)
    lat_t = side[..., : tile_cols * lat_chan].reshape(total, lat_chan).T.astype(F32)
    offsets = side[:, 0, 0, tile_cols * lat_chan].astype(jnp.int32)
    block_ids = jnp.arange(blocks, dtype=jnp.int32)
    thr = block_ids * text_block + offsets
    ids = np.arange(length, dtype=np.int32)
    cell = np.stack([ids // tile_cols, ids % tile_cols])
    at = np.arange(blocks)[:, None]
    steps = rope_tables(ids)
    steps_t = np.ascontiguousarray(np.swapaxes(steps, 1, 2)[:, HD // 2 :])
    starts = rope_tables((at * block_len + np.arange(text_block + 1)).reshape(-1))
    near = (at * block_len + np.arange(text_block)).reshape(-1)
    near, far = rope_tables(near), rope_tables(near + length)

    chunk = lambda kind, rows=length, cols=HD: small((blocks, rows, cols), kind)
    text_kind = small((text_total, HD), BF16)
    text_flip = small((HD, text_total), BF16)
    side_len = max(length, text_total)
    seq = text_total + total
    pre_down, act_t, patch_t, q_img, qt, k_img, kt, v_img, vt = image_rows(
        (high, tile_cols, width, 1), thr, lat_t, cell, conv_t, proj_t, mapped, gram, starts, steps, steps_t,
        text_here[:1]
    )
    part, q_txt, qt_txt, k_txt, kt_txt, v_txt, mix_t, mix_txt_t, mix_txt, lse, lse_txt = call(
        attend_kernel, head,
        [(thr, pltpu.SMEM), (near, None), (far, None), (u, None), (qt, pl.ANY), (k_img.reshape(total, HD), pl.ANY),
         (vt, pl.ANY)]
        + [(a, None) for a in texts],
        [chunk(BF16, length, up_chan), text_kind, text_flip, text_kind, text_flip, text_kind, chunk(BF16, HD, length),
         text_flip, text_kind, small((blocks, 1, length), F32), small((1, text_total), F32)],
        [vmem((2, seq, side_len), F32), vmem((2, seq, side_len), BF16), vmem((text_total, 3 * HD), BF16),
         vmem(qt.shape, BF16), vmem((seq, HD), BF16), vmem((HD + 16, seq), BF16), dma(3)],
        flops=6_000_000_000,
    )

    own_rows = tile_rows * tile_cols
    part = part if repeat == 1 else part * jnp.asarray(copies, BF16)
    parts = lax.all_to_all(part.reshape(devices, own_rows, up_chan), axes, 0, 0)
    wo_room = [vmem((4, heads_here * HD // 4, width), BF16)]
    text_back = call(
        lambda *refs: text_grad_kernel(row_groups, repeat, *refs), head,
        [(w_out, pl.ANY), (mix_txt, None)] + [(a, None) for a in text_parts],
        [bf(text_block, 2 * HD)] * blocks,
        wo_room + [vmem((text_block, heads_here * HD), F32), dma(4)],
        flops=2 * text_block * width * heads_here * HD,
        after=[part],
    )
    text_back = [text_back[0]] + [hop(text_back[k], "sy", k) for k in range(1, blocks)]
    grad_copies, prediction, grad_out_t = call(
        up_kernel, head,
        [(parts, None), (pre_down.reshape(devices, own_rows, down_chan), None), (z, None), (w_up_out, None),
         (pred_grad[0].reshape(own_rows, lat_chan), None)],
        [small((devices, own_rows, up_chan), BF16), small((own_rows, lat_chan), BF16), small((lat_chan, up_chan), F32)],
        flops=2_000_000_000,
        after=text_back[1:],
        room=SMALL_BYTES,
    )
    grad_pre = lax.all_to_all(grad_copies, axes, 0, 0).reshape(blocks, length, up_chan)

    own_part = width // devices
    few = -(-(taps + lat_chan) // (16 * devices)) * 16
    lump = lambda rows: small((pairs, rows, HD), BF16)
    flat = lambda rows: small((rows, HD), BF16)
    vmem = pltpu.VMEM
    def core_sum(keep, send, rows):
        return plain(add_core_kernel, [keep, hop(send, "sy", 1)], [lump(rows)] * row_groups)

    def sx_sum(sums, rows, after=()):
        sums = [sums[0]] + [hop(sums[k], "sx", k) for k in range(1, row_groups)]
        return plain(lambda *refs: add_sx_kernel(row_groups, *refs), sums, [flat(rows)] * pairs, after)

    def z_sum(sums, rows, after=()):
        sums = [sums[0]] + [hop(sums[m], "sy", 2 * m) for m in range(1, pairs)]
        return plain(add_kernel, sums, [flat(rows)], after)[0]

    def spread_z(mine):
        return jnp.stack([mine] + [hop(mine, "sy", 2 * m) for m in range(1, pairs)])

    def spread_sx(mine):
        near = [mine] + [hop(mine, "sx", k) for k in range(1, row_groups)]
        return near + [hop(values, "sy", 1) for values in near]

    mixed = call(
        lambda *refs: text_out_kernel(repeat, blocks, *refs), head,
        [(w_out, pl.ANY)] + [(a, None) for a in text_back],
        [bf(text_rows, width)] * row_groups,
        wo_room + [vmem((text_block, heads_here * HD), BF16), dma(4)],
        flops=2 * text_block * width * heads_here * HD,
        after=[grad_copies],
    )
    mixed = [mixed[0]] + [hop(mixed[k], "sx", k) for k in range(1, row_groups)]
    text_out = (text_local.astype(F32) + sum(m.astype(F32) for m in mixed)).astype(BF16)
    k_rows, v_rows = k_img.reshape(total, HD), v_img.reshape(total, HD)
    strip_room = lambda *lead: [vmem((*lead, side_len), F32)] * 2 + [vmem((*lead, side_len), BF16)] * 2
    dk, dv = call(
        text_backward_kernel, head,
        [(thr, pltpu.SMEM)] + [(a, None) for a in (k_rows, v_rows, q_txt, qt_txt, mix_txt_t, lse_txt, *text_back)],
        [small((total, HD), F32)] * 2,
        [vmem((text_total, HD), BF16)] + [vmem((total, text_total), kind) for kind in (F32, F32, BF16, BF16)],
        flops=2_000_000_000,
        after=mixed[:1] + [grad_copies],
    )
    rows = 2 * own_part + few
    near_arrays = (k_rows, v_rows, qt, kt, q_img, mix_t, dk, dv, pre_down, act_t, patch_t)
    far_arrays = near_arrays + (w_query, w_key, w_value, w_out, w_up_proj, w_down_proj)
    keep, send = call(
        lambda *refs: backward_kernel(share, copies, 1, *refs), head,
        [(thr, pltpu.SMEM)] + [(a, None) for a in (
            grad_pre, k_txt, kt_txt, v_txt, lse, u, proj, gram, z, gain, starts, steps, grad_out_t)]
        + [(a, pl.ANY) for a in far_arrays],
        [small((row_groups, pairs, rows, HD), BF16)] * 2,
        [vmem((2, row_groups, pairs, rows, HD), BF16), vmem((blocks, length, HD), F32), vmem((total, HD), F32),
         vmem((total, HD), F32), vmem((HD, up_chan), F32), vmem((devices * few, HD), F32)]
        + strip_room(2, seq)
        + [vmem((seq, HD), BF16)] * 2 + [vmem(qt.shape, BF16), vmem((HD, seq), BF16)]
        + [vmem(a.shape, a.dtype) for a in (q_img, mix_t, dk, dv, pre_down, act_t, patch_t)]
        + [vmem((width, 3 * HD), BF16), vmem((HD + down_chan, width), BF16), vmem(w_up_proj.shape, BF16),
           pltpu.SemaphoreType.DMA((len(far_arrays),))],
        flops=30_000_000_000,
        after=mixed[1:],
    )
    mine = spread_z(z_sum(sx_sum(core_sum(keep, send, rows), rows), rows))
    grad_conv, grad_down, grad_up, grad_out_t = call(
        lambda *refs: unpack_kernel(row_groups, pairs, own_part, *refs), head,
        [(a, None) for a in spread_sx(mine)],
        [small((taps, down_chan), F32), small((down_chan, width), F32), small((width, up_chan), F32),
         small((lat_chan, up_chan), F32)],
        [vmem((devices * few, HD), F32)],
        room=2 * SMALL_BYTES,
    )
    return (
        prediction.reshape(1, tile_rows, tile_cols * lat_chan),
        text_out[None],
        grad_conv,
        grad_down,
        grad_up,
        grad_out_t.T,
    )


def solution(mesh):
    placed = (
        P("sy", "sx", None),
        P("sy", "sx", None),
        P("sy"),
        P(),
        P(None, "sx"),
        P(None, "sx"),
        P(None, "sx"),
        P("sx", None),
        P(),
        P(),
        P(),
        P(),
        P("sy", "sx", None),
        P("sy", "sx", None),
    )
    return jax.shard_map(
        shards,
        mesh=mesh,
        in_specs=placed,
        out_specs=(P("sy", "sx", None), P("sy", "sx", None), P(), P(), P(), P()),
        check_vma=False,
    )
```

```python
import math

import jax
import jax.numpy as jnp
import numpy as np
from jax import lax
from jax.experimental import pallas as pl
from jax.experimental.pallas import tpu as pltpu
from jax.sharding import PartitionSpec as P

HD = 128
EPSILON = 1e-05
NEG_SCORE = -1e30
ROPE_BASE = 500000.0
SCALE = HD ** (-0.5)
LOG2E = math.log2(math.e)
LN2 = math.log(2.0)
F32 = jnp.float32
BF16 = jnp.bfloat16
MIB = 1024 * 1024
VMEM_BYTES = 56 * MIB
SMALL_BYTES = 16 * MIB


def dot(left, right):
    return jnp.dot(left, right, preferred_element_type=F32)


def dot_nt(left, right):
    return lax.dot_general(left, right, (((1,), (1,)), ((), ())), preferred_element_type=F32)


def silu_slope(values):
    sigma = jax.nn.sigmoid(values)
    return sigma * (1.0 + values * (1.0 - sigma))


def silu(values):
    return values * jax.nn.sigmoid(values)


def iota(shape, dim):
    return lax.broadcasted_iota(jnp.int32, shape, dim)


def flip(values):
    return values.astype(F32).T.astype(BF16)


def call(kernel, place, inputs, outs, scratch=(), flops=0, after=(), room=VMEM_BYTES):
    inputs = [(place, pltpu.SMEM)] + list(inputs)
    count = len(inputs)
    skip = count + len(after)
    moved = sum(math.prod(a.shape) * a.dtype.itemsize for a in list(outs) + [a for a, space in inputs if space is None])
    return pl.pallas_call(
        lambda *refs: kernel(*refs[:count], *refs[skip:]),
        out_shape=outs,
        in_specs=[pl.BlockSpec(memory_space=pltpu.VMEM if space is None else space) for _, space in inputs]
        + [pl.BlockSpec(memory_space=pl.ANY) for _ in after],
        out_specs=[pl.BlockSpec(memory_space=pltpu.VMEM) for _ in outs],
        scratch_shapes=list(scratch),
        compiler_params=pltpu.CompilerParams(vmem_limit_bytes=room),
        cost_estimate=pl.CostEstimate(flops=flops, bytes_accessed=moved, transcendentals=0),
    )(*[a for a, _ in inputs], *after)


def fetch(moves, sems):
    moves = [pltpu.make_async_copy(far, near, sems.at[n]) for n, (far, near) in enumerate(moves)]
    for move in moves:
        move.start()
    return moves


def whole_row(gain):
    return jnp.concatenate([gain[r : r + 1, :].astype(F32) for r in range(gain.shape[0])], axis=1)


def pick(rows, total, spot):
    return (iota((total, rows), 0) == iota((total, rows), 1) + spot).astype(BF16)


def gathered(parts, group):
    rows = parts[0].shape[0]
    total = rows * len(parts)
    return sum(dot(pick(rows, total, (group ^ k) * rows), part[...]) for k, part in enumerate(parts))


def front_kernel(count, repeat, place, gain, w_conv, w_down_far, wq_far, wk_far, wv_far, w_up_far, wo_far, *refs):
    parts = refs[:count]
    proj, proj_t, mapped, u, gram, z, conv_t = refs[count : count + 7]
    outs = refs[count + 7 : -10]
    w_down, wq, wk, wv, w_up, wo, weights, normed, sums, sems = refs[-10:]
    chunks, _, deep, wide = weights.shape
    cols = pl.ds(pl.multiple_of(place[0] * HD, HD), HD)
    half = pl.ds(pl.multiple_of(place[4] * wide, wide), wide)
    moves = fetch(
        [(w_down_far, w_down), (wq_far.at[:, cols], wq), (wk_far.at[:, cols], wk), (wv_far.at[:, cols], wv),
         (w_up_far, w_up), (wo_far.at[cols, :], wo)]
        + [(far.at[c * deep : (c + 1) * deep, half], weights.at[c, n])
           for c in range(chunks) for n, far in enumerate((wq_far, wk_far, wv_far))],
        sems,
    )
    conv_t[...] = flip(w_conv[...])
    rows = normed.shape[0] // 2
    row = whole_row(gain)
    for r in range(2):
        x = gathered([part.at[r] for part in parts], place[2])
        inverse = lax.rsqrt(jnp.mean(x * x, axis=-1, keepdims=True) + EPSILON)
        normed[r * rows : (r + 1) * rows, :] = (x * inverse * row).astype(BF16)
    moves[0].wait()
    down = w_down[...]
    scaled = (down.astype(F32) * row).astype(BF16)
    gram[...] = dot_nt(down, down).astype(BF16)
    for n, w in enumerate((wq, wk, wv)):
        cols = slice(n * HD, (n + 1) * HD)
        moves[1 + n].wait()
        total = dot(scaled, w[...])
        proj[:, cols] = total.astype(BF16)
        proj_t[cols, :] = total.T.astype(BF16)
        mapped[:, cols] = total.astype(BF16)
        if n < 2:
            mapped[:, (3 + n) * HD : (4 + n) * HD] = pltpu.roll(total, HD // 2, 1).astype(BF16)
    moves[4].wait()
    z[...] = dot(down, w_up[...]).astype(BF16)
    moves[5].wait()
    u[...] = dot(wo[...], w_up[...]).astype(BF16)
    for c in range(chunks):
        here = normed[:, c * deep : (c + 1) * deep]
        for n in range(3):
            moves[6 + 3 * c + n].wait()
            term = dot(here, weights[c, n])
            sums[n] = term if c == 0 else sums[n] + term
    for k, out in enumerate(outs):
        head = pl.ds(pl.multiple_of((place[3] ^ k) // repeat * HD, HD), HD)
        for n in range(3):
            out[:, n * HD : (n + 1) * HD] = sums[n, :, head].astype(BF16)


def text_grad_kernel(count, repeat, place, wo_far, mix, *refs):
    parts = refs[:count]
    keep, send, wo, total, sems = refs[count:]
    groups, deep, _ = wo.shape
    moves = fetch([(wo_far.at[g * deep : (g + 1) * deep, :], wo.at[g]) for g in range(groups)], sems)
    grad_t = gathered([part.at[2] for part in parts], place[2]).T.astype(BF16)
    for g in range(groups):
        moves[g].wait()
        total[g * deep : (g + 1) * deep, :] = dot(wo[g], grad_t)
    pairs, rows, _ = keep.shape
    for flip_core, out in enumerate((keep, send)):
        for m in range(pairs):
            peer = (place[3] ^ m) * 2 + (place[4] ^ flip_core)
            out[m, :, :HD] = total[pl.ds(pl.multiple_of(peer // repeat * HD, HD), HD), :].T.astype(BF16)
            out[m, :, HD:] = mix[pl.ds(pl.multiple_of(peer * rows, rows), rows), :]


def merge_kernel(keep, received, *outs):
    rows = keep.shape[1]
    for m, out in enumerate(outs):
        out[:rows, :] = keep[m]
        out[rows:, :] = received[m]


def by_peer(backs, rows):
    return [backs[k // 2].at[k % 2 * rows : (k % 2 + 1) * rows, :] for k in range(2 * len(backs))]


def text_out_kernel(repeat, peers, place, wo_far, *refs):
    outs = refs[peers // 2 : -3]
    wo, mixed, sems = refs[-3:]
    mixes = by_peer(refs[: peers // 2], mixed.shape[0])
    groups, deep, width = wo.shape
    moves = fetch([(wo_far.at[g * deep : (g + 1) * deep, :], wo.at[g]) for g in range(groups)], sems)
    for k, mix in enumerate(mixes):
        peer = place[5] ^ k

        @pl.when(peer % repeat == 0)
        def _():
            mixed[:, pl.ds(pl.multiple_of(peer // repeat * HD, HD), HD)] = mix[:, HD:]

    total = 0.0
    for g in range(groups):
        moves[g].wait()
        total = total + dot(mixed[:, g * deep : (g + 1) * deep], wo[g])
    whole = total.astype(BF16)
    for k, out in enumerate(outs):
        rows = out.shape[0]
        out[...] = dot(pick(rows, whole.shape[0], (place[2] ^ k) * rows).astype(F32).T.astype(BF16), whole).astype(BF16)


def turned(values, cos, sin):
    return values * cos + pltpu.roll(values, HD // 2, 1) * sin


def rope_tables(positions):
    half = HD // 2
    freq = np.exp(-(2.0 * np.arange(half) / HD) * math.log(ROPE_BASE)).astype(np.float32)
    angle = np.asarray(positions, np.float64)[:, None] * np.concatenate([freq, freq])[None].astype(np.float64)
    sign = np.where(np.arange(HD) < half, -1.0, 1.0)[None]
    return np.stack([np.cos(angle), np.sin(angle) * sign]).astype(np.float32)


def angles(cos_start, sin_start, steps):
    return cos_start * steps[0] - sin_start * steps[1], sin_start * steps[0] + cos_start * steps[1]


def start_row(starts, thr, b, extra):
    row = pl.ds(thr[b] + b * extra, 1)
    return starts[0, row, :], starts[1, row, :]


def image_kernel(high, wide, width, extra, thr, lat_all, cell, conv_t, proj_t, mapped, gram, starts, steps, steps_t, *refs):
    pre_down, act_t, patch_t, q_img, qt, k_img, kt, v_img, vt = refs[-9:]
    images, length, _ = pre_down.shape
    for n in range(images):
        number = pl.program_id(0) * images + n
        lanes = slice(n * length, (n + 1) * length)
        lat = lat_all[:, n * length : (n + 1) * length]
        chan = lat.shape[0]
        row = cell[0:1, :]
        col = cell[1:2, :]
        for r in range(3):
            for c in range(3):
                tap = r * 3 + c
                step = (r - 1) * wide + (c - 1)
                moved = pltpu.roll(lat, -step % lat.shape[1], 1) if step else lat
                keep = (row + (r - 1) >= 0) & (row + (r - 1) < high)
                keep &= (col + (c - 1) >= 0) & (col + (c - 1) < wide)
                patch_t[n, tap * chan : (tap + 1) * chan, :] = jnp.where(keep, moved, 0.0).astype(BF16)
        cos_start, sin_start = start_row(starts, thr, number, extra)
        before_t = dot(conv_t[...], patch_t[n])
        flat_t = silu(before_t).astype(BF16)
        act_t[n] = flat_t
        square = jnp.sum(dot(gram[...], flat_t) * flat_t.astype(F32), axis=0, keepdims=True)
        inv = lax.rsqrt(square * (1.0 / width) + EPSILON)
        heads_t = dot(proj_t[...], flat_t) * inv
        half = HD // 2
        column = lambda values: jnp.broadcast_to(values, (8, HD)).T[half:, :1]
        cos, sin = angles(column(cos_start), column(sin_start), steps_t)
        for at, out, scale in ((0, qt.at[n], SCALE * LOG2E), (HD, kt.at[:, lanes], 1.0)):
            first = heads_t[at : at + half]
            second = heads_t[at + half : at + HD]
            out[:half, :] = ((first * cos - second * sin) * scale).astype(BF16)
            out[half:, :] = ((second * cos + first * sin) * scale).astype(BF16)
        vt[:, lanes] = heads_t[2 * HD :].astype(BF16)
        before = before_t.T
        pre_down[n] = before
        act = silu(before).astype(BF16)
        square = jnp.sum(dot(act, gram[...]) * act.astype(F32), axis=-1, keepdims=True)
        inv = lax.rsqrt(square * (1.0 / width) + EPSILON)
        heads = dot(act, mapped[...])
        cos, sin = angles(cos_start, sin_start, steps)
        cos = cos * inv
        sin = sin * inv
        query = heads[:, :HD] * cos + heads[:, 3 * HD : 4 * HD] * sin
        q_img[n] = (query * (SCALE * LOG2E)).astype(BF16)
        k_img[n] = (heads[:, HD : 2 * HD] * cos + heads[:, 4 * HD :] * sin).astype(BF16)
        v_img[n] = (heads[:, 2 * HD : 3 * HD] * inv).astype(BF16)


def image_rows(sizes, thr, lat_t, cell, conv_t, proj_t, mapped, gram, starts, steps, steps_t, after):
    blocks = thr.shape[0]
    length = steps.shape[1]
    chan = lat_t.shape[0]
    down_chan, taps = conv_t.shape
    whole = lambda a: pl.BlockSpec(a.shape, lambda b: (0,) * len(a.shape))
    outs = [(length, down_chan, F32), (down_chan, length, BF16), (taps, length, BF16), (length, HD, BF16),
            (HD, length, BF16), (length, HD, BF16), None, (length, HD, BF16), None]
    per = math.gcd(blocks, 4)
    flat = pl.BlockSpec((HD, per * length), lambda b: (0, b))
    return pl.pallas_call(
        lambda *refs: image_kernel(*sizes, *refs),
        out_shape=[jax.ShapeDtypeStruct((blocks, *o[:2]), o[2]) if o else jax.ShapeDtypeStruct((HD, blocks * length), BF16)
                   for o in outs],
        grid=(blocks // per,),
        in_specs=[pl.BlockSpec(memory_space=pltpu.SMEM), pl.BlockSpec((chan, per * length), lambda b: (0, b))]
        + [whole(a) for a in (cell, conv_t, proj_t, mapped, gram, starts, steps, steps_t)]
        + [pl.BlockSpec(memory_space=pl.ANY) for _ in after],
        out_specs=[pl.BlockSpec((per, *o[:2]), lambda b: (b, 0, 0)) if o else flat for o in outs],
        compiler_params=pltpu.CompilerParams(vmem_limit_bytes=VMEM_BYTES),
        cost_estimate=pl.CostEstimate(flops=8_000_000_000, bytes_accessed=8_000_000, transcendentals=0),
    )(thr, lat_t, cell, conv_t, proj_t, mapped, gram, starts, steps, steps_t, *after)


STRIP = 128


def strips(rows):
    return [slice(at, at + STRIP) for at in range(0, rows, STRIP)]


def attend_kernel(
    head, thr, near, far, u, qt_far, k_img_far, vt_far, *refs,
):
    texts = refs[:-18]
    (part, q_txt, qt_txt, k_txt, kt_txt, v_txt, mix_t, mix_txt_t, mix_txt, lse, lse_txt,
     scores, probs, text, qt, keys, vt, sems) = refs[-18:]
    blocks, length, _ = part.shape
    text_total = q_txt.shape[0]
    moves = fetch(
        [(k_img_far, keys.at[text_total:, :]), (qt_far, qt), (vt_far, vt.at[:HD, text_total:])], sems
    )
    row = iota((text_total, 1), 0)
    rows = text_total // blocks
    core = head[5] // len(texts)
    for k, values in enumerate(texts):
        pair = head[5] % len(texts) ^ k
        for r in range(2):
            spot = pl.ds(pl.multiple_of((2 * pair + (core ^ r)) * rows, rows), rows)
            text[spot, :] = values[r * rows : (r + 1) * rows, :]
    shifted = row >= sum(jnp.where(row // rows == b, thr[b], 0) for b in range(blocks))
    cos = jnp.where(shifted, far[0], near[0])
    sin = jnp.where(shifted, far[1], near[1])
    query = turned(text[:, :HD].astype(F32), cos, sin) * (SCALE * LOG2E)
    q_txt[...] = query.astype(BF16)
    qt_txt[...] = query.T.astype(BF16)
    key = turned(text[:, HD : 2 * HD].astype(F32), cos, sin)
    k_txt[...] = key.astype(BF16)
    keys[:text_total, :] = key.astype(BF16)
    kt_txt[...] = key.T.astype(BF16)
    v_txt[...] = text[:, 2 * HD :]
    vt[:HD, :text_total] = flip(text[:, 2 * HD :])
    vt[HD:, :] = jnp.ones((vt.shape[0] - HD, vt.shape[1]), BF16)
    for move in moves:
        move.wait()

    def begin(n):
        turned_query, count, _ = jobs[n]
        scores[n % 2, :count, : turned_query.shape[1]] = dot(keys[:count, :], turned_query)

    def softmax(n):
        turned_query, count, seen = jobs[n]
        wide = turned_query.shape[1]
        here = scores.at[n % 2]
        weights = probs.at[n % 2]
        fold = lambda values: values.reshape(STRIP // 8, 8, wide)
        top = None
        for at in strips(count):
            s = here[at, :wide]
            mask = seen(at)
            if mask is not None:
                s = jnp.where(mask, s, NEG_SCORE)
                here[at, :wide] = s
            peak = jnp.max(fold(s), axis=0)
            top = peak if top is None else jnp.maximum(top, peak)
        top = jnp.max(top, axis=0, keepdims=True)
        for at in strips(count):
            p = jnp.exp2(here[at, :wide] - top)
            mask = seen(at)
            if mask is not None:
                p = jnp.where(mask, p, 0.0)
            weights[at, :wide] = p.astype(BF16)
        mixed = dot(vt[:, :count], weights[:count, :wide])
        whole = mixed[HD : HD + 1, :]
        return mixed[:HD] / whole, top + jnp.log2(whole)

    def image_seen(i):
        return lambda at: iota((STRIP, length), 0) + at.start < thr[i] if at.start < text_total else None

    lane = iota((1, text_total), 1)
    jobs = [(qt[i], text_total + (i + 1) * length, image_seen(i)) for i in range(blocks)]
    jobs.append((
        qt_txt[...], text_total + blocks * length,
        lambda at: iota((STRIP, text_total), 0) + at.start <= lane
        if at.start < text_total else lane >= thr[(at.start - text_total) // length],
    ))
    begin(0)
    for i in range(blocks):
        begin(i + 1)
        mixed, logs = softmax(i)
        lse[i] = logs
        mix_t[i] = mixed.astype(BF16)
        part[i] = dot(mixed.T.astype(BF16), u[...]).astype(part.dtype)
    mixed, logs = softmax(blocks)
    lse_txt[...] = logs
    mix_txt_t[...] = mixed.astype(BF16)
    mix_txt[...] = mixed.T.astype(BF16)


def up_kernel(head, parts, pre_down, z, w_up_out, preds, grad_copies, prediction, grad_out_t):
    act = silu(pre_down[head[1]]).astype(BF16)
    pre_up = dot(act, z[...])
    for p in range(parts.shape[0]):
        pre_up = pre_up + parts[p].astype(F32)
    up_act = silu(pre_up).astype(BF16)
    grad = (dot_nt(preds[...], w_up_out[...]) * silu_slope(pre_up)).astype(BF16)
    for p in range(parts.shape[0]):
        grad_copies[p] = grad
    prediction[...] = dot(up_act, w_up_out[...]).astype(BF16)
    grad_out_t[...] = dot(flip(preds[...]), up_act)


def piece_spot(place, groups, pairs, number):
    group = number // (2 * pairs) ^ place[2]
    pair = number // 2 % pairs ^ place[3]
    return group, pair, number % 2 ^ place[4]


def put_piece(place, pieces, number, rows, values):
    _, groups, pairs, _, _ = pieces.shape
    group, pair, core = piece_spot(place, groups, pairs, number)
    pieces[core, group, pair, rows, :] = values


def add_core_kernel(keep, received, *outs):
    for k, out in enumerate(outs):
        out[...] = (keep[k].astype(F32) + received[k].astype(F32)).astype(BF16)


def add_sx_kernel(count, *refs):
    for m, out in enumerate(refs[count:]):
        out[...] = sum(r[m].astype(F32) for r in refs[:count]).astype(BF16)


def add_kernel(*refs):
    refs[-1][...] = sum(r[...].astype(F32) for r in refs[:-1]).astype(BF16)


def unpack_kernel(groups, pairs, own, place, *refs):
    count = 2 * groups
    grad_conv, grad_down, grad_up, grad_out_t, rest = refs[count:]
    few = refs[0].shape[1] - 2 * own
    per = HD // own
    for n, part in enumerate(refs[:count]):
        for m in range(pairs):
            number = ((place[2] ^ n % groups) * pairs + (place[3] ^ m)) * 2 + (place[4] ^ n // groups)
            grad_up[pl.ds(pl.multiple_of(number * own, own), own), :] = part[m, :own, :].astype(F32)
            cols = pl.ds(pl.multiple_of(number // per * HD, HD), HD)
            rows = pl.ds(pl.multiple_of(number % per * own, own), own)
            grad_down[rows, cols] = part[m, own : 2 * own, :].astype(F32)
            rest[pl.ds(pl.multiple_of(number * few, few), few), :] = part[m, 2 * own :, :].astype(F32)
    taps = grad_conv.shape[0]
    grad_conv[...] = rest[:taps, :]
    grad_out_t[...] = rest[taps : taps + grad_out_t.shape[0], :]


def plain(kernel, inputs, outs, after=()):
    whole = lambda a: pl.BlockSpec(a.shape, lambda: (0,) * len(a.shape))
    moved = sum(math.prod(a.shape) * a.dtype.itemsize for a in list(inputs) + list(outs))
    return pl.pallas_call(
        lambda *refs: kernel(*refs[: len(inputs)], *refs[len(inputs) + len(after) :]),
        out_shape=outs,
        in_specs=[whole(a) for a in inputs] + [pl.BlockSpec(memory_space=pl.ANY) for _ in after],
        out_specs=[whole(a) for a in outs],
        compiler_params=pltpu.CompilerParams(vmem_limit_bytes=SMALL_BYTES),
        cost_estimate=pl.CostEstimate(flops=0, bytes_accessed=moved, transcendentals=0),
    )(*inputs, *after)


def score_products(keys, values, room, first, last, turned_query, turned_grad):
    scores, pulls = room[:2]
    wide = turned_query.shape[1]
    scores[first:last, :wide] = dot(keys[first:last, :], turned_query)
    pulls[first:last, :wide] = dot(values[first:last, :], turned_grad)


def score_grads(room, first, last, logs, delta, seen):
    scores, pulls, probs, slopes = room
    wide = logs.shape[1]
    for at in strips(last)[first // STRIP :]:
        p = jnp.exp2(scores[at, :wide] - logs)
        mask = seen(at)
        if mask is not None:
            p = jnp.where(mask, p, 0.0)
        probs[at, :wide] = p.astype(BF16)
        slopes[at, :wide] = (p * (pulls[at, :wide] - delta)).astype(BF16)


def text_backward_kernel(place, thr, k_img, v_img, q_txt, qt_txt, mix_txt_t, lse_txt, *refs):
    dk, dv, d_txt, *room = refs[-7:]
    text_total = q_txt.shape[0]
    total = k_img.shape[0]
    blocks = thr.shape[0]
    rows = text_total // blocks
    for k, back in enumerate(by_peer(refs[:-7], rows)):
        d_txt[pl.ds(pl.multiple_of((place[5] ^ k) * rows, rows), rows), :] = back[:, :HD]
    d_txt_t = d_txt[...].astype(F32).T
    delta = jnp.sum(d_txt_t * mix_txt_t[...].astype(F32), axis=0, keepdims=True)
    lane = iota((1, text_total), 1)
    score_products(k_img, v_img, room, 0, total, qt_txt[...], d_txt_t.astype(BF16))
    score_grads(
        room, 0, total, lse_txt[...], delta,
        lambda at: lane >= thr[at.start // (total // blocks)],
    )
    probs, slopes = room[2:]
    dk[...] = dot(slopes[...], q_txt[...])
    dv[...] = dot(probs[...], d_txt[...])


def backward_kernel(
    share, copies, extra, place, thr, grad_pre, k_txt, kt_txt, v_txt, lse, u, proj, gram, z, gain, starts, steps, grad_out_t, *refs,
):
    blocks, length, _ = grad_pre.shape
    (k_img_far, v_img_far, qt_far, kt_far, q_img_far, mix_t_far, dk_far, dv_far, pre_down_far, act_t_far, patch_t_far,
     wq_far, wk_far, wv_far, wo_far, w_up_far, w_down_far,
     keep, send,
     pieces, dq, dk, dv, cross_sum, small_sum, scores, pulls, probs, slopes,
     keys, values, qt, kt, q_img, mix_t, dk_text, dv_text, pre_down, act_t, patch_t, w_cols, w_rows, w_up,
     sems) = refs
    text_total = k_txt.shape[0]
    width = w_up.shape[0]
    cols = pl.ds(pl.multiple_of(place[0] * HD, HD), HD)
    moves = fetch(
        [(k_img_far, keys.at[text_total:, :]), (v_img_far, values.at[text_total:, :]), (qt_far, qt),
         (kt_far, kt.at[:, text_total:]), (q_img_far, q_img), (mix_t_far, mix_t), (dk_far, dk_text), (dv_far, dv_text),
         (pre_down_far, pre_down), (act_t_far, act_t), (patch_t_far, patch_t),
         (wq_far.at[:, cols], w_cols.at[:, :HD]), (wk_far.at[:, cols], w_cols.at[:, HD : 2 * HD]),
         (wv_far.at[:, cols], w_cols.at[:, 2 * HD :]), (wo_far.at[cols, :], w_rows.at[:HD, :]),
         (w_up_far, w_up), (w_down_far, w_rows.at[HD:, :])],
        sems,
    )
    cross_sum[...] = jnp.zeros_like(cross_sum)
    small_sum[...] = jnp.zeros_like(small_sum)
    keys[:text_total, :] = k_txt[...]
    values[:text_total, :] = v_txt[...]
    kt[:, :text_total] = kt_txt[...]
    for move in moves[:6]:
        move.wait()

    def begin(i):
        grad = grad_pre[i]
        cross_sum[...] += dot(mix_t[i], grad)
        d_t = dot_nt(u[...], grad).astype(BF16)
        delta = jnp.sum(d_t.astype(F32) * mix_t[i].astype(F32), axis=0, keepdims=True)
        room = [ref.at[i % 2] for ref in (scores, pulls, probs, slopes)]
        score_products(keys, values, room, 0, text_total + (i + 1) * length, qt[i], d_t)
        return room, delta, dot_nt(grad, u[...]).astype(BF16)

    def add(total, before, values):
        if before:
            total[:before, :] += values[:before]
        total[before : before + length, :] = values[before:]

    ahead = begin(0)
    for i in range(blocks):
        room, delta, d_out = ahead
        if i + 1 < blocks:
            ahead = begin(i + 1)
        before = i * length
        end = text_total + before + length
        score_grads(
            room, 0, end, lse[i], delta,
            lambda at: iota((STRIP, length), 0) + at.start < thr[i] if at.start < text_total else None,
        )
        add(dv, before, dot(room[2][text_total:end, :length], d_out))
        add(dk, before, dot(room[3][text_total:end, :length], q_img[i]))
        dq[i] = dot(kt[:, :end], room[3][:end, :length]).T
    for move in moves[6:11]:
        move.wait()
    taps = patch_t.shape[1]

    def block(b, query):
        cos, sin = angles(*start_row(starts, thr, b, extra), steps)
        own_rows = pl.ds(pl.multiple_of(b * length, length), length)

        def back(values):
            return values * cos - pltpu.roll(values, HD // 2, 1) * sin

        before = pre_down[b]
        act = silu(before).astype(BF16)
        act_wide = act.astype(F32)
        image = dot(act, gram[...])
        square = jnp.sum(image * act_wide, axis=-1, keepdims=True)
        inv = lax.rsqrt(square * (1.0 / width) + EPSILON)
        heads = jnp.concatenate(
            [back(query) * (inv * SCALE), back(dk[own_rows, :] + dk_text[own_rows, :]) * (inv * LN2),
             (dv[own_rows, :] + dv_text[own_rows, :]) * inv], axis=1
        ).astype(BF16)
        lift = dot_nt(heads, proj[...])
        crow = inv * inv * (jnp.sum(act_wide * lift, axis=-1, keepdims=True) * (1.0 / width))
        grad = grad_pre[b]
        d_act = (lift - crow * image) * copies + dot_nt(grad, z[...]) * share
        slope = (d_act * silu_slope(before)).astype(BF16)
        flipped = act_t[b]
        return (
            dot(patch_t[b], slope),
            dot(flipped, heads),
            dot(flipped, (act_wide * crow).astype(BF16)),
            dot(flipped, grad),
        )

    def step(n, carry):
        for b in (n, blocks // 4 + n, blocks // 2 + n, 3 * (blocks // 4) + n):
            conv, *more = block(b, dq[b])
            small_sum[:taps, :] += conv
            carry = tuple(a + m for a, m in zip(carry, more))
        return carry

    rank = act_t.shape[1]
    spread, pull, inner = lax.fori_loop(
        0, blocks // 4, step,
        (jnp.zeros((rank, 3 * HD), F32), jnp.zeros((rank, rank), F32), jnp.zeros((rank, grad_pre.shape[2]), F32)),
    )
    for move in moves[11:]:
        move.wait()
    spread = (spread * copies).astype(BF16)
    pull = (pull * copies).astype(BF16)
    cross = (cross_sum[...] * copies).T.astype(BF16)
    inner_t = (inner * share).T.astype(BF16)
    inner = (inner * share).astype(BF16)
    small_sum[taps : taps + grad_out_t.shape[0], :] = grad_out_t[...]
    _, groups, pairs, rows, _ = pieces.shape
    own = width // (2 * groups * pairs)
    few = rows - 2 * own
    both_t = jnp.concatenate([cross, inner_t], axis=1)
    for at in range(0, width, 2 * HD):
        cols = slice(at, at + 2 * HD)
        scale = whole_row(gain[at // HD : at // HD + 2, :])
        down = dot_nt(spread, w_cols[cols, :]) * scale
        down = (down - dot(pull, w_rows[HD:, cols]) + dot_nt(inner, w_up[cols, :])).astype(BF16)
        up = dot(both_t, w_rows[:, cols]).T.astype(BF16)
        for part in range(0, 2 * HD, own):
            number = (at + part) // own
            tile = part // HD * HD
            put_piece(place, pieces, number, slice(0, own), up[part : part + own])
            put_piece(place, pieces, number, slice(own, 2 * own), down[part - tile : part - tile + own, tile : tile + HD])
    for number in range(2 * groups * pairs):
        put_piece(place, pieces, number, slice(2 * own, rows), small_sum[number * few : (number + 1) * few, :].astype(BF16))
    for move in fetch([(pieces.at[0], keep), (pieces.at[1], send)], sems):
        move.wait()


def shards(
    text_tokens,
    latent,
    image_offset,
    norm_gain,
    w_query,
    w_key,
    w_value,
    w_out,
    w_down_conv,
    w_down_proj,
    w_up_proj,
    w_up_out,
    pred_grad,
    text_grad,
):
    axes = ("sy", "sx")
    text_local = text_tokens[0]
    text_rows, width = text_local.shape
    lat_chan = w_up_out.shape[1]
    up_chan = w_up_proj.shape[1]
    down_chan = w_down_conv.shape[1]
    taps = w_down_conv.shape[0]
    tile_rows = latent.shape[1]
    tile_cols = latent.shape[2] // lat_chan
    row_groups = lax.axis_size("sx")
    blocks = lax.axis_size("sy")
    devices = row_groups * blocks
    high = tile_rows * row_groups
    length = high * tile_cols
    text_block = text_rows * row_groups
    text_total = text_block * blocks
    total = length * blocks
    block_len = length + text_block
    heads_here = w_query.shape[1] // HD
    repeat = blocks // heads_here
    assert heads_here * repeat == blocks and blocks % 2 == 0
    own = lax.axis_index("sy")
    share = 1.0 / devices
    copies = 1.0 / repeat

    device = own * row_groups + lax.axis_index("sx").astype(jnp.int32)
    group = lax.axis_index("sx").astype(jnp.int32)
    own = own.astype(jnp.int32)
    head = jnp.stack([own // repeat, device, group, own // 2, own % 2, own])

    def spread_over(values, axis, count):
        return lax.all_to_all(jnp.broadcast_to(values[None], (count,) + values.shape), axis, 0, 0)

    tag = jnp.broadcast_to(image_offset.astype(BF16)[:, None], (tile_rows, HD))
    packed = jnp.concatenate([latent[0], tag], axis=1)
    hop = lambda values, axis, by: lax.ppermute(
        values, axis, [(i, i ^ by) for i in range(row_groups if axis == "sx" else blocks)]
    )
    trio = jnp.stack([text_local, hop(text_local, "sy", 1), text_grad[0]])
    packed, trio = lax.optimization_barrier((packed, trio))
    text_parts = [trio] + [hop(trio, "sx", k) for k in range(1, row_groups)]
    side = spread_over(packed, axes, devices)

    gain = norm_gain.reshape(width // HD, HD)
    small = jax.ShapeDtypeStruct
    square = small((down_chan, down_chan), BF16)
    pairs = blocks // 2
    vmem = pltpu.VMEM
    dma = lambda count: pltpu.SemaphoreType.DMA((count,))
    bf = lambda *shape: small(shape, BF16)
    both = 2 * text_block
    chunks = 8
    wide = heads_here * HD // 2
    proj, proj_t, mapped, u, gram, z, conv_t, *text_here = call(
        lambda *refs: front_kernel(row_groups, repeat, *refs), head,
        [(gain, None), (w_down_conv, None)]
        + [(a, pl.ANY) for a in (w_down_proj, w_query, w_key, w_value, w_up_proj, w_out)]
        + [(a, None) for a in text_parts],
        [bf(down_chan, 3 * HD), bf(3 * HD, down_chan), bf(down_chan, 5 * HD), bf(HD, up_chan),
         bf(down_chan, down_chan), bf(down_chan, up_chan), bf(down_chan, taps)] + [bf(both, 3 * HD)] * pairs,
        [vmem((down_chan, width), BF16)] + [vmem((width, HD), BF16)] * 3
        + [vmem((width, up_chan), BF16), vmem((HD, width), BF16),
           vmem((chunks, 3, width // chunks, wide), BF16), vmem((both, width), BF16), vmem((3, both, wide), F32),
           dma(6 + 3 * chunks)],
        flops=4_000_000_000 + 6 * both * width * wide,
    )
    texts = [
        lax.ppermute(values, "sy", [(2 * z + c, c * pairs + (z ^ k)) for z in range(pairs) for c in range(2)])
        for k, values in enumerate(text_here)
    ]

    side = side.reshape(blocks, row_groups, tile_rows, -1)
    lat_t = side[..., : tile_cols * lat_chan].reshape(total, lat_chan).T.astype(F32)
    offsets = side[:, 0, 0, tile_cols * lat_chan].astype(jnp.int32)
    block_ids = jnp.arange(blocks, dtype=jnp.int32)
    thr = block_ids * text_block + offsets
    ids = np.arange(length, dtype=np.int32)
    cell = np.stack([ids // tile_cols, ids % tile_cols])
    at = np.arange(blocks)[:, None]
    steps = rope_tables(ids)
    steps_t = np.ascontiguousarray(np.swapaxes(steps, 1, 2)[:, HD // 2 :])
    starts = rope_tables((at * block_len + np.arange(text_block + 1)).reshape(-1))
    near = (at * block_len + np.arange(text_block)).reshape(-1)
    near, far = rope_tables(near), rope_tables(near + length)

    chunk = lambda kind, rows=length, cols=HD: small((blocks, rows, cols), kind)
    text_kind = small((text_total, HD), BF16)
    text_flip = small((HD, text_total), BF16)
    side_len = max(length, text_total)
    seq = text_total + total
    pre_down, act_t, patch_t, q_img, qt, k_img, kt, v_img, vt = image_rows(
        (high, tile_cols, width, 1), thr, lat_t, cell, conv_t, proj_t, mapped, gram, starts, steps, steps_t,
        text_here[:1]
    )
    part, q_txt, qt_txt, k_txt, kt_txt, v_txt, mix_t, mix_txt_t, mix_txt, lse, lse_txt = call(
        attend_kernel, head,
        [(thr, pltpu.SMEM), (near, None), (far, None), (u, None), (qt, pl.ANY), (k_img.reshape(total, HD), pl.ANY),
         (vt, pl.ANY)]
        + [(a, None) for a in texts],
        [chunk(BF16, length, up_chan), text_kind, text_flip, text_kind, text_flip, text_kind, chunk(BF16, HD, length),
         text_flip, text_kind, small((blocks, 1, length), F32), small((1, text_total), F32)],
        [vmem((2, seq, side_len), F32), vmem((2, seq, side_len), BF16), vmem((text_total, 3 * HD), BF16),
         vmem(qt.shape, BF16), vmem((seq, HD), BF16), vmem((HD + 16, seq), BF16), dma(3)],
        flops=6_000_000_000,
    )

    own_rows = tile_rows * tile_cols
    part = part if repeat == 1 else part * jnp.asarray(copies, BF16)
    parts = lax.all_to_all(part.reshape(devices, own_rows, up_chan), axes, 0, 0)
    wo_room = [vmem((4, heads_here * HD // 4, width), BF16)]
    text_back = call(
        lambda *refs: text_grad_kernel(row_groups, repeat, *refs), head,
        [(w_out, pl.ANY), (mix_txt, None)] + [(a, None) for a in text_parts],
        [bf(pairs, text_block, 2 * HD)] * 2,
        wo_room + [vmem((heads_here * HD, text_block), F32), dma(4)],
        flops=2 * text_block * width * heads_here * HD,
        after=[part],
    )
    keep, send = text_back
    text_back = plain(merge_kernel, [keep, hop(send, "sy", 1)], [bf(2 * text_block, 2 * HD)] * pairs)
    text_back = [text_back[0]] + [hop(text_back[m], "sy", 2 * m) for m in range(1, pairs)]
    grad_copies, prediction, grad_out_t = call(
        up_kernel, head,
        [(parts, None), (pre_down.reshape(devices, own_rows, down_chan), None), (z, None), (w_up_out, None),
         (pred_grad[0].reshape(own_rows, lat_chan), None)],
        [small((devices, own_rows, up_chan), BF16), small((own_rows, lat_chan), BF16), small((lat_chan, up_chan), F32)],
        flops=2_000_000_000,
        after=text_back[1:],
        room=SMALL_BYTES,
    )
    grad_pre = lax.all_to_all(grad_copies, axes, 0, 0).reshape(blocks, length, up_chan)

    own_part = width // devices
    few = -(-(taps + lat_chan) // (16 * devices)) * 16
    lump = lambda rows: small((pairs, rows, HD), BF16)
    flat = lambda rows: small((rows, HD), BF16)
    vmem = pltpu.VMEM
    def core_sum(keep, send, rows):
        return plain(add_core_kernel, [keep, hop(send, "sy", 1)], [lump(rows)] * row_groups)

    def sx_sum(sums, rows, after=()):
        sums = [sums[0]] + [hop(sums[k], "sx", k) for k in range(1, row_groups)]
        return plain(lambda *refs: add_sx_kernel(row_groups, *refs), sums, [flat(rows)] * pairs, after)

    def z_sum(sums, rows, after=()):
        sums = [sums[0]] + [hop(sums[m], "sy", 2 * m) for m in range(1, pairs)]
        return plain(add_kernel, sums, [flat(rows)], after)[0]

    def spread_z(mine):
        return jnp.stack([mine] + [hop(mine, "sy", 2 * m) for m in range(1, pairs)])

    def spread_sx(mine):
        near = [mine] + [hop(mine, "sx", k) for k in range(1, row_groups)]
        return near + [hop(values, "sy", 1) for values in near]

    mixed = call(
        lambda *refs: text_out_kernel(repeat, blocks, *refs), head,
        [(w_out, pl.ANY)] + [(a, None) for a in text_back],
        [bf(text_rows, width)] * row_groups,
        wo_room + [vmem((text_block, heads_here * HD), BF16), dma(4)],
        flops=2 * text_block * width * heads_here * HD,
        after=[grad_copies],
    )
    mixed = [mixed[0]] + [hop(mixed[k], "sx", k) for k in range(1, row_groups)]
    text_out = (text_local.astype(F32) + sum(m.astype(F32) for m in mixed)).astype(BF16)
    k_rows, v_rows = k_img.reshape(total, HD), v_img.reshape(total, HD)
    strip_room = lambda *lead: [vmem((*lead, side_len), F32)] * 2 + [vmem((*lead, side_len), BF16)] * 2
    dk, dv = call(
        text_backward_kernel, head,
        [(thr, pltpu.SMEM)] + [(a, None) for a in (k_rows, v_rows, q_txt, qt_txt, mix_txt_t, lse_txt, *text_back)],
        [small((total, HD), F32)] * 2,
        [vmem((text_total, HD), BF16)] + [vmem((total, text_total), kind) for kind in (F32, F32, BF16, BF16)],
        flops=2_000_000_000,
        after=mixed[:1] + [grad_copies],
    )
    rows = 2 * own_part + few
    near_arrays = (k_rows, v_rows, qt, kt, q_img, mix_t, dk, dv, pre_down, act_t, patch_t)
    far_arrays = near_arrays + (w_query, w_key, w_value, w_out, w_up_proj, w_down_proj)
    keep, send = call(
        lambda *refs: backward_kernel(share, copies, 1, *refs), head,
        [(thr, pltpu.SMEM)] + [(a, None) for a in (
            grad_pre, k_txt, kt_txt, v_txt, lse, u, proj, gram, z, gain, starts, steps, grad_out_t)]
        + [(a, pl.ANY) for a in far_arrays],
        [small((row_groups, pairs, rows, HD), BF16)] * 2,
        [vmem((2, row_groups, pairs, rows, HD), BF16), vmem((blocks, length, HD), F32), vmem((total, HD), F32),
         vmem((total, HD), F32), vmem((HD, up_chan), F32), vmem((devices * few, HD), F32)]
        + strip_room(2, seq)
        + [vmem((seq, HD), BF16)] * 2 + [vmem(qt.shape, BF16), vmem((HD, seq), BF16)]
        + [vmem(a.shape, a.dtype) for a in (q_img, mix_t, dk, dv, pre_down, act_t, patch_t)]
        + [vmem((width, 3 * HD), BF16), vmem((HD + down_chan, width), BF16), vmem(w_up_proj.shape, BF16),
           pltpu.SemaphoreType.DMA((len(far_arrays),))],
        flops=30_000_000_000,
        after=mixed[1:],
    )
    mine = spread_z(z_sum(sx_sum(core_sum(keep, send, rows), rows), rows))
    grad_conv, grad_down, grad_up, grad_out_t = call(
        lambda *refs: unpack_kernel(row_groups, pairs, own_part, *refs), head,
        [(a, None) for a in spread_sx(mine)],
        [small((taps, down_chan), F32), small((down_chan, width), F32), small((width, up_chan), F32),
         small((lat_chan, up_chan), F32)],
        [vmem((devices * few, HD), F32)],
        room=2 * SMALL_BYTES,
    )
    return (
        prediction.reshape(1, tile_rows, tile_cols * lat_chan),
        text_out[None],
        grad_conv,
        grad_down,
        grad_up,
        grad_out_t.T,
    )


def solution(mesh):
    placed = (
        P("sy", "sx", None),
        P("sy", "sx", None),
        P("sy"),
        P(),
        P(None, "sx"),
        P(None, "sx"),
        P(None, "sx"),
        P("sx", None),
        P(),
        P(),
        P(),
        P(),
        P("sy", "sx", None),
        P("sy", "sx", None),
    )
    return jax.shard_map(
        shards,
        mesh=mesh,
        in_specs=placed,
        out_specs=(P("sy", "sx", None), P("sy", "sx", None), P(), P(), P(), P()),
        check_vma=False,
    )
```

```python
import math

import jax
import jax.numpy as jnp
import numpy as np
from jax import lax
from jax.experimental import pallas as pl
from jax.experimental.pallas import tpu as pltpu
from jax.sharding import PartitionSpec as P

HD = 128
EPSILON = 1e-05
NEG_SCORE = -1e30
ROPE_BASE = 500000.0
SCALE = HD ** (-0.5)
LOG2E = math.log2(math.e)
LN2 = math.log(2.0)
F32 = jnp.float32
BF16 = jnp.bfloat16
MIB = 1024 * 1024
VMEM_BYTES = 56 * MIB
SMALL_BYTES = 16 * MIB


def dot(left, right):
    return jnp.dot(left, right, preferred_element_type=F32)


def dot_nt(left, right):
    return lax.dot_general(left, right, (((1,), (1,)), ((), ())), preferred_element_type=F32)


def silu_slope(values):
    sigma = jax.nn.sigmoid(values)
    return sigma * (1.0 + values * (1.0 - sigma))


def silu(values):
    return values * jax.nn.sigmoid(values)


def iota(shape, dim):
    return lax.broadcasted_iota(jnp.int32, shape, dim)


def flip(values):
    return values.astype(F32).T.astype(BF16)


def call(kernel, place, inputs, outs, scratch=(), flops=0, after=(), room=VMEM_BYTES, far=False):
    inputs = [(place, pltpu.SMEM)] + list(inputs)
    count = len(inputs)
    skip = count + len(after)
    moved = sum(math.prod(a.shape) * a.dtype.itemsize for a in list(outs) + [a for a, space in inputs if space is None])
    return pl.pallas_call(
        lambda *refs: kernel(*refs[:count], *refs[skip:]),
        out_shape=outs,
        in_specs=[pl.BlockSpec(memory_space=pltpu.VMEM if space is None else space) for _, space in inputs]
        + [pl.BlockSpec(memory_space=pl.ANY) for _ in after],
        out_specs=[pl.BlockSpec(memory_space=pl.ANY if far else pltpu.VMEM) for _ in outs],
        scratch_shapes=list(scratch),
        compiler_params=pltpu.CompilerParams(vmem_limit_bytes=room),
        cost_estimate=pl.CostEstimate(flops=flops, bytes_accessed=moved, transcendentals=0),
    )(*[a for a, _ in inputs], *after)


def fetch(moves, sems):
    moves = [pltpu.make_async_copy(far, near, sems.at[n]) for n, (far, near) in enumerate(moves)]
    for move in moves:
        move.start()
    return moves


def whole_row(gain):
    return jnp.concatenate([gain[r : r + 1, :].astype(F32) for r in range(gain.shape[0])], axis=1)


def pick(rows, total, spot):
    return (iota((total, rows), 0) == iota((total, rows), 1) + spot).astype(BF16)


def gathered(parts, group):
    rows = parts[0].shape[0]
    total = rows * len(parts)
    return sum(dot(pick(rows, total, (group ^ k) * rows), part[...]) for k, part in enumerate(parts))


def front_kernel(count, repeat, place, gain, w_conv, w_down_far, wq_far, wk_far, wv_far, w_up_far, wo_far, *refs):
    parts = refs[:count]
    proj, proj_t, mapped, u, gram, z, conv_t = refs[count : count + 7]
    outs = refs[count + 7 : -10]
    w_down, wq, wk, wv, w_up, wo, weights, normed, sums, sems = refs[-10:]
    chunks, _, deep, wide = weights.shape
    cols = pl.ds(pl.multiple_of(place[0] * HD, HD), HD)
    half = pl.ds(pl.multiple_of(place[4] * wide, wide), wide)
    moves = fetch(
        [(w_down_far, w_down), (wq_far.at[:, cols], wq), (wk_far.at[:, cols], wk), (wv_far.at[:, cols], wv),
         (w_up_far, w_up), (wo_far.at[cols, :], wo)]
        + [(far.at[c * deep : (c + 1) * deep, half], weights.at[c, n])
           for c in range(chunks) for n, far in enumerate((wq_far, wk_far, wv_far))],
        sems,
    )
    conv_t[...] = flip(w_conv[...])
    rows = normed.shape[0] // 2
    row = whole_row(gain)
    for r in range(2):
        x = gathered([part.at[r] for part in parts], place[2])
        inverse = lax.rsqrt(jnp.mean(x * x, axis=-1, keepdims=True) + EPSILON)
        normed[r * rows : (r + 1) * rows, :] = (x * inverse * row).astype(BF16)
    moves[0].wait()
    down = w_down[...]
    scaled = (down.astype(F32) * row).astype(BF16)
    gram[...] = dot_nt(down, down).astype(BF16)
    for n, w in enumerate((wq, wk, wv)):
        cols = slice(n * HD, (n + 1) * HD)
        moves[1 + n].wait()
        total = dot(scaled, w[...])
        proj[:, cols] = total.astype(BF16)
        proj_t[cols, :] = total.T.astype(BF16)
        mapped[:, cols] = total.astype(BF16)
        if n < 2:
            mapped[:, (3 + n) * HD : (4 + n) * HD] = pltpu.roll(total, HD // 2, 1).astype(BF16)
    moves[4].wait()
    z[...] = dot(down, w_up[...]).astype(BF16)
    moves[5].wait()
    u[...] = dot(wo[...], w_up[...]).astype(BF16)
    for c in range(chunks):
        here = normed[:, c * deep : (c + 1) * deep]
        for n in range(3):
            moves[6 + 3 * c + n].wait()
            term = dot(here, weights[c, n])
            sums[n] = term if c == 0 else sums[n] + term
    for k, out in enumerate(outs):
        head = pl.ds(pl.multiple_of((place[3] ^ k) // repeat * HD, HD), HD)
        for n in range(3):
            out[:, n * HD : (n + 1) * HD] = sums[n, :, head].astype(BF16)


def text_grad_kernel(count, repeat, place, wo_far, mix, *refs):
    parts = refs[:count]
    keep, send, wo, total, sems = refs[count:]
    groups, deep, _ = wo.shape
    moves = fetch([(wo_far.at[g * deep : (g + 1) * deep, :], wo.at[g]) for g in range(groups)], sems)
    grad_t = gathered([part.at[2] for part in parts], place[2]).T.astype(BF16)
    for g in range(groups):
        moves[g].wait()
        total[g * deep : (g + 1) * deep, :] = dot(wo[g], grad_t)
    pairs, rows, _ = keep.shape
    for flip_core, out in enumerate((keep, send)):
        for m in range(pairs):
            peer = (place[3] ^ m) * 2 + (place[4] ^ flip_core)
            out[m, :, :HD] = total[pl.ds(pl.multiple_of(peer // repeat * HD, HD), HD), :].T.astype(BF16)
            out[m, :, HD:] = mix[pl.ds(pl.multiple_of(peer * rows, rows), rows), :]


def merge_kernel(keep, received, *outs):
    rows = keep.shape[1]
    for m, out in enumerate(outs):
        out[:rows, :] = keep[m]
        out[rows:, :] = received[m]


def by_peer(backs, rows):
    return [backs[k // 2].at[k % 2 * rows : (k % 2 + 1) * rows, :] for k in range(2 * len(backs))]


def text_out_kernel(repeat, peers, place, wo_far, *refs):
    outs = refs[peers // 2 : -3]
    wo, mixed, sems = refs[-3:]
    mixes = by_peer(refs[: peers // 2], mixed.shape[0])
    groups, deep, width = wo.shape
    moves = fetch([(wo_far.at[g * deep : (g + 1) * deep, :], wo.at[g]) for g in range(groups)], sems)
    for k, mix in enumerate(mixes):
        peer = place[5] ^ k

        @pl.when(peer % repeat == 0)
        def _():
            mixed[:, pl.ds(pl.multiple_of(peer // repeat * HD, HD), HD)] = mix[:, HD:]

    total = 0.0
    for g in range(groups):
        moves[g].wait()
        total = total + dot(mixed[:, g * deep : (g + 1) * deep], wo[g])
    whole = total.astype(BF16)
    for k, out in enumerate(outs):
        rows = out.shape[0]
        out[...] = dot(pick(rows, whole.shape[0], (place[2] ^ k) * rows).astype(F32).T.astype(BF16), whole).astype(BF16)


def turned(values, cos, sin):
    return values * cos + pltpu.roll(values, HD // 2, 1) * sin


def rope_tables(positions):
    half = HD // 2
    freq = np.exp(-(2.0 * np.arange(half) / HD) * math.log(ROPE_BASE)).astype(np.float32)
    angle = np.asarray(positions, np.float64)[:, None] * np.concatenate([freq, freq])[None].astype(np.float64)
    sign = np.where(np.arange(HD) < half, -1.0, 1.0)[None]
    return np.stack([np.cos(angle), np.sin(angle) * sign]).astype(np.float32)


def angles(cos_start, sin_start, steps):
    return cos_start * steps[0] - sin_start * steps[1], sin_start * steps[0] + cos_start * steps[1]


def start_row(starts, thr, b, extra):
    row = pl.ds(thr[b] + b * extra, 1)
    return starts[0, row, :], starts[1, row, :]


def image_kernel(high, wide, width, extra, thr, lat_all, cell, conv_t, proj_t, mapped, gram, starts, steps, steps_t, *refs):
    pre_down, act_t, patch_t, q_img, qt, k_img, kt, v_img, vt = refs[-9:]
    images, length, _ = pre_down.shape
    for n in range(images):
        number = pl.program_id(0) * images + n
        lanes = slice(n * length, (n + 1) * length)
        lat = lat_all[:, n * length : (n + 1) * length]
        chan = lat.shape[0]
        row = cell[0:1, :]
        col = cell[1:2, :]
        for r in range(3):
            for c in range(3):
                tap = r * 3 + c
                step = (r - 1) * wide + (c - 1)
                moved = pltpu.roll(lat, -step % lat.shape[1], 1) if step else lat
                keep = (row + (r - 1) >= 0) & (row + (r - 1) < high)
                keep &= (col + (c - 1) >= 0) & (col + (c - 1) < wide)
                patch_t[n, tap * chan : (tap + 1) * chan, :] = jnp.where(keep, moved, 0.0).astype(BF16)
        cos_start, sin_start = start_row(starts, thr, number, extra)
        before_t = dot(conv_t[...], patch_t[n])
        flat_t = silu(before_t).astype(BF16)
        act_t[n] = flat_t
        square = jnp.sum(dot(gram[...], flat_t) * flat_t.astype(F32), axis=0, keepdims=True)
        inv = lax.rsqrt(square * (1.0 / width) + EPSILON)
        heads_t = dot(proj_t[...], flat_t) * inv
        half = HD // 2
        column = lambda values: jnp.broadcast_to(values, (8, HD)).T[half:, :1]
        cos, sin = angles(column(cos_start), column(sin_start), steps_t)
        for at, out, scale in ((0, qt.at[n], SCALE * LOG2E), (HD, kt.at[:, lanes], 1.0)):
            first = heads_t[at : at + half]
            second = heads_t[at + half : at + HD]
            out[:half, :] = ((first * cos - second * sin) * scale).astype(BF16)
            out[half:, :] = ((second * cos + first * sin) * scale).astype(BF16)
        vt[:, lanes] = heads_t[2 * HD :].astype(BF16)
        before = before_t.T
        pre_down[n] = before
        act = silu(before).astype(BF16)
        square = jnp.sum(dot(act, gram[...]) * act.astype(F32), axis=-1, keepdims=True)
        inv = lax.rsqrt(square * (1.0 / width) + EPSILON)
        heads = dot(act, mapped[...])
        cos, sin = angles(cos_start, sin_start, steps)
        cos = cos * inv
        sin = sin * inv
        query = heads[:, :HD] * cos + heads[:, 3 * HD : 4 * HD] * sin
        q_img[n] = (query * (SCALE * LOG2E)).astype(BF16)
        k_img[n] = (heads[:, HD : 2 * HD] * cos + heads[:, 4 * HD :] * sin).astype(BF16)
        v_img[n] = (heads[:, 2 * HD : 3 * HD] * inv).astype(BF16)


def image_rows(sizes, thr, lat_t, cell, conv_t, proj_t, mapped, gram, starts, steps, steps_t, after):
    blocks = thr.shape[0]
    length = steps.shape[1]
    chan = lat_t.shape[0]
    down_chan, taps = conv_t.shape
    whole = lambda a: pl.BlockSpec(a.shape, lambda b: (0,) * len(a.shape))
    outs = [(length, down_chan, F32), (down_chan, length, BF16), (taps, length, BF16), (length, HD, BF16),
            (HD, length, BF16), (length, HD, BF16), None, (length, HD, BF16), None]
    per = math.gcd(blocks, 4)
    flat = pl.BlockSpec((HD, per * length), lambda b: (0, b))
    return pl.pallas_call(
        lambda *refs: image_kernel(*sizes, *refs),
        out_shape=[jax.ShapeDtypeStruct((blocks, *o[:2]), o[2]) if o else jax.ShapeDtypeStruct((HD, blocks * length), BF16)
                   for o in outs],
        grid=(blocks // per,),
        in_specs=[pl.BlockSpec(memory_space=pltpu.SMEM), pl.BlockSpec((chan, per * length), lambda b: (0, b))]
        + [whole(a) for a in (cell, conv_t, proj_t, mapped, gram, starts, steps, steps_t)]
        + [pl.BlockSpec(memory_space=pl.ANY) for _ in after],
        out_specs=[pl.BlockSpec((per, *o[:2]), lambda b: (b, 0, 0)) if o else flat for o in outs],
        compiler_params=pltpu.CompilerParams(vmem_limit_bytes=VMEM_BYTES),
        cost_estimate=pl.CostEstimate(flops=8_000_000_000, bytes_accessed=8_000_000, transcendentals=0),
    )(thr, lat_t, cell, conv_t, proj_t, mapped, gram, starts, steps, steps_t, *after)


STRIP = 128


def strips(rows):
    return [slice(at, at + STRIP) for at in range(0, rows, STRIP)]


def attend_kernel(
    head, thr, near, far, u, qt_far, k_img_far, vt_far, *refs,
):
    texts = refs[:-18]
    (part, q_txt, qt_txt, k_txt, kt_txt, v_txt, mix_t, mix_txt_t, mix_txt, lse, lse_txt,
     scores, probs, text, qt, keys, vt, sems) = refs[-18:]
    blocks, length, _ = part.shape
    text_total = q_txt.shape[0]
    moves = fetch(
        [(k_img_far, keys.at[text_total:, :]), (qt_far, qt), (vt_far, vt.at[:HD, text_total:])], sems
    )
    row = iota((text_total, 1), 0)
    rows = text_total // blocks
    core = head[5] // len(texts)
    for k, values in enumerate(texts):
        pair = head[5] % len(texts) ^ k
        for r in range(2):
            spot = pl.ds(pl.multiple_of((2 * pair + (core ^ r)) * rows, rows), rows)
            text[spot, :] = values[r * rows : (r + 1) * rows, :]
    shifted = row >= sum(jnp.where(row // rows == b, thr[b], 0) for b in range(blocks))
    cos = jnp.where(shifted, far[0], near[0])
    sin = jnp.where(shifted, far[1], near[1])
    query = turned(text[:, :HD].astype(F32), cos, sin) * (SCALE * LOG2E)
    q_txt[...] = query.astype(BF16)
    qt_txt[...] = query.T.astype(BF16)
    key = turned(text[:, HD : 2 * HD].astype(F32), cos, sin)
    k_txt[...] = key.astype(BF16)
    keys[:text_total, :] = key.astype(BF16)
    kt_txt[...] = key.T.astype(BF16)
    v_txt[...] = text[:, 2 * HD :]
    vt[:HD, :text_total] = flip(text[:, 2 * HD :])
    vt[HD:, :] = jnp.ones((vt.shape[0] - HD, vt.shape[1]), BF16)
    for move in moves:
        move.wait()

    def begin(n):
        turned_query, count, _ = jobs[n]
        scores[n % 2, :count, : turned_query.shape[1]] = dot(keys[:count, :], turned_query)

    def softmax(n):
        turned_query, count, seen = jobs[n]
        wide = turned_query.shape[1]
        here = scores.at[n % 2]
        weights = probs.at[n % 2]
        fold = lambda values: values.reshape(STRIP // 8, 8, wide)
        top = None
        for at in strips(count):
            s = here[at, :wide]
            mask = seen(at)
            if mask is not None:
                s = jnp.where(mask, s, NEG_SCORE)
                here[at, :wide] = s
            peak = jnp.max(fold(s), axis=0)
            top = peak if top is None else jnp.maximum(top, peak)
        top = jnp.max(top, axis=0, keepdims=True)
        for at in strips(count):
            p = jnp.exp2(here[at, :wide] - top)
            mask = seen(at)
            if mask is not None:
                p = jnp.where(mask, p, 0.0)
            weights[at, :wide] = p.astype(BF16)
        mixed = dot(vt[:, :count], weights[:count, :wide])
        whole = mixed[HD : HD + 1, :]
        return mixed[:HD] / whole, top + jnp.log2(whole)

    def image_seen(i):
        return lambda at: iota((STRIP, length), 0) + at.start < thr[i] if at.start < text_total else None

    lane = iota((1, text_total), 1)
    jobs = [(qt[i], text_total + (i + 1) * length, image_seen(i)) for i in range(blocks)]
    jobs.append((
        qt_txt[...], text_total + blocks * length,
        lambda at: iota((STRIP, text_total), 0) + at.start <= lane
        if at.start < text_total else lane >= thr[(at.start - text_total) // length],
    ))
    begin(0)
    for i in range(blocks):
        begin(i + 1)
        mixed, logs = softmax(i)
        lse[i] = logs
        mix_t[i] = mixed.astype(BF16)
        part[i] = dot(mixed.T.astype(BF16), u[...]).astype(part.dtype)
    mixed, logs = softmax(blocks)
    lse_txt[...] = logs
    mix_txt_t[...] = mixed.astype(BF16)
    mix_txt[...] = mixed.T.astype(BF16)


def up_kernel(head, parts, pre_down, z, w_up_out, preds, grad_copies, prediction, grad_out_t):
    act = silu(pre_down[head[1]]).astype(BF16)
    pre_up = dot(act, z[...])
    for p in range(parts.shape[0]):
        pre_up = pre_up + parts[p].astype(F32)
    up_act = silu(pre_up).astype(BF16)
    grad = (dot_nt(preds[...], w_up_out[...]) * silu_slope(pre_up)).astype(BF16)
    for p in range(parts.shape[0]):
        grad_copies[p] = grad
    prediction[...] = dot(up_act, w_up_out[...]).astype(BF16)
    grad_out_t[...] = dot(flip(preds[...]), up_act)


def piece_spot(place, groups, pairs, number):
    group = number // (2 * pairs) ^ place[2]
    pair = number // 2 % pairs ^ place[3]
    return group, pair, number % 2 ^ place[4]


def put_piece(place, pieces, number, rows, values):
    _, groups, pairs, _, _ = pieces.shape
    group, pair, core = piece_spot(place, groups, pairs, number)
    pieces[core, group, pair, rows, :] = values


def add_core_kernel(keep, received, *outs):
    for k, out in enumerate(outs):
        out[...] = (keep[k].astype(F32) + received[k].astype(F32)).astype(BF16)


def add_sx_kernel(count, *refs):
    for m, out in enumerate(refs[count:]):
        out[...] = sum(r[m].astype(F32) for r in refs[:count]).astype(BF16)


def add_kernel(*refs):
    refs[-1][...] = sum(r[...].astype(F32) for r in refs[:-1]).astype(BF16)


def unpack_kernel(groups, pairs, own, place, *refs):
    count = 2 * groups
    grad_conv, grad_down, grad_up, grad_out_t, rest = refs[count:]
    few = refs[0].shape[1] - 2 * own
    per = HD // own
    for n, part in enumerate(refs[:count]):
        for m in range(pairs):
            number = ((place[2] ^ n % groups) * pairs + (place[3] ^ m)) * 2 + (place[4] ^ n // groups)
            grad_up[pl.ds(pl.multiple_of(number * own, own), own), :] = part[m, :own, :].astype(F32)
            cols = pl.ds(pl.multiple_of(number // per * HD, HD), HD)
            rows = pl.ds(pl.multiple_of(number % per * own, own), own)
            grad_down[rows, cols] = part[m, own : 2 * own, :].astype(F32)
            rest[pl.ds(pl.multiple_of(number * few, few), few), :] = part[m, 2 * own :, :].astype(F32)
    taps = grad_conv.shape[0]
    grad_conv[...] = rest[:taps, :]
    grad_out_t[...] = rest[taps : taps + grad_out_t.shape[0], :]


def plain(kernel, inputs, outs, after=()):
    whole = lambda a: pl.BlockSpec(a.shape, lambda: (0,) * len(a.shape))
    moved = sum(math.prod(a.shape) * a.dtype.itemsize for a in list(inputs) + list(outs))
    return pl.pallas_call(
        lambda *refs: kernel(*refs[: len(inputs)], *refs[len(inputs) + len(after) :]),
        out_shape=outs,
        in_specs=[whole(a) for a in inputs] + [pl.BlockSpec(memory_space=pl.ANY) for _ in after],
        out_specs=[whole(a) for a in outs],
        compiler_params=pltpu.CompilerParams(vmem_limit_bytes=SMALL_BYTES),
        cost_estimate=pl.CostEstimate(flops=0, bytes_accessed=moved, transcendentals=0),
    )(*inputs, *after)


def score_products(keys, values, room, first, last, turned_query, turned_grad):
    scores, pulls = room[:2]
    wide = turned_query.shape[1]
    scores[first:last, :wide] = dot(keys[first:last, :], turned_query)
    pulls[first:last, :wide] = dot(values[first:last, :], turned_grad)


def score_grads(room, first, last, logs, delta, seen):
    scores, pulls, probs, slopes = room
    wide = logs.shape[1]
    for at in strips(last)[first // STRIP :]:
        p = jnp.exp2(scores[at, :wide] - logs)
        mask = seen(at)
        if mask is not None:
            p = jnp.where(mask, p, 0.0)
        probs[at, :wide] = p.astype(BF16)
        slopes[at, :wide] = (p * (pulls[at, :wide] - delta)).astype(BF16)


def text_backward_kernel(place, thr, k_img, v_img, q_txt, qt_txt, mix_txt_t, lse_txt, *refs):
    dk, dv, d_txt, *room = refs[-7:]
    text_total = q_txt.shape[0]
    total = k_img.shape[0]
    blocks = thr.shape[0]
    rows = text_total // blocks
    for k, back in enumerate(by_peer(refs[:-7], rows)):
        d_txt[pl.ds(pl.multiple_of((place[5] ^ k) * rows, rows), rows), :] = back[:, :HD]
    d_txt_t = d_txt[...].astype(F32).T
    delta = jnp.sum(d_txt_t * mix_txt_t[...].astype(F32), axis=0, keepdims=True)
    lane = iota((1, text_total), 1)
    score_products(k_img, v_img, room, 0, total, qt_txt[...], d_txt_t.astype(BF16))
    score_grads(
        room, 0, total, lse_txt[...], delta,
        lambda at: lane >= thr[at.start // (total // blocks)],
    )
    probs, slopes = room[2:]
    dk[...] = dot(slopes[...], q_txt[...])
    dv[...] = dot(probs[...], d_txt[...])


def backward_kernel(
    share, copies, extra, place, thr, grad_pre, k_txt, kt_txt, v_txt, lse, u, proj, gram, z, gain, starts, steps, grad_out_t, *refs,
):
    blocks, length, _ = grad_pre.shape
    (k_img_far, v_img_far, qt_far, kt_far, q_img_far, mix_t_far, dk_far, dv_far, pre_down_far, act_t_far, patch_t_far,
     wq_far, wk_far, wv_far, wo_far, w_up_far, w_down_far,
     keep, send,
     pieces, dq, dk, dv, cross_sum, small_sum, scores, pulls, probs, slopes,
     keys, values, qt, kt, q_img, mix_t, dk_text, dv_text, pre_down, act_t, patch_t, w_cols, w_rows, w_up,
     sems) = refs
    text_total = k_txt.shape[0]
    width = w_up.shape[0]
    cols = pl.ds(pl.multiple_of(place[0] * HD, HD), HD)
    moves = fetch(
        [(k_img_far, keys.at[text_total:, :]), (v_img_far, values.at[text_total:, :]), (qt_far, qt),
         (kt_far, kt.at[:, text_total:]), (q_img_far, q_img), (mix_t_far, mix_t), (dk_far, dk_text), (dv_far, dv_text),
         (pre_down_far, pre_down), (act_t_far, act_t), (patch_t_far, patch_t),
         (wq_far.at[:, cols], w_cols.at[:, :HD]), (wk_far.at[:, cols], w_cols.at[:, HD : 2 * HD]),
         (wv_far.at[:, cols], w_cols.at[:, 2 * HD :]), (wo_far.at[cols, :], w_rows.at[:HD, :]),
         (w_up_far, w_up), (w_down_far, w_rows.at[HD:, :])],
        sems,
    )
    cross_sum[...] = jnp.zeros_like(cross_sum)
    small_sum[...] = jnp.zeros_like(small_sum)
    keys[:text_total, :] = k_txt[...]
    values[:text_total, :] = v_txt[...]
    kt[:, :text_total] = kt_txt[...]
    for move in moves[:6]:
        move.wait()

    def begin(i):
        grad = grad_pre[i]
        cross_sum[...] += dot(mix_t[i], grad)
        d_t = dot_nt(u[...], grad).astype(BF16)
        delta = jnp.sum(d_t.astype(F32) * mix_t[i].astype(F32), axis=0, keepdims=True)
        room = [ref.at[i % 2] for ref in (scores, pulls, probs, slopes)]
        score_products(keys, values, room, 0, text_total + (i + 1) * length, qt[i], d_t)
        return room, delta, dot_nt(grad, u[...]).astype(BF16)

    def add(total, before, values):
        if before:
            total[:before, :] += values[:before]
        total[before : before + length, :] = values[before:]

    ahead = begin(0)
    for i in range(blocks):
        room, delta, d_out = ahead
        if i + 1 < blocks:
            ahead = begin(i + 1)
        before = i * length
        end = text_total + before + length
        score_grads(
            room, 0, end, lse[i], delta,
            lambda at: iota((STRIP, length), 0) + at.start < thr[i] if at.start < text_total else None,
        )
        add(dv, before, dot(room[2][text_total:end, :length], d_out))
        add(dk, before, dot(room[3][text_total:end, :length], q_img[i]))
        dq[i] = dot(kt[:, :end], room[3][:end, :length]).T
    for move in moves[6:11]:
        move.wait()
    taps = patch_t.shape[1]

    def block(b, query):
        cos, sin = angles(*start_row(starts, thr, b, extra), steps)
        own_rows = slice(b * length, (b + 1) * length)

        def back(values):
            return values * cos - pltpu.roll(values, HD // 2, 1) * sin

        before = pre_down[b]
        act = silu(before).astype(BF16)
        act_wide = act.astype(F32)
        image = dot(act, gram[...])
        square = jnp.sum(image * act_wide, axis=-1, keepdims=True)
        inv = lax.rsqrt(square * (1.0 / width) + EPSILON)
        heads = jnp.concatenate(
            [back(query) * (inv * SCALE), back(dk[own_rows, :] + dk_text[own_rows, :]) * (inv * LN2),
             (dv[own_rows, :] + dv_text[own_rows, :]) * inv], axis=1
        ).astype(BF16)
        lift = dot_nt(heads, proj[...])
        crow = inv * inv * (jnp.sum(act_wide * lift, axis=-1, keepdims=True) * (1.0 / width))
        grad = grad_pre[b]
        d_act = (lift - crow * image) * copies + dot_nt(grad, z[...]) * share
        slope = (d_act * silu_slope(before)).astype(BF16)
        flipped = act_t[b]
        return (
            dot(patch_t[b], slope),
            dot(flipped, heads),
            dot(flipped, (act_wide * crow).astype(BF16)),
            dot(flipped, grad),
        )

    rank = act_t.shape[1]
    sums = [jnp.zeros((rank, 3 * HD), F32), jnp.zeros((rank, rank), F32), jnp.zeros((rank, grad_pre.shape[2]), F32)]
    for b in range(blocks):
        conv, *more = block(b, dq[b])
        small_sum[:taps, :] += conv
        sums = [a + m for a, m in zip(sums, more)]
    spread, pull, inner = sums
    for move in moves[11:]:
        move.wait()
    spread = (spread * copies).astype(BF16)
    pull = (pull * copies).astype(BF16)
    cross = (cross_sum[...] * copies).T.astype(BF16)
    inner_t = (inner * share).T.astype(BF16)
    inner = (inner * share).astype(BF16)
    small_sum[taps : taps + grad_out_t.shape[0], :] = grad_out_t[...]
    _, groups, pairs, rows, _ = pieces.shape
    own = width // (2 * groups * pairs)
    few = rows - 2 * own
    both_t = jnp.concatenate([cross, inner_t], axis=1)
    for at in range(0, width, 2 * HD):
        cols = slice(at, at + 2 * HD)
        scale = whole_row(gain[at // HD : at // HD + 2, :])
        down = dot_nt(spread, w_cols[cols, :]) * scale
        down = (down - dot(pull, w_rows[HD:, cols]) + dot_nt(inner, w_up[cols, :])).astype(BF16)
        up = dot(both_t, w_rows[:, cols]).T.astype(BF16)
        for part in range(0, 2 * HD, own):
            number = (at + part) // own
            tile = part // HD * HD
            put_piece(place, pieces, number, slice(0, own), up[part : part + own])
            put_piece(place, pieces, number, slice(own, 2 * own), down[part - tile : part - tile + own, tile : tile + HD])
    for number in range(2 * groups * pairs):
        put_piece(place, pieces, number, slice(2 * own, rows), small_sum[number * few : (number + 1) * few, :].astype(BF16))
    for move in fetch([(pieces.at[0], keep), (pieces.at[1], send)], sems):
        move.wait()


def shards(
    text_tokens,
    latent,
    image_offset,
    norm_gain,
    w_query,
    w_key,
    w_value,
    w_out,
    w_down_conv,
    w_down_proj,
    w_up_proj,
    w_up_out,
    pred_grad,
    text_grad,
):
    axes = ("sy", "sx")
    text_local = text_tokens[0]
    text_rows, width = text_local.shape
    lat_chan = w_up_out.shape[1]
    up_chan = w_up_proj.shape[1]
    down_chan = w_down_conv.shape[1]
    taps = w_down_conv.shape[0]
    tile_rows = latent.shape[1]
    tile_cols = latent.shape[2] // lat_chan
    row_groups = lax.axis_size("sx")
    blocks = lax.axis_size("sy")
    devices = row_groups * blocks
    high = tile_rows * row_groups
    length = high * tile_cols
    text_block = text_rows * row_groups
    text_total = text_block * blocks
    total = length * blocks
    block_len = length + text_block
    heads_here = w_query.shape[1] // HD
    repeat = blocks // heads_here
    assert heads_here * repeat == blocks and blocks % 2 == 0
    own = lax.axis_index("sy")
    share = 1.0 / devices
    copies = 1.0 / repeat

    device = own * row_groups + lax.axis_index("sx").astype(jnp.int32)
    group = lax.axis_index("sx").astype(jnp.int32)
    own = own.astype(jnp.int32)
    head = jnp.stack([own // repeat, device, group, own // 2, own % 2, own])

    def spread_over(values, axis, count):
        return lax.all_to_all(jnp.broadcast_to(values[None], (count,) + values.shape), axis, 0, 0)

    tag = jnp.broadcast_to(image_offset.astype(BF16)[:, None], (tile_rows, HD))
    packed = jnp.concatenate([latent[0], tag], axis=1)
    hop = lambda values, axis, by: lax.ppermute(
        values, axis, [(i, i ^ by) for i in range(row_groups if axis == "sx" else blocks)]
    )
    trio = jnp.stack([text_local, hop(text_local, "sy", 1), text_grad[0]])
    packed, trio = lax.optimization_barrier((packed, trio))
    text_parts = [trio] + [hop(trio, "sx", k) for k in range(1, row_groups)]
    side = spread_over(packed, axes, devices)

    gain = norm_gain.reshape(width // HD, HD)
    small = jax.ShapeDtypeStruct
    square = small((down_chan, down_chan), BF16)
    pairs = blocks // 2
    vmem = pltpu.VMEM
    dma = lambda count: pltpu.SemaphoreType.DMA((count,))
    bf = lambda *shape: small(shape, BF16)
    both = 2 * text_block
    chunks = 8
    wide = heads_here * HD // 2
    proj, proj_t, mapped, u, gram, z, conv_t, *text_here = call(
        lambda *refs: front_kernel(row_groups, repeat, *refs), head,
        [(gain, None), (w_down_conv, None)]
        + [(a, pl.ANY) for a in (w_down_proj, w_query, w_key, w_value, w_up_proj, w_out)]
        + [(a, None) for a in text_parts],
        [bf(down_chan, 3 * HD), bf(3 * HD, down_chan), bf(down_chan, 5 * HD), bf(HD, up_chan),
         bf(down_chan, down_chan), bf(down_chan, up_chan), bf(down_chan, taps)] + [bf(both, 3 * HD)] * pairs,
        [vmem((down_chan, width), BF16)] + [vmem((width, HD), BF16)] * 3
        + [vmem((width, up_chan), BF16), vmem((HD, width), BF16),
           vmem((chunks, 3, width // chunks, wide), BF16), vmem((both, width), BF16), vmem((3, both, wide), F32),
           dma(6 + 3 * chunks)],
        flops=4_000_000_000 + 6 * both * width * wide,
    )
    texts = [
        lax.ppermute(values, "sy", [(2 * z + c, c * pairs + (z ^ k)) for z in range(pairs) for c in range(2)])
        for k, values in enumerate(text_here)
    ]

    side = side.reshape(blocks, row_groups, tile_rows, -1)
    lat_t = side[..., : tile_cols * lat_chan].reshape(total, lat_chan).T.astype(F32)
    offsets = side[:, 0, 0, tile_cols * lat_chan].astype(jnp.int32)
    block_ids = jnp.arange(blocks, dtype=jnp.int32)
    thr = block_ids * text_block + offsets
    ids = np.arange(length, dtype=np.int32)
    cell = np.stack([ids // tile_cols, ids % tile_cols])
    at = np.arange(blocks)[:, None]
    steps = rope_tables(ids)
    steps_t = np.ascontiguousarray(np.swapaxes(steps, 1, 2)[:, HD // 2 :])
    starts = rope_tables((at * block_len + np.arange(text_block + 1)).reshape(-1))
    near = (at * block_len + np.arange(text_block)).reshape(-1)
    near, far = rope_tables(near), rope_tables(near + length)

    chunk = lambda kind, rows=length, cols=HD: small((blocks, rows, cols), kind)
    text_kind = small((text_total, HD), BF16)
    text_flip = small((HD, text_total), BF16)
    side_len = max(length, text_total)
    seq = text_total + total
    pre_down, act_t, patch_t, q_img, qt, k_img, kt, v_img, vt = image_rows(
        (high, tile_cols, width, 1), thr, lat_t, cell, conv_t, proj_t, mapped, gram, starts, steps, steps_t,
        text_here[:1]
    )
    part, q_txt, qt_txt, k_txt, kt_txt, v_txt, mix_t, mix_txt_t, mix_txt, lse, lse_txt = call(
        attend_kernel, head,
        [(thr, pltpu.SMEM), (near, None), (far, None), (u, None), (qt, pl.ANY), (k_img.reshape(total, HD), pl.ANY),
         (vt, pl.ANY)]
        + [(a, None) for a in texts],
        [chunk(BF16, length, up_chan), text_kind, text_flip, text_kind, text_flip, text_kind, chunk(BF16, HD, length),
         text_flip, text_kind, small((blocks, 1, length), F32), small((1, text_total), F32)],
        [vmem((2, seq, side_len), F32), vmem((2, seq, side_len), BF16), vmem((text_total, 3 * HD), BF16),
         vmem(qt.shape, BF16), vmem((seq, HD), BF16), vmem((HD + 16, seq), BF16), dma(3)],
        flops=6_000_000_000,
    )

    own_rows = tile_rows * tile_cols
    part = part if repeat == 1 else part * jnp.asarray(copies, BF16)
    parts = lax.all_to_all(part.reshape(devices, own_rows, up_chan), axes, 0, 0)
    wo_room = [vmem((4, heads_here * HD // 4, width), BF16)]
    text_back = call(
        lambda *refs: text_grad_kernel(row_groups, repeat, *refs), head,
        [(w_out, pl.ANY), (mix_txt, None)] + [(a, None) for a in text_parts],
        [bf(pairs, text_block, 2 * HD)] * 2,
        wo_room + [vmem((heads_here * HD, text_block), F32), dma(4)],
        flops=2 * text_block * width * heads_here * HD,
        after=[part],
    )
    keep, send = text_back
    text_back = plain(merge_kernel, [keep, hop(send, "sy", 1)], [bf(2 * text_block, 2 * HD)] * pairs)
    text_back = [text_back[0]] + [hop(text_back[m], "sy", 2 * m) for m in range(1, pairs)]
    grad_copies, prediction, grad_out_t = call(
        up_kernel, head,
        [(parts, None), (pre_down.reshape(devices, own_rows, down_chan), None), (z, None), (w_up_out, None),
         (pred_grad[0].reshape(own_rows, lat_chan), None)],
        [small((devices, own_rows, up_chan), BF16), small((own_rows, lat_chan), BF16), small((lat_chan, up_chan), F32)],
        flops=2_000_000_000,
        after=text_back[1:],
        room=SMALL_BYTES,
    )
    grad_pre = lax.all_to_all(grad_copies, axes, 0, 0).reshape(blocks, length, up_chan)

    own_part = width // devices
    few = -(-(taps + lat_chan) // (16 * devices)) * 16
    lump = lambda rows: small((pairs, rows, HD), BF16)
    flat = lambda rows: small((rows, HD), BF16)
    vmem = pltpu.VMEM
    def core_sum(keep, send, rows):
        return plain(add_core_kernel, [keep, hop(send, "sy", 1)], [lump(rows)] * row_groups)

    def sx_sum(sums, rows, after=()):
        sums = [sums[0]] + [hop(sums[k], "sx", k) for k in range(1, row_groups)]
        return plain(lambda *refs: add_sx_kernel(row_groups, *refs), sums, [flat(rows)] * pairs, after)

    def z_sum(sums, rows, after=()):
        sums = [sums[0]] + [hop(sums[m], "sy", 2 * m) for m in range(1, pairs)]
        return plain(add_kernel, sums, [flat(rows)], after)[0]

    def spread_z(mine):
        return jnp.stack([mine] + [hop(mine, "sy", 2 * m) for m in range(1, pairs)])

    def spread_sx(mine):
        near = [mine] + [hop(mine, "sx", k) for k in range(1, row_groups)]
        return near + [hop(values, "sy", 1) for values in near]

    mixed = call(
        lambda *refs: text_out_kernel(repeat, blocks, *refs), head,
        [(w_out, pl.ANY)] + [(a, None) for a in text_back],
        [bf(text_rows, width)] * row_groups,
        wo_room + [vmem((text_block, heads_here * HD), BF16), dma(4)],
        flops=2 * text_block * width * heads_here * HD,
        after=[grad_copies],
    )
    mixed = [mixed[0]] + [hop(mixed[k], "sx", k) for k in range(1, row_groups)]
    text_out = (text_local.astype(F32) + sum(m.astype(F32) for m in mixed)).astype(BF16)
    k_rows, v_rows = k_img.reshape(total, HD), v_img.reshape(total, HD)
    strip_room = lambda *lead: [vmem((*lead, side_len), F32)] * 2 + [vmem((*lead, side_len), BF16)] * 2
    dk, dv = call(
        text_backward_kernel, head,
        [(thr, pltpu.SMEM)] + [(a, None) for a in (k_rows, v_rows, q_txt, qt_txt, mix_txt_t, lse_txt, *text_back)],
        [small((total, HD), F32)] * 2,
        [vmem((text_total, HD), BF16)] + [vmem((total, text_total), kind) for kind in (F32, F32, BF16, BF16)],
        flops=2_000_000_000,
        after=mixed[:1] + [grad_copies],
    )
    rows = 2 * own_part + few
    near_arrays = (k_rows, v_rows, qt, kt, q_img, mix_t, dk, dv, pre_down, act_t, patch_t)
    far_arrays = near_arrays + (w_query, w_key, w_value, w_out, w_up_proj, w_down_proj)
    keep, send = call(
        lambda *refs: backward_kernel(share, copies, 1, *refs), head,
        [(thr, pltpu.SMEM)] + [(a, None) for a in (
            grad_pre, k_txt, kt_txt, v_txt, lse, u, proj, gram, z, gain, starts, steps, grad_out_t)]
        + [(a, pl.ANY) for a in far_arrays],
        [small((row_groups, pairs, rows, HD), BF16)] * 2,
        [vmem((2, row_groups, pairs, rows, HD), BF16), vmem((blocks, length, HD), F32), vmem((total, HD), F32),
         vmem((total, HD), F32), vmem((HD, up_chan), F32), vmem((devices * few, HD), F32)]
        + strip_room(2, seq)
        + [vmem((seq, HD), BF16)] * 2 + [vmem(qt.shape, BF16), vmem((HD, seq), BF16)]
        + [vmem(a.shape, a.dtype) for a in (q_img, mix_t, dk, dv, pre_down, act_t, patch_t)]
        + [vmem((width, 3 * HD), BF16), vmem((HD + down_chan, width), BF16), vmem(w_up_proj.shape, BF16),
           pltpu.SemaphoreType.DMA((len(far_arrays),))],
        flops=30_000_000_000,
        after=mixed[1:],
        far=True,
    )
    mine = spread_z(z_sum(sx_sum(core_sum(keep, send, rows), rows), rows))
    grad_conv, grad_down, grad_up, grad_out_t = call(
        lambda *refs: unpack_kernel(row_groups, pairs, own_part, *refs), head,
        [(a, None) for a in spread_sx(mine)],
        [small((taps, down_chan), F32), small((down_chan, width), F32), small((width, up_chan), F32),
         small((lat_chan, up_chan), F32)],
        [vmem((devices * few, HD), F32)],
        room=2 * SMALL_BYTES,
    )
    return (
        prediction.reshape(1, tile_rows, tile_cols * lat_chan),
        text_out[None],
        grad_conv,
        grad_down,
        grad_up,
        grad_out_t.T,
    )


def solution(mesh):
    placed = (
        P("sy", "sx", None),
        P("sy", "sx", None),
        P("sy"),
        P(),
        P(None, "sx"),
        P(None, "sx"),
        P(None, "sx"),
        P("sx", None),
        P(),
        P(),
        P(),
        P(),
        P("sy", "sx", None),
        P("sy", "sx", None),
    )
    return jax.shard_map(
        shards,
        mesh=mesh,
        in_specs=placed,
        out_specs=(P("sy", "sx", None), P("sy", "sx", None), P(), P(), P(), P()),
        check_vma=False,
    )
```
